32 devices in a mesh: dp: 8 (over z, x), tensor: 4 (over y, core).
Axes of the slice: x: 2, y: 2, z: 4, core: 2. Of those that a mesh axis runs over, the one named last changes fastest.
Arguments:
- tokens: bfloat16 [15360, 768], P('dp'), may hold values from -6 to 6
- patch_grids: int32 [24, 4, 2], P('dp'), may hold values from 6 to 12
- ln1_gain: float32 [768], replicated, may hold values from 0.5 to 1.5
- ln1_bias: float32 [768], replicated, may hold values from -3 to 3
- w_qkv: bfloat16 [3, 768, 768], P(None, None, 'tensor'), may hold values from -0.21875 to 0.21875
- b_qv: float32 [2, 768], P(None, 'tensor'), may hold values from -3 to 3
- w_proj: bfloat16 [768, 768], P('tensor'), may hold values from -1.75 to 1.75
- b_proj: float32 [768], replicated, may hold values from -3 to 3
- scale1: float32 [768], replicated, may hold values from 0.05 to 0.2
- ln2_gain: float32 [768], replicated, may hold values from 0.5 to 1.5
- ln2_bias: float32 [768], replicated, may hold values from -3 to 3
- w_fc1: bfloat16 [768, 3072], P(None, 'tensor'), may hold values from -0.21875 to 0.21875
- b_fc1: float32 [3072], P('tensor'), may hold values from -3 to 3
- w_fc2: bfloat16 [3072, 768], P('tensor'), may hold values from -0.109375 to 0.109375
- b_fc2: float32 [768], replicated, may hold values from -3 to 3
- scale2: float32 [768], replicated, may hold values from 0.05 to 0.2
- cotangent: bfloat16 [15360, 768], P('dp'), may hold values from -6 to 6
Outputs:
- out: bfloat16 [15360, 768], P('dp')
- grad_tokens: bfloat16 [15360, 768], P('dp')
- grad_ln1_gain: float32 [768], replicated
- grad_ln1_bias: float32 [768], replicated
- grad_w_qkv: float32 [3, 768, 768], P(None, 'dp', 'tensor')
- grad_b_qv: float32 [2, 768], P(None, 'tensor')
- grad_w_proj: float32 [768, 768], P('tensor', 'dp')
- grad_b_proj: float32 [768], replicated
- grad_scale1: float32 [768], replicated
- grad_ln2_gain: float32 [768], replicated
- grad_ln2_bias: float32 [768], replicated
- grad_w_fc1: float32 [768, 3072], P('dp', 'tensor')
- grad_b_fc1: float32 [3072], P('tensor')
- grad_w_fc2: float32 [3072, 768], P('tensor', 'dp')
- grad_b_fc2: float32 [768], replicated
- grad_scale2: float32 [768], replicated
The draws below stay inside these ranges and needn't reach their ends.
Inputs may be any that keep to these rules, and one draw needn't show every extreme that they name: `patch_grids`: Patch-grid height and width of each of a pack's 4 images; image i takes the next h * w + 5 rows after the images before it, and the rows after the last image are padding.
All inputs are finite; a program needn't handle non-finite values.
Results may differ from the reference program's by a relative error of at most 0.015.
Values may be sent and summed in bfloat16 or wider, within the bound.
No kernel may reach another device: no remote copies, remote signals or barrier semaphores. Data moves between devices by JAX's collectives and lax.ppermute only.
A program may use at most 128 MiB of HBM per device.

```python
import math
import jax
import jax.numpy as jnp
from jax import lax

D = 768
H = 12
HD = 64
FF = 3072
PACK_ROWS = 640
IMGS = 4
EXTRA = 5
GRID_LO = 6
GRID_HI = 12
GROUPS = 4
PACKS = 24
TOKENS = 15360


def with_ends(entries, own_key, low, top_value):
    longest = entries.shape.index(max(entries.shape))
    spots = []
    for shift in (0, 1):
        where = [jax.random.randint(jax.random.fold_in(own_key, axis), (), 0, length) for axis, length in enumerate(entries.shape)]
        where[longest] = (where[longest] + shift) % entries.shape[longest]
        spots.append(tuple(where))
    return entries.at[spots[0]].set(low).at[spots[1]].set(top_value)


def spiked(drawn, own_key, source, target, blocks, factor):
    owner, partner = [(jnp.arange(drawn.shape[axis_at]) // (drawn.shape[axis_at] // blocks)).reshape([-1 if axis == axis_at else 1 for axis in range(drawn.ndim)]) for axis_at in (source, target)]
    chosen = jax.random.permutation(own_key, blocks)[partner]
    strong = (owner == chosen) | (owner == (partner + blocks // 2) % blocks)
    return jnp.where(strong, factor * drawn, drawn)


def block_levels(rng, extent, pieces, least, largest):
    def one(axis_at, parts):
        heights = jax.random.uniform(jax.random.fold_in(jax.random.fold_in(rng, 6), axis_at), (parts,), jnp.float32, least / len(pieces), largest / len(pieces))
        return jnp.repeat(jnp.exp(heights), extent[axis_at] // parts).reshape((-1,) + (1,) * (len(extent) - axis_at - 1))

    factor_of = one(*pieces[0])
    for cut in pieces[1:]:
        factor_of = factor_of * one(*cut)
    return factor_of


def noise(stream_key, dims, deviation, most, cuts=(), held_as=jnp.bfloat16):
    array = jax.random.normal(stream_key, dims, jnp.float32) * deviation
    if len(cuts) > 0:
        array = block_levels(stream_key, dims, cuts, -0.22, 0.18) * array
    return jnp.clip(array, min=-most, max=most).astype(held_as)


def gaussian_with(stream_key, extent, scale, limit, pieces, heavy, held_as=jnp.bfloat16):
    values = scale * jax.random.normal(stream_key, extent, jnp.float32)
    if pieces:
        values = values * block_levels(stream_key, extent, pieces, -0.22, 0.18)
    return jnp.clip(spiked(values, jax.random.fold_in(stream_key, 3), *heavy), -limit, limit).astype(held_as)


def setup_inputs(seed: int = 0) -> dict:
    key_list = jax.random.split(jax.random.key(seed), 18)
    tokens = noise(key_list[0], (TOKENS, D), 1.0, 6.0, ((0, 8),))
    patch_grids = with_ends(jax.random.randint(key_list[1], (PACKS, IMGS, 2), GRID_LO, GRID_HI + 1), jax.random.fold_in(key_list[1], 1), GRID_LO, GRID_HI).astype(jnp.int32)
    ln1_gain = jnp.clip(1.0 + 0.1 * jax.random.normal(key_list[2], (D,), jnp.float32), 0.5, 1.5)
    ln1_bias = noise(key_list[3], (D,), 0.3, 3.0, (), jnp.float32)
    w_qkv = noise(key_list[4], (3, D, H * HD), D ** -0.5, 0.21875, ((2, 4),))
    b_qv = noise(key_list[5], (2, H * HD), 0.3, 3.0, ((1, 4),), jnp.float32)
    w_proj = noise(key_list[6], (H * HD, D), (max(D // 64, 4)) ** -0.5, 1.75, ((0, 4),))
    b_proj = noise(key_list[7], (D,), 0.5, 3.0, (), jnp.float32)
    scale1 = jnp.clip(jax.random.uniform(key_list[8], (D,), jnp.float32, 0.05, 0.2), 0.05, 0.2)
    ln2_gain = jnp.clip(1.0 + 0.1 * jax.random.normal(key_list[9], (D,), jnp.float32), 0.5, 1.5)
    ln2_bias = noise(key_list[10], (D,), 0.3, 3.0, (), jnp.float32)
    w_fc1 = noise(key_list[11], (D, FF), D ** -0.5, 0.21875, ((1, 4),))
    b_fc1 = noise(key_list[12], (FF,), 0.5, 3.0, ((0, 4),), jnp.float32)
    w_fc2 = noise(key_list[13], (FF, D), FF ** -0.5, 0.109375, ((0, 4),))
    b_fc2 = noise(key_list[14], (D,), 0.5, 3.0, (), jnp.float32)
    scale2 = jnp.clip(jax.random.uniform(key_list[15], (D,), jnp.float32, 0.05, 0.2), 0.05, 0.2)
    cotangent = gaussian_with(key_list[16], (TOKENS, D), 1.0, 6.0, ((0, 8),), (0, 1, 8, 2.0))
    return {"tokens": tokens, "patch_grids": patch_grids, "ln1_gain": ln1_gain, "ln1_bias": ln1_bias, "w_qkv": w_qkv, "b_qv": b_qv, "w_proj": w_proj, "b_proj": b_proj, "scale1": scale1, "ln2_gain": ln2_gain, "ln2_bias": ln2_bias, "w_fc1": w_fc1, "b_fc1": b_fc1, "w_fc2": w_fc2, "b_fc2": b_fc2, "scale2": scale2, "cotangent": cotangent}


norm_eps = 1e-06

@jax.custom_vjp
def low(v):
    return lax.optimization_barrier(v.astype(jnp.bfloat16)).astype(jnp.float32)

@jax.custom_vjp
def low_back(v):
    return v

def low_keep(v):
    return (low(v), None)

def low_pass(kept, grad):
    return (grad,)

def back_keep(v):
    return (v, None)

def back_low(kept, grad):
    return (low(grad),)
low.defvjp(low_keep, low_pass)
low_back.defvjp(back_keep, back_low)

def layer_norm(field, ln_gain, ln_bias):
    row_mean = lax.optimization_barrier(jnp.mean(field, axis=-1, keepdims=True))
    centred = field - row_mean
    spread = lax.optimization_barrier(jnp.mean(centred * centred, axis=-1, keepdims=True))
    return centred * lax.rsqrt(spread + norm_eps) * ln_gain + ln_bias

def segment_rows(pack_grid):
    lengths = (pack_grid[:, 0] * pack_grid[:, 1] + EXTRA).astype(jnp.int32)
    image_ends = jnp.cumsum(lengths).astype(jnp.int32)
    row_index = jnp.arange(PACK_ROWS, dtype=jnp.int32)
    return lax.optimization_barrier(jnp.sum((row_index[:, None] >= image_ends[None, :]).astype(jnp.int32), axis=1)).astype(jnp.int32)

def forward(inputs, segment, weights_all):
    ln1_gain, ln1_bias, w_qkv, b_qv, w_proj, b_proj, scale1, ln2_gain, ln2_bias, w_fc1, b_fc1, w_fc2, b_fc2, scale2 = weights_all
    highest = lax.Precision.HIGHEST
    row_count = inputs.shape[0]
    att_scale = 1.0 / math.sqrt(HD)
    live_rows = (segment < IMGS).astype(jnp.float32)
    normed1 = low(layer_norm(inputs, ln1_gain, ln1_bias))
    queries = low_back(low(jnp.dot(normed1, w_qkv[0], precision=highest) + b_qv[0]))
    key_rows = low_back(low(jnp.dot(normed1, w_qkv[1], precision=highest)))
    values = low_back(low(jnp.dot(normed1, w_qkv[2], precision=highest) + b_qv[1]))
    query_heads = queries.reshape(row_count, H, HD)
    key_heads = key_rows.reshape(row_count, H, HD)
    value_heads = values.reshape(row_count, H, HD)
    scores = jnp.einsum('qhd,khd->hqk', query_heads, key_heads, precision=highest) * att_scale
    same_image = segment[:, None] == segment[None, :]
    scores = low_back(jnp.where(same_image[None], scores, -1e+30))
    probs = low(jax.nn.softmax(scores, axis=-1))
    attended = jnp.einsum('hqk,khd->qhd', probs, value_heads, precision=highest)
    attended = low_back(low(attended)).reshape(row_count, H * HD)
    group_parts = jnp.einsum('rgc,gcd->rgd', attended.reshape(row_count, GROUPS, -1), w_proj.reshape(GROUPS, -1, D), precision=highest)
    mixed = low_back(lax.optimization_barrier(jnp.sum(low(group_parts), axis=1)))
    hidden1 = inputs + scale1 * (mixed + b_proj)
    normed2 = low(layer_norm(hidden1, ln2_gain, ln2_bias))
    hidden_pre = low_back(jnp.dot(normed2, w_fc1, precision=highest) + b_fc1)
    active = low(jax.nn.gelu(hidden_pre, approximate=False))
    mlp_parts = jnp.einsum('rgf,gfd->rgd', active.reshape(row_count, GROUPS, -1), w_fc2.reshape(GROUPS, -1, D), precision=highest)
    output = low_back(lax.optimization_barrier(jnp.sum(low(mlp_parts), axis=1)))
    return (hidden1 + scale2 * (output + b_fc2)) * live_rows[:, None]

def reference(tokens, patch_grids, ln1_gain, ln1_bias, w_qkv, b_qv, w_proj, b_proj, scale1, ln2_gain, ln2_bias, w_fc1, b_fc1, w_fc2, b_fc2, scale2, cotangent):
    weights_all = tuple((w.astype(jnp.float32) for w in (ln1_gain, ln1_bias, w_qkv, b_qv, w_proj, b_proj, scale1, ln2_gain, ln2_bias, w_fc1, b_fc1, w_fc2, b_fc2, scale2)))
    segments = jax.vmap(segment_rows)(patch_grids)
    input_packs = tokens.astype(jnp.float32).reshape(PACKS, PACK_ROWS, D)
    cot_packs = cotangent.astype(jnp.float32).reshape(PACKS, PACK_ROWS, D)

    def pack_step(totals, pack_item):
        inputs, segment, cot_rows = pack_item

        def run_pack(inner_in, inner_weights):
            return forward(inner_in, segment, inner_weights)
        result, pullback = jax.vjp(run_pack, inputs, weights_all)
        grad_in, pack_grads = pullback(cot_rows)
        totals = tuple((a + b for a, b in zip(totals, pack_grads)))
        return (totals, (result, grad_in))
    zero_grads = tuple((jnp.zeros_like(w) for w in weights_all))
    totals, (results, grad_ins) = lax.scan(pack_step, zero_grads, (input_packs, segments, cot_packs))
    return (results.reshape(TOKENS, D).astype(jnp.bfloat16), grad_ins.reshape(TOKENS, D).astype(jnp.bfloat16), totals[0], totals[1], totals[2], totals[3], totals[4], totals[5], totals[6], totals[7], totals[8], totals[9], totals[10], totals[11], totals[12], totals[13])
```

```python
import functools
import math

import jax
import jax.numpy as jnp
from jax import lax
from jax.experimental import pallas as pl
from jax.experimental.pallas import tpu as pltpu
from jax.sharding import PartitionSpec as P

HD = 64
ROWS = 640
HALF = 320
EXTRA = 5
EPS = 1e-06
MASKED = -1e30
F32 = jnp.float32
BF16 = jnp.bfloat16
MIB = 1024 * 1024
VM = pltpu.VMEM


def nn(a, b):
    return lax.dot_general(a, b, (((1,), (0,)), ((), ())), preferred_element_type=F32)


def nt(a, b):
    return lax.dot_general(a, b, (((1,), (1,)), ((), ())), preferred_element_type=F32)


def tn(a, b):
    return lax.dot_general(a, b, (((0,), (0,)), ((), ())), preferred_element_type=F32)


def row(ref):
    return ref[...].reshape(1, ref.shape[-1])


def stats(v):
    mean = jnp.mean(v, axis=-1, keepdims=True)
    centred = v - mean
    spread = jnp.mean(centred * centred, axis=-1, keepdims=True)
    rstd = lax.rsqrt(spread + EPS)
    return centred * rstd, rstd


def ends_of(grid_ref, pack):
    ends = []
    total = jnp.int32(0)
    for image in range(4):
        total = total + grid_ref[pack, image, 0] * grid_ref[pack, image, 1] + EXTRA
        ends.append(total)
    return ends


def segment_at(position, ends):
    found = jnp.zeros(position.shape, jnp.int32)
    for end in ends:
        found = found + jnp.where(position >= end, 1, 0)
    return found


def key_extras(ends, base):
    shape = (ROWS, 128)
    seg = segment_at(lax.broadcasted_iota(jnp.int32, shape, 0), ends)
    lane = lax.broadcasted_iota(jnp.int32, shape, 1) - base
    mask = jnp.where(lane == seg, 0.0, MASKED)
    inside = (lane >= 0) & (lane < 5)
    ones = (lane >= 5) & (lane < 8)
    return jnp.where(inside, mask, jnp.where(ones, 1.0, 0.0)).astype(BF16)


def query_extras(ends, shift):
    shape = (16, ROWS)
    part = lax.broadcasted_iota(jnp.int32, shape, 0)
    if ends is None:
        extra = jnp.zeros(shape, F32)
    else:
        seg = segment_at(lax.broadcasted_iota(jnp.int32, shape, 1), ends)
        extra = jnp.where(part == seg, 1.0, 0.0)
    if shift is not None:
        high = shift.astype(BF16).astype(F32)
        rest = shift - high
        middle = rest.astype(BF16).astype(F32)
        low = rest - middle
        extra = jnp.where(part == 5, high, extra)
        extra = jnp.where(part == 6, middle, extra)
        extra = jnp.where(part == 7, low, extra)
    return jnp.concatenate([extra.astype(BF16), jnp.zeros((48, ROWS), BF16)], axis=0)


def keys_of(head, tiles_ref, low_extra, high_extra):
    lane = lax.broadcasted_iota(jnp.int32, (ROWS, 128), 1)
    tile = tiles_ref[:, 128 * (head // 2) : 128 * (head // 2) + 128]
    if head % 2 == 0:
        return jnp.where(lane < 64, tile, high_extra)
    return jnp.where(lane < 64, low_extra, tile)


def queries_of(head, rows_ref, extra):
    own = rows_ref[64 * head : 64 * head + 64, :]
    return jnp.concatenate([own, extra] if head % 2 == 0 else [extra, own], axis=0)


def attention_forward(
    pack,
    grid_ref,
    x_ref,
    gain_ref,
    bias_ref,
    w_ref,
    bqv_ref,
    n1_ref,
    q_ref,
    qt_ref,
    k_ref,
    kt_ref,
    v_ref,
    o_ref,
    ot_ref,
    lse_ref,
    vt_ref,
):
    gain, bias = row(gain_ref), row(bias_ref)
    for r in range(0, ROWS, 160):
        normed, _ = stats(x_ref[r : r + 160, :].astype(F32))
        n1_ref[r : r + 160, :] = (normed * gain + bias).astype(BF16)
    n1 = n1_ref[...]
    cols = 3 * HD
    q = (nn(n1, w_ref[0]) + bqv_ref[0:1, :]) * (1.0 / math.sqrt(HD))
    q_ref[...] = q.astype(BF16)
    qt_ref[...] = q.T.astype(BF16)
    k = nn(n1, w_ref[1])
    k_ref[:, :cols] = k.astype(BF16)
    kt_ref[...] = k.T.astype(BF16)
    v = nn(n1, w_ref[2]) + bqv_ref[1:2, :]
    v_ref[:, :cols] = v.astype(BF16)
    vt_ref[...] = v.T.astype(BF16)
    ends = ends_of(grid_ref, pack)
    low_extra, high_extra = key_extras(ends, 0), key_extras(ends, 64)
    extra = query_extras(ends, None)
    for head in range(3):
        s = nn(keys_of(head, k_ref, low_extra, high_extra), queries_of(head, qt_ref, extra))
        top = jnp.max(s, axis=0, keepdims=True)
        e = jnp.exp(s - top)
        total = jnp.sum(e, axis=0, keepdims=True)
        o = nn(vt_ref[64 * head : 64 * head + 64, :], e.astype(BF16)) / total
        ot_ref[64 * head : 64 * head + 64, :] = o.astype(BF16)
        lse_ref[head : head + 1, :] = top + jnp.log(total)
    o_ref[...] = ot_ref[...].astype(F32).T.astype(BF16)


def attention_backward(
    pack,
    has_sum,
    last,
    place_ref,
    grid_ref,
    mine_ref,
    other_ref,
    wp_ref,
    w_ref,
    n1_ref,
    q_ref,
    qt_ref,
    k_ref,
    kt_ref,
    v_ref,
    o_ref,
    ot_ref,
    lse_ref,
    *rest,
):
    if has_sum:
        g_in_ref, b_in_ref, *rest = rest
    keep_ref, send_ref, g_ref, b_ref, dy_ref, do_ref, dot_ref, dqt_ref, dqkv_ref, dn_ref = rest
    half = place_ref[0]
    dy_ref[pl.ds(pl.multiple_of(half * HALF, HALF), HALF), :] = mine_ref[...]
    dy_ref[pl.ds(pl.multiple_of((1 - half) * HALF, HALF), HALF), :] = other_ref[...]
    dy = dy_ref[...]
    do_ref[...] = nt(dy, wp_ref[...]).astype(BF16)
    dot_ref[...] = nt(wp_ref[...], dy).astype(BF16)
    ends = ends_of(grid_ref, pack)
    low_extra, high_extra = key_extras(ends, 0), key_extras(ends, 64)
    cols = 3 * HD
    for head in range(3):
        a, b = 64 * head, 64 * head + 64
        inner = jnp.sum(
            ot_ref[a:b, :].astype(F32) * dot_ref[a:b, :].astype(F32), axis=0, keepdims=True
        )
        shifted = query_extras(ends, -lse_ref[head : head + 1, :])
        p = jnp.exp(
            nn(keys_of(head, k_ref, low_extra, high_extra), queries_of(head, qt_ref, shifted))
        )
        dp = nn(
            keys_of(head, v_ref, low_extra, high_extra),
            queries_of(head, dot_ref, query_extras(None, -inner)),
        )
        ds = (p * dp).astype(BF16)
        dqkv_ref[:, 2 * cols + a : 2 * cols + b] = nn(p.astype(BF16), do_ref[:, a:b]).astype(BF16)
        dqkv_ref[:, cols + a : cols + b] = nn(ds, q_ref[:, a:b]).astype(BF16)
        dqt_ref[a:b, :] = nn(kt_ref[a:b, :], ds)
    dqkv_ref[:, :cols] = (dqt_ref[...].T * (1.0 / math.sqrt(HD))).astype(BF16)
    dn = nt(dqkv_ref[:, :cols], w_ref[0])
    dn = dn + nt(dqkv_ref[:, cols : 2 * cols], w_ref[1])
    dn = dn + nt(dqkv_ref[:, 2 * cols : 3 * cols], w_ref[2])
    dn_ref[...] = dn
    keep_ref[...] = dn_ref[pl.ds(pl.multiple_of(half * HALF, HALF), HALF), :].astype(BF16)
    send_ref[...] = dn_ref[pl.ds(pl.multiple_of((1 - half) * HALF, HALF), HALF), :].astype(BF16)
    g_qkv = tn(n1_ref[...], dqkv_ref[...])
    g_proj = tn(dy, o_ref[...])
    if has_sum:
        g_qkv = g_qkv + g_in_ref[:, : 3 * cols]
        g_proj = g_proj + g_in_ref[:, 3 * cols :]
    g_ref[:, : 3 * cols] = g_qkv.astype(g_ref.dtype)
    g_ref[:, 3 * cols :] = g_proj.astype(g_ref.dtype)
    sums = jnp.sum(dqkv_ref[...].astype(F32), axis=0, keepdims=True)
    b_ref[...] = sums + b_in_ref[...] if has_sum else sums


def project(
    place_ref, x_ref, o0, o1, o2, o3, w0, w1, w2, w3, bp_ref, s1_ref, gain_ref, bias_ref, n2_ref, yb_ref, y_ref
):
    near = nn(o0[...], w0[...]).astype(BF16).astype(F32) + nn(o1[...], w1[...]).astype(BF16).astype(F32)
    far = nn(o2[...], w2[...]).astype(BF16).astype(F32) + nn(o3[...], w3[...]).astype(BF16).astype(F32)
    y_ref[...] = near + far + row(bp_ref)
    scale, gain, bias = row(s1_ref), row(gain_ref), row(bias_ref)
    for r in range(0, ROWS, 160):
        h1 = x_ref[r : r + 160, :].astype(F32) + scale * y_ref[r : r + 160, :]
        normed, _ = stats(h1)
        n2_ref[r : r + 160, :] = (normed * gain + bias).astype(BF16)
    yb_ref[...] = y_ref[pl.ds(pl.multiple_of(place_ref[0] * HALF, HALF), HALF), :]


def mlp(
    pack,
    place_ref,
    grid_ref,
    n2_ref,
    cot_ref,
    s2_ref,
    w1_ref,
    b1_ref,
    w2_ref,
    dk_ref,
    ds_ref,
    zk_ref,
    zs_ref,
    g_ref,
    du_ref,
    dz_ref,
    db_ref,
):
    half = place_ref[0]
    live_end = ends_of(grid_ref, pack)[3]
    scale, b1 = row(s2_ref), row(b1_ref)
    sums = jnp.zeros((1, b1.shape[-1]), F32)
    for first in range(2):
        which = half if first == 0 else 1 - half
        at = pl.ds(pl.multiple_of(which * HALF, HALF), HALF)
        position = lax.broadcasted_iota(jnp.int32, (HALF, 1), 0) + which * HALF
        live = jnp.where(position < live_end, 1.0, 0.0)
        dz = (scale * (cot_ref[at, :].astype(F32) * live)).astype(BF16)
        dz_ref[at, :] = dz
        u = nn(n2_ref[at, :], w1_ref[...]) + b1
        cdf = 0.5 * (1.0 + lax.erf(u * (1.0 / math.sqrt(2.0))))
        density = jnp.exp(-0.5 * (u * u)) * (1.0 / math.sqrt(2.0 * math.pi))
        g = (u * cdf).astype(BF16)
        g_ref[at, :] = g
        du = (nt(dz, w2_ref[...]) * (cdf + u * density)).astype(BF16)
        du_ref[at, :] = du
        sums = sums + jnp.sum(du.astype(F32), axis=0, keepdims=True)
        (dk_ref if first == 0 else ds_ref)[...] = nt(du, w1_ref[...]).astype(BF16)
        (zk_ref if first == 0 else zs_ref)[...] = nn(g, w2_ref[...]).astype(BF16)
    db_ref[...] = sums


def mlp_weights(n0, n1, n2, z0, z1, z2, u0, u1, u2, g0, g1, g2, out_ref):
    mid = u0.shape[1]
    first = tn(n0[...], u0[...]) + tn(n1[...], u1[...]) + tn(n2[...], u2[...])
    out_ref[:, :mid] = first.astype(BF16)
    second = tn(z0[...], g0[...]) + tn(z1[...], g1[...]) + tn(z2[...], g2[...])
    out_ref[:, mid:] = second.astype(BF16)


def live_half(grid_ref, pack, half):
    position = lax.broadcasted_iota(jnp.int32, (HALF, 1), 0) + half * HALF
    return jnp.where(position < ends_of(grid_ref, pack)[3], 1.0, 0.0)


def colsum(v):
    return jnp.sum(v, axis=0, keepdims=True)


def norm2_backward(
    pack, place_ref, grid_ref, a_ref, b_ref, x_ref, cot_ref, yb_ref, s1_ref, gain_ref, dh_ref, dy_ref, sum_ref
):
    half = place_ref[0]
    live = live_half(grid_ref, pack, half)
    scale = row(s1_ref)
    yb = yb_ref[...]
    h1 = x_ref[...].astype(F32) + scale * yb
    nh, rstd = stats(h1)
    dn2 = a_ref[...].astype(F32) + b_ref[...].astype(F32)
    e = dn2 * row(gain_ref)
    inner = e - jnp.mean(e, axis=-1, keepdims=True) - nh * jnp.mean(e * nh, axis=-1, keepdims=True)
    dh1 = cot_ref[...].astype(F32) * live + inner * rstd
    dh_ref[...] = dh1
    dy_ref[...] = (scale * dh1).astype(BF16)
    sum_ref[0:1, :] = colsum(dn2 * nh)
    sum_ref[1:2, :] = colsum(dn2)
    sum_ref[2:3, :] = colsum(dh1 * yb)
    sum_ref[3:4, :] = colsum(dh1)


def output_rows(
    pack, place_ref, grid_ref, a_ref, b_ref, x_ref, cot_ref, yb_ref, s1_ref, s2_ref, bf_ref, out_ref, sum_ref
):
    half = place_ref[0]
    live = live_half(grid_ref, pack, half)
    h1 = x_ref[...].astype(F32) + row(s1_ref) * yb_ref[...]
    zb = a_ref[...].astype(F32) + b_ref[...].astype(F32) + row(bf_ref)
    out_ref[...] = (live * (h1 + row(s2_ref) * zb)).astype(BF16)
    dd = cot_ref[...].astype(F32) * live
    sum_ref[0:1, :] = colsum(dd * zb)
    sum_ref[1:2, :] = colsum(dd)


def norm1_backward(a_ref, b_ref, x_ref, dh_ref, gain_ref, gt_ref, sum_ref):
    nx, rstd = stats(x_ref[...].astype(F32))
    dn1 = a_ref[...].astype(F32) + b_ref[...].astype(F32)
    e = dn1 * row(gain_ref)
    inner = e - jnp.mean(e, axis=-1, keepdims=True) - nx * jnp.mean(e * nx, axis=-1, keepdims=True)
    gt_ref[...] = (dh_ref[...] + inner * rstd).astype(BF16)
    sum_ref[0:1, :] = colsum(dn1 * nx)
    sum_ref[1:2, :] = colsum(dn1)


def full():
    return pl.BlockSpec(memory_space=VM)


def smem():
    return pl.BlockSpec(memory_space=pltpu.SMEM)


def shaped(*shape, dtype=BF16):
    return jax.ShapeDtypeStruct(shape, dtype)


def call(body, operands, in_specs, out_shape, flops, place=None, out_specs=None, scratch=(), steps=1, limit=40, name=None):
    prefetch = 0 if place is None else 1
    count = len(out_shape)
    moved = sum(math.prod(s.shape) * s.dtype.itemsize for s in out_shape)
    moved += sum(o.size * o.dtype.itemsize for o in operands)
    fixed = []
    for spec, operand in zip(in_specs, operands):
        if spec is None:
            rank = operand.ndim
            spec = pl.BlockSpec(operand.shape, lambda *_, rank=rank: (0,) * rank)
        fixed.append(spec)
    outs = []
    for index, shape in enumerate(out_shape):
        spec = out_specs[index] if out_specs else None
        if spec is None:
            rank = len(shape.shape)
            spec = pl.BlockSpec(shape.shape, lambda *_, rank=rank: (0,) * rank)
        outs.append(spec)
    grid_spec = pltpu.PrefetchScalarGridSpec(
        num_scalar_prefetch=prefetch,
        grid=(steps,),
        in_specs=fixed,
        out_specs=outs,
        scratch_shapes=list(scratch),
    )
    made = pl.pallas_call(
        body,
        out_shape=list(out_shape),
        grid_spec=grid_spec,
        compiler_params=pltpu.CompilerParams(vmem_limit_bytes=limit * MIB),
        cost_estimate=pl.CostEstimate(flops=int(flops), bytes_accessed=int(moved), transcendentals=0),
        name=name,
    )
    del count
    return made(*(() if place is None else (place,)), *operands)


CORE = [(0, 1), (1, 0), (2, 3), (3, 2)]
OVER_Y = [(0, 2), (2, 0), (1, 3), (3, 1)]


def to_core(v):
    return lax.ppermute(v, "tensor", CORE)


def to_y(v):
    return lax.ppermute(v, "tensor", OVER_Y)


def to_dp(v, flip, count):
    return lax.ppermute(v, "dp", [(i, i ^ flip) for i in range(count)])


def scatter_start(grads, count):
    rows, columns = grads.shape
    low_bit = lax.axis_index("dp") % 2
    blocks = grads.reshape(count // 2, 2, rows // count, columns)
    mine = lax.dynamic_index_in_dim(blocks, low_bit, 1, keepdims=False)
    theirs = lax.dynamic_index_in_dim(blocks, 1 - low_bit, 1, keepdims=False)
    return (mine.astype(F32) + to_dp(theirs, 1, count).astype(F32)).astype(BF16)


def scatter_end(blocks, count):
    place = lax.axis_index("dp") // 2
    total = lax.dynamic_index_in_dim(blocks, place, 0, keepdims=False).astype(F32)
    parts = []
    for flip in range(1, count // 2):
        block = lax.dynamic_index_in_dim(blocks, place ^ flip, 0, keepdims=False)
        parts.append(to_dp(block, 2 * flip, count))
    for part in parts:
        total = total + part.astype(F32)
    return total


def small_sum(v, count):
    flip = 1
    while flip < count:
        v = v + to_dp(v, flip, count)
        flip *= 2
    return v


def on_device(
    count,
    tokens,
    patch_grids,
    ln1_gain,
    ln1_bias,
    w_qkv,
    b_qv,
    w_proj,
    b_proj,
    scale1,
    ln2_gain,
    ln2_bias,
    w_fc1,
    b_fc1,
    w_fc2,
    b_fc2,
    scale2,
    cotangent,
):
    packs = patch_grids.shape[0]
    width = tokens.shape[1]
    cols = w_qkv.shape[2]
    hidden = w_fc1.shape[1]
    half = lax.axis_index("tensor") % 2
    place = jnp.full((1,), half, jnp.int32)

    def whole_pack(p):
        return pl.BlockSpec((ROWS, width), lambda *_, p=p: (p, 0))

    def half_pack(p):
        return pl.BlockSpec((HALF, width), lambda i, at, p=p: (2 * p + at[0], 0))

    wp1 = to_core(w_proj)
    wp2 = to_y(w_proj)
    wp3 = to_core(wp2)

    kept = []
    heads = []
    for p in range(packs):
        forward = call(
            functools.partial(attention_forward, p),
            (patch_grids, tokens, ln1_gain, ln1_bias, w_qkv, b_qv),
            (smem(), whole_pack(p), None, None, None, None),
            (
                shaped(ROWS, width),
                shaped(ROWS, cols),
                shaped(cols, ROWS),
                shaped(ROWS, 256),
                shaped(cols, ROWS),
                shaped(ROWS, 256),
                shaped(ROWS, cols),
                shaped(cols, ROWS),
                shaped(8, ROWS, dtype=F32),
            ),
            2 * ROWS * width * 3 * cols + 4 * 3 * ROWS * ROWS * 256,
            scratch=(pltpu.VMEM((cols, ROWS), BF16),),
            name=f"attention_forward_{p}",
        )
        kept.append(forward)
        o0 = forward[6]
        o1 = to_core(o0)
        o2 = to_y(o0)
        o3 = to_core(o2)
        heads.append((o0, o1, o2, o3))

    middle = []
    for p in range(packs):
        n2, yb = call(
            project,
            (tokens, *heads[p], w_proj, wp1, wp2, wp3, b_proj, scale1, ln2_gain, ln2_bias),
            (whole_pack(p),) + (None,) * 12,
            (shaped(ROWS, width), shaped(HALF, width, dtype=F32)),
            2 * ROWS * width * 4 * 256,
            place=place,
            scratch=(pltpu.VMEM((ROWS, width), F32),),
            name=f"project_{p}",
        )
        dk, ds, zk, zs, g, du, dz, db = call(
            functools.partial(mlp, p),
            (patch_grids, n2, cotangent, scale2, w_fc1, b_fc1, w_fc2),
            (smem(), None, whole_pack(p), None, None, None, None),
            (
                shaped(HALF, width),
                shaped(HALF, width),
                shaped(HALF, width),
                shaped(HALF, width),
                shaped(ROWS, hidden),
                shaped(ROWS, hidden),
                shaped(ROWS, width),
                shaped(1, hidden, dtype=F32),
            ),
            8 * ROWS * width * hidden,
            place=place,
            name=f"mlp_{p}",
        )
        middle.append((n2, yb, dk, ds, zk, zs, g, du, dz, db))

    def across(keep, send):
        near = (keep.astype(F32) + to_core(send).astype(F32)).astype(BF16)
        return near, to_y(near)

    steps = width // 256
    lanes = [pl.BlockSpec((ROWS, 256), lambda i: (0, i)) for _ in range(2 * packs)]
    (g_fc,) = call(
        mlp_weights,
        [m[0] for m in middle] + [m[8] for m in middle] + [m[7] for m in middle] + [m[6] for m in middle],
        lanes + [None] * (2 * packs),
        (shaped(width, 2 * hidden),),
        4 * packs * ROWS * width * hidden,
        out_specs=[pl.BlockSpec((256, 2 * hidden), lambda i: (i, 0))],
        steps=steps,
        name="mlp_weights",
    )
    fc_blocks = scatter_start(g_fc, count)

    sums2 = []
    sums3 = []
    backs = []
    for p in range(packs):
        n2, yb, dk, ds, zk, zs, g, du, dz, db = middle[p]
        near, far = across(dk, ds)
        dh1, dy, part = call(
            functools.partial(norm2_backward, p),
            (patch_grids, near, far, tokens, cotangent, yb, scale1, ln2_gain),
            (smem(), None, None, half_pack(p), half_pack(p), None, None, None),
            (shaped(HALF, width, dtype=F32), shaped(HALF, width), shaped(4, width, dtype=F32)),
            30 * HALF * width,
            place=place,
            name=f"norm2_backward_{p}",
        )
        sums2.append(part)
        backs.append((dh1, dy, to_core(dy)))

    outs = []
    for p in range(packs):
        n2, yb, dk, ds, zk, zs, g, du, dz, db = middle[p]
        near, far = across(zk, zs)
        rows, part = call(
            functools.partial(output_rows, p),
            (patch_grids, near, far, tokens, cotangent, yb, scale1, scale2, b_fc2),
            (smem(), None, None, half_pack(p), half_pack(p), None, None, None, None),
            (shaped(HALF, width), shaped(2, width, dtype=F32)),
            10 * HALF * width,
            place=place,
            name=f"output_rows_{p}",
        )
        sums3.append(part)
        outs.append((rows, to_core(rows)))

    g_attn = bias_sums = None
    sums1 = []
    grads = []
    for p in range(packs):
        n1, q, qt, k, kt, v, o, ot, lse = kept[p]
        dh1, dy, dy_other = backs[p]
        last = p == packs - 1
        operands = [patch_grids, dy, dy_other, w_proj, w_qkv, n1, q, qt, k, kt, v, o, ot, lse]
        specs = [smem()] + [None] * 13
        if p:
            operands += [g_attn, bias_sums]
            specs += [None, None]
        keep, send, g_attn, bias_sums = call(
            functools.partial(attention_backward, p, p > 0, last),
            operands,
            specs,
            (
                shaped(HALF, width),
                shaped(HALF, width),
                shaped(width, 4 * cols, dtype=BF16 if last else F32),
                shaped(1, 3 * cols, dtype=F32),
            ),
            12 * ROWS * width * cols + 10 * 3 * ROWS * ROWS * 256,
            place=place,
            scratch=(
                pltpu.VMEM((ROWS, width), BF16),
                pltpu.VMEM((ROWS, cols), BF16),
                pltpu.VMEM((cols, ROWS), BF16),
                pltpu.VMEM((cols, ROWS), F32),
                pltpu.VMEM((ROWS, 3 * cols), BF16),
                pltpu.VMEM((ROWS, width), F32),
            ),
            name=f"attention_backward_{p}",
        )
        near, far = across(keep, send)
        rows, part = call(
            norm1_body,
            (near, far, tokens, dh1, ln1_gain),
            (None, None, half_pack(p), None, None),
            (shaped(HALF, width), shaped(2, width, dtype=F32)),
            20 * HALF * width,
            place=place,
            name=f"norm1_backward_{p}",
        )
        sums1.append(part)
        grads.append((rows, to_core(rows)))

    fc = scatter_end(fc_blocks, count)
    attn = scatter_end(scatter_start(g_attn, count), count)

    s1 = sum(sums1)
    s2 = sum(sums2)
    s3 = sum(sums3)
    by_rows = jnp.concatenate([s1, s2, s3], axis=0)
    by_rows = by_rows + to_core(by_rows)
    by_hidden = sum(m[9] for m in middle)
    wide = max(width, hidden, 3 * cols)

    def widened(v):
        return jnp.pad(v, ((0, 0), (0, wide - v.shape[1])))

    small = small_sum(
        jnp.concatenate([widened(by_rows), widened(by_hidden), widened(bias_sums)], axis=0), count
    )

    def ordered(pairs):
        flat = []
        for mine, other in pairs:
            flat += [jnp.where(half == 0, mine, other), jnp.where(half == 0, other, mine)]
        return jnp.concatenate(flat, axis=0)

    share = width // count
    return (
        ordered(outs),
        ordered(grads),
        small[0, :width],
        small[1, :width],
        jnp.stack([attn[:, i * cols : (i + 1) * cols] for i in range(3)]),
        jnp.stack([small[9, :cols], small[9, 2 * cols : 3 * cols]]),
        attn[:, 3 * cols :].reshape(share, cols).T,
        scale1 * small[5, :width],
        small[4, :width],
        small[2, :width],
        small[3, :width],
        fc[:, :hidden],
        small[8, :hidden],
        fc[:, hidden:].T,
        scale2 * small[7, :width],
        small[6, :width],
    )


def norm1_body(place_ref, *refs):
    norm1_backward(*refs)


def solution(mesh):
    placed = (
        P("dp", None),
        P("dp", None, None),
        P(),
        P(),
        P(None, None, "tensor"),
        P(None, "tensor"),
        P("tensor", None),
        P(),
        P(),
        P(),
        P(),
        P(None, "tensor"),
        P("tensor"),
        P("tensor", None),
        P(),
        P(),
        P("dp", None),
    )
    return jax.shard_map(
        functools.partial(on_device, mesh.shape["dp"]),
        mesh=mesh,
        in_specs=placed,
        out_specs=(
            P("dp", None),
            P("dp", None),
            P(),
            P(),
            P(None, "dp", "tensor"),
            P(None, "tensor"),
            P("tensor", "dp"),
            P(),
            P(),
            P(),
            P(),
            P("dp", "tensor"),
            P("tensor"),
            P("tensor", "dp"),
            P(),
            P(),
        ),
        check_vma=False,
    )
```

```python
import functools
import math

import jax
import jax.numpy as jnp
from jax import lax
from jax.experimental import pallas as pl
from jax.experimental.pallas import tpu as pltpu
from jax.sharding import PartitionSpec as P

HD = 64
ROWS = 640
HALF = 320
EXTRA = 5
EPS = 1e-06
MASKED = -1e30
F32 = jnp.float32
BF16 = jnp.bfloat16
MIB = 1024 * 1024
VM = pltpu.VMEM


def nn(a, b):
    return lax.dot_general(a, b, (((1,), (0,)), ((), ())), preferred_element_type=F32)


def nt(a, b):
    return lax.dot_general(a, b, (((1,), (1,)), ((), ())), preferred_element_type=F32)


def tn(a, b):
    return lax.dot_general(a, b, (((0,), (0,)), ((), ())), preferred_element_type=F32)


def row(ref):
    return ref[...].reshape(1, ref.shape[-1])


def stats(v):
    mean = jnp.mean(v, axis=-1, keepdims=True)
    centred = v - mean
    spread = jnp.mean(centred * centred, axis=-1, keepdims=True)
    rstd = lax.rsqrt(spread + EPS)
    return centred * rstd, rstd


def ends_of(grid_ref, pack):
    ends = []
    total = jnp.int32(0)
    for image in range(4):
        total = total + grid_ref[pack, image, 0] * grid_ref[pack, image, 1] + EXTRA
        ends.append(total)
    return ends


def segment_at(position, ends):
    found = jnp.zeros(position.shape, jnp.int32)
    for end in ends:
        found = found + jnp.where(position >= end, 1, 0)
    return found


def key_extras(ends, base):
    shape = (ROWS, 128)
    seg = segment_at(lax.broadcasted_iota(jnp.int32, shape, 0), ends)
    lane = lax.broadcasted_iota(jnp.int32, shape, 1) - base
    mask = jnp.where(lane == seg, 0.0, MASKED)
    inside = (lane >= 0) & (lane < 5)
    ones = (lane >= 5) & (lane < 8)
    return jnp.where(inside, mask, jnp.where(ones, 1.0, 0.0)).astype(BF16)


def query_extras(ends, shift):
    shape = (16, ROWS)
    part = lax.broadcasted_iota(jnp.int32, shape, 0)
    if ends is None:
        extra = jnp.zeros(shape, F32)
    else:
        seg = segment_at(lax.broadcasted_iota(jnp.int32, shape, 1), ends)
        extra = jnp.where(part == seg, 1.0, 0.0)
    if shift is not None:
        high = shift.astype(BF16).astype(F32)
        rest = shift - high
        middle = rest.astype(BF16).astype(F32)
        low = rest - middle
        extra = jnp.where(part == 5, high, extra)
        extra = jnp.where(part == 6, middle, extra)
        extra = jnp.where(part == 7, low, extra)
    return jnp.concatenate([extra.astype(BF16), jnp.zeros((48, ROWS), BF16)], axis=0)


def keys_of(head, tiles_ref, start, low_extra, high_extra):
    lane = lax.broadcasted_iota(jnp.int32, (ROWS, 128), 1)
    at = start + 128 * (head // 2)
    tile = tiles_ref[:, at : at + 128]
    if head % 2 == 0:
        return jnp.where(lane < 64, tile, high_extra)
    return jnp.where(lane < 64, low_extra, tile)


def queries_of(head, rows_ref, extra):
    own = rows_ref[64 * head : 64 * head + 64, :]
    return jnp.concatenate([own, extra] if head % 2 == 0 else [extra, own], axis=0)


def attention_forward(
    pack,
    place_ref,
    grid_ref,
    x_ref,
    gain_ref,
    bias_ref,
    w_ref,
    bqv_ref,
    saved_ref,
    keep_ref,
    send_ref,
    lse_ref,
    qt_ref,
    vt_ref,
    ot_ref,
    o_ref,
):
    gain, bias = row(gain_ref), row(bias_ref)
    width = x_ref.shape[1]
    for r in range(0, ROWS, 160):
        normed, _ = stats(x_ref[r : r + 160, :].astype(F32))
        saved_ref[r : r + 160, :width] = (normed * gain + bias).astype(BF16)
    n1 = saved_ref[:, :width]
    cols = 3 * HD
    q = (nn(n1, w_ref[0]) + bqv_ref[0:1, :]) * (1.0 / math.sqrt(HD))
    saved_ref[:, width : width + cols] = q.astype(BF16)
    qt_ref[...] = q.T.astype(BF16)
    saved_ref[:, width + 256 : width + 256 + cols] = nn(n1, w_ref[1]).astype(BF16)
    v = nn(n1, w_ref[2]) + bqv_ref[1:2, :]
    saved_ref[:, width + 512 : width + 512 + cols] = v.astype(BF16)
    vt_ref[...] = v.T.astype(BF16)
    ends = ends_of(grid_ref, pack)
    low_extra, high_extra = key_extras(ends, 0), key_extras(ends, 64)
    extra = query_extras(ends, None)
    for head in range(3):
        s = nn(keys_of(head, saved_ref, width + 256, low_extra, high_extra), queries_of(head, qt_ref, extra))
        top = jnp.max(s, axis=0, keepdims=True)
        e = jnp.exp(s - top)
        total = jnp.sum(e, axis=0, keepdims=True)
        o = nn(vt_ref[64 * head : 64 * head + 64, :], e.astype(BF16)) / total
        ot_ref[64 * head : 64 * head + 64, :] = o
        lse_ref[head : head + 1, :] = top + jnp.log(total)
    o_ref[...] = ot_ref[...].T
    half = place_ref[0]
    saved_ref[:, width + 768 : width + 768 + cols] = o_ref[...].astype(BF16)
    keep_ref[...] = o_ref[pl.ds(pl.multiple_of(half * HALF, HALF), HALF), :].astype(BF16)
    send_ref[...] = o_ref[pl.ds(pl.multiple_of((1 - half) * HALF, HALF), HALF), :].astype(BF16)


def attention_backward(
    pack,
    has_sum,
    last,
    place_ref,
    grid_ref,
    mine_ref,
    other_ref,
    wp_ref,
    w_ref,
    saved_ref,
    lse_ref,
    *rest,
):
    if has_sum:
        g_in_ref, b_in_ref, *rest = rest
    if last:
        gain_ref, bias_ref, keep_ref, send_ref, l_ref, *rest = rest
    else:
        keep_ref, send_ref, *rest = rest
    g_ref, b_ref, dy_ref, do_ref, dot_ref, dqt_ref, dqkv_ref, dn_ref, qt_ref, kt_ref = rest
    half = place_ref[0]
    dy_ref[pl.ds(pl.multiple_of(half * HALF, HALF), HALF), :] = mine_ref[...]
    dy_ref[pl.ds(pl.multiple_of((1 - half) * HALF, HALF), HALF), :] = other_ref[...]
    dy = dy_ref[...]
    do_ref[...] = nt(dy, wp_ref[...]).astype(BF16)
    dot_ref[...] = nt(wp_ref[...], dy).astype(BF16)
    ends = ends_of(grid_ref, pack)
    low_extra, high_extra = key_extras(ends, 0), key_extras(ends, 64)
    cols = 3 * HD
    width = dy.shape[1]
    q_at, k_at, v_at = width, width + 256, width + 512
    qt_ref[...] = saved_ref[:, q_at : q_at + cols].T
    kt_ref[...] = saved_ref[:, k_at : k_at + cols].T
    o = saved_ref[:, width + 768 : width + 768 + cols]
    weighted = o.astype(F32) * do_ref[...].astype(F32)
    dqt_ref[...] = weighted.T
    inners = [jnp.sum(dqt_ref[64 * h : 64 * h + 64, :], axis=0, keepdims=True) for h in range(3)]
    for head in range(3):
        a, b = 64 * head, 64 * head + 64
        inner = inners[head]
        shifted = query_extras(ends, -lse_ref[head : head + 1, :])
        p = jnp.exp(
            nn(keys_of(head, saved_ref, k_at, low_extra, high_extra), queries_of(head, qt_ref, shifted))
        )
        dp = nn(
            keys_of(head, saved_ref, v_at, low_extra, high_extra),
            queries_of(head, dot_ref, query_extras(None, -inner)),
        )
        ds = (p * dp).astype(BF16)
        dqkv_ref[:, 2 * cols + a : 2 * cols + b] = nn(p.astype(BF16), do_ref[:, a:b]).astype(BF16)
        dqkv_ref[:, cols + a : cols + b] = nn(ds, saved_ref[:, q_at + a : q_at + b]).astype(BF16)
        dqt_ref[a:b, :] = nn(kt_ref[a:b, :], ds)
    dqkv_ref[:, :cols] = (dqt_ref[...].T * (1.0 / math.sqrt(HD))).astype(BF16)
    dn = nt(dqkv_ref[:, :cols], w_ref[0])
    dn = dn + nt(dqkv_ref[:, cols : 2 * cols], w_ref[1])
    dn = dn + nt(dqkv_ref[:, 2 * cols : 3 * cols], w_ref[2])
    dn_ref[...] = dn
    keep_ref[...] = dn_ref[pl.ds(pl.multiple_of(half * HALF, HALF), HALF), :].astype(BF16)
    send_ref[...] = dn_ref[pl.ds(pl.multiple_of((1 - half) * HALF, HALF), HALF), :].astype(BF16)
    g_qkv = tn(saved_ref[:, :width], dqkv_ref[...])
    g_proj = tn(dy, o)
    if has_sum:
        g_qkv = g_qkv + g_in_ref[:, : 3 * cols]
        g_proj = g_proj + g_in_ref[:, 3 * cols :]
    g_ref[:, : 3 * cols] = g_qkv.astype(g_ref.dtype)
    g_ref[:, 3 * cols :] = g_proj.astype(g_ref.dtype)
    sums = jnp.sum(dqkv_ref[...].astype(F32), axis=0, keepdims=True)
    sums = sums + b_in_ref[...] if has_sum else sums
    b_ref[...] = sums
    if last:
        plain = sum(jnp.sum(w_ref[c].astype(F32) * sums[:, c * cols : (c + 1) * cols], axis=1, keepdims=True) for c in range(3))
        mixed = sum(jnp.sum(w_ref[c].astype(F32) * g_qkv[:, c * cols : (c + 1) * cols], axis=1, keepdims=True) for c in range(3))
        wide = jnp.concatenate([mixed, plain, jnp.zeros((width, 126), F32)], axis=1).T
        l_ref[0:1, :] = (wide[0:1, :] - row(bias_ref) * wide[1:2, :]) / row(gain_ref)
        l_ref[1:2, :] = wide[1:2, :]


def hidden_part(n2, dz, w1_ref, b1, w2_ref):
    u = nn(n2, w1_ref[...]) + b1
    cdf = 0.5 * (1.0 + lax.erf(u * (1.0 / math.sqrt(2.0))))
    density = jnp.exp(-0.5 * (u * u)) * (1.0 / math.sqrt(2.0 * math.pi))
    g = (u * cdf).astype(BF16)
    du = (nt(dz, w2_ref[...]) * (cdf + u * density)).astype(BF16)
    return g, du, nt(du, w1_ref[...])


def project_mlp(
    pack,
    place_ref,
    grid_ref,
    x_ref,
    o0,
    o1,
    o2,
    o3,
    p0,
    p1,
    p2,
    p3,
    bp_ref,
    s1_ref,
    gain_ref,
    bias_ref,
    cot_ref,
    s2_ref,
    w1_ref,
    b1_ref,
    w2_ref,
    v1_ref,
    c1_ref,
    v2_ref,
    yb_ref,
    n2_ref,
    dn_ref,
    g_ref,
    du_ref,
    dz_ref,
    sum_ref,
):
    y0, y1, y2, y3 = (nn(o[...], p[...]).astype(BF16).astype(F32) for o, p in ((o0, p0), (o1, p1), (o2, p2), (o3, p3)))
    yb = (y0 + y1) + (y2 + y3) + row(bp_ref)
    yb_ref[...] = yb
    normed, _ = stats(x_ref[...].astype(F32) + row(s1_ref) * yb)
    n2 = (normed * row(gain_ref) + row(bias_ref)).astype(BF16)
    n2_ref[...] = n2
    dd = cot_ref[...].astype(F32) * live_half(grid_ref, pack, place_ref[0])
    dz = (row(s2_ref) * dd).astype(BF16)
    dz_ref[...] = dz
    hidden = w1_ref.shape[1]
    g, du, dn = hidden_part(n2, dz, w1_ref, row(b1_ref), w2_ref)
    g_ref[:, :hidden] = g
    du_ref[:, :hidden] = du
    sum_ref[0:1, :] = colsum(du.astype(F32))
    g, du, dn_other = hidden_part(n2, dz, v1_ref, row(c1_ref), v2_ref)
    g_ref[:, hidden:] = g
    du_ref[:, hidden:] = du
    sum_ref[1:2, :] = colsum(du.astype(F32))
    dn_ref[...] = (dn + dn_other).astype(BF16)


def mlp_output(pack, place_ref, grid_ref, g_ref, w2_ref, v2_ref, cot_ref, z_ref, sum_ref):
    hidden = w2_ref.shape[0]
    z = nn(g_ref[:, :hidden], w2_ref[...]) + nn(g_ref[:, hidden:], v2_ref[...])
    z_ref[...] = z.astype(BF16)
    dd = cot_ref[...].astype(F32) * live_half(grid_ref, pack, place_ref[0])
    sum_ref[0:1, :] = colsum(dd * z)
    sum_ref[1:2, :] = colsum(dd)


def add_rows(a_ref, b_ref, out_ref):
    out_ref[...] = (a_ref[...].astype(F32) + b_ref[...].astype(F32)).astype(BF16)


def mlp_weights(n0, n1, n2, z0, z1, z2, u0, u1, u2, g0, g1, g2, *rest):
    *added, out_ref = rest
    mid = u0.shape[1]
    first = tn(n0[...], u0[...]) + tn(n1[...], u1[...]) + tn(n2[...], u2[...])
    second = tn(z0[...], g0[...]) + tn(z1[...], g1[...]) + tn(z2[...], g2[...])
    if added:
        first = first + added[0][:, :mid].astype(F32)
        second = second + added[0][:, mid:].astype(F32)
    out_ref[:, :mid] = first.astype(BF16)
    out_ref[:, mid:] = second.astype(BF16)


def live_half(grid_ref, pack, half):
    position = lax.broadcasted_iota(jnp.int32, (HALF, 1), 0) + half * HALF
    return jnp.where(position < ends_of(grid_ref, pack)[3], 1.0, 0.0)


def colsum(v):
    return jnp.sum(v, axis=0, keepdims=True)


def norm2_backward(
    pack, place_ref, grid_ref, a_ref, b_ref, x_ref, cot_ref, yb_ref, s1_ref, gain_ref, dh_ref, dy_ref, sum_ref
):
    half = place_ref[0]
    live = live_half(grid_ref, pack, half)
    scale = row(s1_ref)
    yb = yb_ref[...]
    h1 = x_ref[...].astype(F32) + scale * yb
    nh, rstd = stats(h1)
    dn2 = a_ref[...].astype(F32) + b_ref[...].astype(F32)
    e = dn2 * row(gain_ref)
    inner = e - jnp.mean(e, axis=-1, keepdims=True) - nh * jnp.mean(e * nh, axis=-1, keepdims=True)
    dh1 = cot_ref[...].astype(F32) * live + inner * rstd
    dh_ref[...] = dh1
    dy_ref[...] = (scale * dh1).astype(BF16)
    sum_ref[0:1, :] = colsum(dn2 * nh)
    sum_ref[1:2, :] = colsum(dn2)
    sum_ref[2:3, :] = colsum(dh1 * yb)
    sum_ref[3:4, :] = colsum(dh1)


def output_rows(
    pack, place_ref, grid_ref, a_ref, b_ref, x_ref, yb_ref, s1_ref, s2_ref, bf_ref, out_ref
):
    live = live_half(grid_ref, pack, place_ref[0])
    h1 = x_ref[...].astype(F32) + row(s1_ref) * yb_ref[...]
    zb = a_ref[...].astype(F32) + b_ref[...].astype(F32) + row(bf_ref)
    out_ref[...] = (live * (h1 + row(s2_ref) * zb)).astype(BF16)


def norm1_backward(place_ref, a_ref, b_ref, x_ref, dh_ref, gain_ref, gt_ref):
    nx, rstd = stats(x_ref[...].astype(F32))
    dn1 = a_ref[...].astype(F32) + b_ref[...].astype(F32)
    e = dn1 * row(gain_ref)
    inner = e - jnp.mean(e, axis=-1, keepdims=True) - nx * jnp.mean(e * nx, axis=-1, keepdims=True)
    gt_ref[...] = (dh_ref[...] + inner * rstd).astype(BF16)


def full():
    return pl.BlockSpec(memory_space=VM)


def smem():
    return pl.BlockSpec(memory_space=pltpu.SMEM)


def shaped(*shape, dtype=BF16):
    return jax.ShapeDtypeStruct(shape, dtype)


def kernel_call(pinned, body, operands, in_specs, out_shape, flops, place=None, out_specs=None, scratch=(), steps=1, limit=16, name=None, after=()):
    prefetch = 0 if place is None else 1
    operands = [pltpu.with_memory_space_constraint(o, pltpu.HBM) if id(o) in pinned else o for o in operands]
    count = len(out_shape)
    moved = sum(math.prod(s.shape) * s.dtype.itemsize for s in out_shape)
    moved += sum(o.size * o.dtype.itemsize for o in operands)
    if after:
        skip = prefetch + len(operands)
        inner = body

        def body(*refs):
            inner(*refs[:skip], *refs[skip + len(after) :])

        operands = (*operands, *after)
        in_specs = (*in_specs, *(pl.BlockSpec(memory_space=pl.ANY) for _ in after))
    fixed = []
    for spec, operand in zip(in_specs, operands):
        if spec is None:
            rank = operand.ndim
            spec = pl.BlockSpec(operand.shape, lambda *_, rank=rank: (0,) * rank)
        fixed.append(spec)
    outs = []
    for index, shape in enumerate(out_shape):
        spec = out_specs[index] if out_specs else None
        if spec is None:
            rank = len(shape.shape)
            spec = pl.BlockSpec(shape.shape, lambda *_, rank=rank: (0,) * rank)
        outs.append(spec)
    grid_spec = pltpu.PrefetchScalarGridSpec(
        num_scalar_prefetch=prefetch,
        grid=(steps,),
        in_specs=fixed,
        out_specs=outs,
        scratch_shapes=list(scratch),
    )
    made = pl.pallas_call(
        body,
        out_shape=list(out_shape),
        grid_spec=grid_spec,
        compiler_params=pltpu.CompilerParams(vmem_limit_bytes=limit * MIB),
        cost_estimate=pl.CostEstimate(flops=10**12, bytes_accessed=int(moved), transcendentals=0),
        name=name,
    )
    del count
    return made(*(() if place is None else (place,)), *operands)


CORE = [(0, 1), (1, 0), (2, 3), (3, 2)]
OVER_Y = [(0, 2), (2, 0), (1, 3), (3, 1)]


def to_core(v):
    return lax.ppermute(v, "tensor", CORE)


def to_far(v):
    return lax.ppermute(v, "tensor", [(0, 3), (3, 0), (1, 2), (2, 1)])


def to_y(v):
    return lax.ppermute(v, "tensor", OVER_Y)


def to_dp(v, flip, count):
    return lax.ppermute(v, "dp", [(i, i ^ flip) for i in range(count)])


def swapped(grads, count):
    rows, columns = grads.shape
    return lax.all_to_all(grads.reshape(count, rows // count, columns), "dp", 0, 0)


def summed_share(grads, count):
    rows, columns = grads.shape
    low, high = lax.axis_index("dp") % 2, lax.axis_index("dp") // 2
    blocks = grads.reshape(count // 2, 2, rows // count, columns)
    mine = lax.dynamic_index_in_dim(blocks, low, 1, keepdims=False)
    theirs = lax.dynamic_index_in_dim(blocks, 1 - low, 1, keepdims=False)
    blocks = (mine.astype(F32) + to_dp(theirs, 1, count).astype(F32)).astype(BF16)
    parts = [lax.dynamic_index_in_dim(blocks, high, 0)]
    for flip in range(1, count // 2):
        parts.append(to_dp(lax.dynamic_index_in_dim(blocks, high ^ flip, 0), 2 * flip, count))
    return parts


def on_device(
    count,
    tokens,
    patch_grids,
    ln1_gain,
    ln1_bias,
    w_qkv,
    b_qv,
    w_proj,
    b_proj,
    scale1,
    ln2_gain,
    ln2_bias,
    w_fc1,
    b_fc1,
    w_fc2,
    b_fc2,
    scale2,
    cotangent,
):
    packs = patch_grids.shape[0]
    width = tokens.shape[1]
    cols = w_qkv.shape[2]
    hidden = w_fc1.shape[1]
    half = lax.axis_index("tensor") % 2
    place = jnp.full((1,), half, jnp.int32)

    fixed = (tokens, cotangent, ln1_gain, ln1_bias, b_qv, b_proj, scale1, ln2_gain, ln2_bias, b_fc1, b_fc2, scale2)
    call = functools.partial(kernel_call, [id(v) for v in fixed])

    def whole_pack(p):
        return pl.BlockSpec((ROWS, width), lambda *_, p=p: (p, 0))

    def half_pack(p):
        return pl.BlockSpec((HALF, width), lambda i, at, p=p: (2 * p + at[0], 0))

    wp1 = to_core(w_proj)
    wp2 = to_y(w_proj)
    wp3 = to_far(w_proj)
    near_w1, near_w2, near_b1 = to_core(w_fc1), to_core(w_fc2), to_core(b_fc1)

    previous = []

    def run(*args, after=(), **settings):
        made = call(*args, after=(*previous, *after), **settings)
        previous[:] = [made[-1]]
        return made

    def near_sum(keep, send, name):
        (total,) = run(add_rows, (keep, send), (None, None), (shaped(HALF, width),), HALF * width, name=name)
        return total

    kept = []
    heads = []
    for p in range(packs):
        saved, keep, send, lse = run(
            functools.partial(attention_forward, p),
            (patch_grids, tokens, ln1_gain, ln1_bias, w_qkv, b_qv),
            (smem(), whole_pack(p), None, None, None, None),
            (pltpu.HBM((ROWS, width + 1024), BF16), shaped(HALF, cols), shaped(HALF, cols), shaped(8, ROWS, dtype=F32)),
            2 * ROWS * width * 3 * cols + 4 * 3 * ROWS * ROWS * 256,
            place=place,
            scratch=(
                pltpu.VMEM((cols, ROWS), BF16),
                pltpu.VMEM((cols, ROWS), BF16),
                pltpu.VMEM((cols, ROWS), F32),
                pltpu.VMEM((ROWS, cols), F32),
            ),
            name=f"attention_forward_{p}",
            after=((), (near_w1, near_w2, near_b1, wp1), (heads[0][1], wp2, wp3) if heads else ())[p] if p < 3 else (),
        )
        kept.append((saved, lse))
        heads.append((keep, to_core(send), to_y(keep), to_far(send)))

    parts = []

    def hidden_pack(p):
        parts.append(
            run(
                functools.partial(project_mlp, p),
                (
                    patch_grids,
                    tokens,
                    *heads[p],
                    w_proj,
                    wp1,
                    wp2,
                    wp3,
                    b_proj,
                    scale1,
                    ln2_gain,
                    ln2_bias,
                    cotangent,
                    scale2,
                    w_fc1,
                    b_fc1,
                    w_fc2,
                    near_w1,
                    near_b1,
                    near_w2,
                ),
                (smem(), half_pack(p)) + (None,) * 12 + (half_pack(p),) + (None,) * 7,
                (
                    shaped(HALF, width, dtype=F32),
                    shaped(HALF, width),
                    shaped(HALF, width),
                    shaped(HALF, 2 * hidden),
                    shaped(HALF, 2 * hidden),
                    shaped(HALF, width),
                    shaped(2, hidden, dtype=F32),
                ),
                8 * ROWS * width * hidden,
                place=place,
                limit=28,
                name=f"project_mlp_{p}",
            )
        )

    def weights(part, added, name):
        lanes = [pl.BlockSpec((HALF, 256), lambda i: (0, i)) for _ in range(2 * packs)]
        units = [pl.BlockSpec((HALF, hidden), lambda i: (0, part)) for _ in range(2 * packs)]
        (g_fc,) = run(
            mlp_weights,
            [v[i] for i in (1, 5, 4, 3) for v in parts] + added,
            lanes + units + [pl.BlockSpec((256, 2 * hidden), lambda i: (i, 0)) for _ in added],
            (shaped(width, 2 * hidden),),
            4 * packs * ROWS * width * hidden,
            out_specs=[pl.BlockSpec((256, 2 * hidden), lambda i: (i, 0))],
            steps=width // 256,
            name=name,
        )
        return g_fc

    def norm2_pack(p, near, far):
        dh1, dy, part = run(
            functools.partial(norm2_backward, p),
            (patch_grids, near, far, tokens, cotangent, parts[p][0], scale1, ln2_gain),
            (smem(), None, None, half_pack(p), half_pack(p), None, None, None),
            (shaped(HALF, width, dtype=F32), shaped(HALF, width), shaped(4, width, dtype=F32)),
            30 * HALF * width,
            place=place,
            name=f"norm2_backward_{p}",
        )
        return dh1, dy, to_core(dy), part

    def attention_pack(p, dy, dy_other, before):
        saved, lse = kept[p]
        last = p == packs - 1
        operands = [patch_grids, dy, dy_other, w_proj, w_qkv, saved, lse, *before]
        if last:
            operands += [ln1_gain, ln1_bias]
        keep, send, *norm_sums, g_attn, bias_sums = run(
            functools.partial(attention_backward, p, bool(before), last),
            operands,
            [smem()] + [None] * (len(operands) - 1),
            (
                shaped(HALF, width),
                shaped(HALF, width),
                *([shaped(2, width, dtype=F32)] if last else []),
                shaped(width, 4 * cols, dtype=BF16 if last else F32),
                shaped(1, 3 * cols, dtype=F32),
            ),
            12 * ROWS * width * cols + 10 * 3 * ROWS * ROWS * 256,
            place=place,
            scratch=(
                pltpu.VMEM((ROWS, width), BF16),
                pltpu.VMEM((ROWS, cols), BF16),
                pltpu.VMEM((cols, ROWS), BF16),
                pltpu.VMEM((cols, ROWS), F32),
                pltpu.VMEM((ROWS, 3 * cols), BF16),
                pltpu.VMEM((ROWS, width), F32),
                pltpu.VMEM((cols, ROWS), BF16),
                pltpu.VMEM((cols, ROWS), BF16),
            ),
            name=f"attention_backward_{p}",
        )
        return keep, to_core(send), (g_attn, bias_sums), norm_sums

    def norm1_pack(p, near, far, dh1):
        (rows,) = run(
            norm1_backward,
            (near, far, tokens, dh1, ln1_gain),
            (None, None, half_pack(p), None, None),
            (shaped(HALF, width),),
            20 * HALF * width,
            place=place,
            name=f"norm1_backward_{p}",
        )
        return rows, to_core(rows)

    def output_pack(p, near, far):
        (rows,) = run(
            functools.partial(output_rows, p),
            (patch_grids, near, far, tokens, parts[p][0], scale1, scale2, b_fc2),
            (smem(), None, None, half_pack(p), None, None, None, None),
            (shaped(HALF, width),),
            10 * HALF * width,
            place=place,
            name=f"output_rows_{p}",
        )
        return rows, to_core(rows)

    for p in range(packs):
        hidden_pack(p)
    far2 = [to_y(v[2]) for v in parts]
    near3 = []

    def output_part(p):
        near3.append(
            run(
                functools.partial(mlp_output, p),
                (patch_grids, parts[p][3], w_fc2, near_w2, cotangent),
                (smem(), None, None, None, half_pack(p)),
                (shaped(HALF, width), shaped(2, width, dtype=F32)),
                4 * HALF * width * hidden,
                place=place,
                name=f"mlp_output_{p}",
            )
        )

    g_near = to_core(weights(1, [], "mlp_weights_near"))
    back2 = [norm2_pack(0, parts[0][2], far2[0])]
    fc_parts = swapped(weights(0, [g_near], "mlp_weights_own"), count)
    back2.append(norm2_pack(1, parts[1][2], far2[1]))
    output_part(0)
    near1 = []
    carried = ()
    for p in range(packs):
        keep, other, carried, norm_sums = attention_pack(p, back2[p][1], back2[p][2], carried)
        if p + 2 < packs:
            back2.append(norm2_pack(p + 2, parts[p + 2][2], far2[p + 2]))
        else:
            output_part(p)
        near1.append(near_sum(keep, other, f"near1_{p}"))
    far1 = [to_y(v) for v in near1]
    far3 = [to_y(v[0]) for v in near3]
    attn_parts = summed_share(carried[0], count)
    (small,) = run(
        gather_small,
        (norm_sums[0], *[b[3] for b in back2], *[v[6] for v in parts], *[v[1] for v in near3], carried[1]),
        (None,) * (2 + 3 * packs),
        (shaped(16, max(width, hidden), dtype=F32),),
        width,
        name="gather_small",
    )

    back1 = []
    outs = []
    for p in range(packs):
        if p == packs - 1:
            grad_w_fc1, grad_w_fc2 = run(
                finish_mlp,
                (fc_parts,),
                (None,),
                (shaped(width // count, hidden, dtype=F32), shaped(hidden, width // count, dtype=F32)),
                width * hidden,
                name="finish_mlp",
            )
        back1.append(norm1_pack(p, near1[p], far1[p], back2[p][0]))
        if p == 0:
            (small,) = run(
                small_core, (small, to_core(small)), (None, None), (shaped(*small.shape, dtype=F32),), width, name="small_core"
            )
        if p < packs - 1:
            outs.append(output_pack(p, near3[p][0], far3[p]))
        if p == 0:
            (small,) = run(
                small_y, (small, to_y(small)), (None, None), (shaped(count, *small.shape, dtype=F32),), width, name="small_y"
            )
            small = lax.all_to_all(small, "dp", 0, 0)
    vector = shaped(width, dtype=F32)
    vectors = run(
        finish_small,
        (small, scale1, scale2, b_fc2),
        (None,) * 4,
        (vector, vector, shaped(2, cols, dtype=F32), vector, vector, vector, vector, shaped(hidden, dtype=F32), vector, vector),
        width,
        name="finish_small",
    )
    gain1, bias1, bqv, bp, sc1, gain2, bias2, b1, b2, sc2 = vectors
    grad_w_qkv, grad_w_proj = run(
        finish_attention,
        attn_parts,
        (None,) * len(attn_parts),
        (shaped(3, width // count, cols, dtype=F32), shaped(cols, width // count, dtype=F32)),
        width * cols,
        name="finish_attention",
    )
    outs.append(output_pack(packs - 1, near3[-1][0], far3[-1]))

    def whole(pairs, name):
        halves = [v for pair in pairs for v in pair[:2]]
        (made,) = call(
            collect,
            halves,
            (None,) * len(halves),
            (pltpu.HBM((packs * ROWS, width), BF16),),
            packs * ROWS * width,
            place=place,
            name=name,
        )
        return made

    return (
        whole(outs, "collect_out"),
        whole(back1, "collect_grad"),
        gain1,
        bias1,
        grad_w_qkv,
        bqv,
        grad_w_proj,
        bp,
        sc1,
        gain2,
        bias2,
        grad_w_fc1,
        b1,
        grad_w_fc2,
        b2,
        sc2,
    )


def collect(place_ref, *refs):
    *halves, out_ref = refs
    half = place_ref[0]
    for p in range(len(halves) // 2):
        at = pl.multiple_of((2 * p + half) * HALF, HALF)
        out_ref[pl.ds(at, HALF), :] = halves[2 * p][...]
        at = pl.multiple_of((2 * p + 1 - half) * HALF, HALF)
        out_ref[pl.ds(at, HALF), :] = halves[2 * p + 1][...]


def total_of(*parts_refs):
    total = 0.0
    for ref in parts_refs:
        for i in range(ref.shape[0]):
            total = total + ref[i].astype(F32)
    return total


def finish_mlp(parts_ref, w1_ref, w2_ref):
    total = total_of(parts_ref)
    hidden = w1_ref.shape[1]
    w1_ref[...] = total[:, :hidden]
    w2_ref[...] = total[:, hidden:].T


def finish_attention(*refs):
    *parts, qkv_ref, proj_ref = refs
    total = total_of(*parts)
    cols = qkv_ref.shape[2]
    for i in range(3):
        qkv_ref[i] = total[:, i * cols : (i + 1) * cols]
    proj_ref[...] = total[:, 3 * cols :].T


def gather_small(ln_ref, n0, n1, n2, h0, h1, h2, z0, z1, z2, bias_ref, out_ref):
    width, hidden, cols = ln_ref.shape[1], h0.shape[1], bias_ref.shape[1] // 3
    out_ref[...] = jnp.zeros(out_ref.shape, F32)
    out_ref[0:2, :width] = ln_ref[...]
    out_ref[2:6, :width] = n0[...] + n1[...] + n2[...]
    mlp_sums = h0[...] + h1[...] + h2[...]
    out_ref[6:8, :width] = z0[...] + z1[...] + z2[...]
    out_ref[8:9, :hidden] = mlp_sums[0:1, :hidden]
    out_ref[11:12, :hidden] = mlp_sums[1:2, :hidden]
    out_ref[9:10, :cols] = bias_ref[:, :cols]
    out_ref[10:11, :cols] = bias_ref[:, 2 * cols :]


def small_core(own_ref, other_ref, out_ref):
    out_ref[...] = own_ref[...]
    out_ref[0:8, :] = own_ref[0:8, :] + other_ref[0:8, :]
    out_ref[8:9, :] = own_ref[8:9, :] + other_ref[11:12, :]


def small_y(own_ref, other_ref, out_ref):
    out_ref[0] = own_ref[...]
    out_ref[0, 0:2, :] = own_ref[0:2, :] + other_ref[0:2, :]
    out_ref[0, 6:7, :] = own_ref[6:7, :] + other_ref[6:7, :]
    for i in range(1, out_ref.shape[0]):
        out_ref[i] = out_ref[0]


def finish_small(parts_ref, s1_ref, s2_ref, b2_ref, *outs):
    total = total_of(parts_ref)
    gain1, bias1, bqv, bp, scale1, gain2, bias2, b1, b2, scale2 = outs
    width, hidden, cols = gain1.shape[0], b1.shape[0], bqv.shape[1]
    gain1[...] = total[0, :width]
    bias1[...] = total[1, :width]
    gain2[...] = total[2, :width]
    bias2[...] = total[3, :width]
    scale1[...] = total[4, :width]
    bp[...] = total[5, :width] * s1_ref[...]
    scale2[...] = total[6, :width] + total[7, :width] * b2_ref[...]
    b2[...] = total[7, :width] * s2_ref[...]
    b1[...] = total[8, :hidden]
    bqv[0:1, :] = total[9:10, :cols]
    bqv[1:2, :] = total[10:11, :cols]


def solution(mesh):
    placed = (
        P("dp", None),
        P("dp", None, None),
        P(),
        P(),
        P(None, None, "tensor"),
        P(None, "tensor"),
        P("tensor", None),
        P(),
        P(),
        P(),
        P(),
        P(None, "tensor"),
        P("tensor"),
        P("tensor", None),
        P(),
        P(),
        P("dp", None),
    )
    return jax.shard_map(
        functools.partial(on_device, mesh.shape["dp"]),
        mesh=mesh,
        in_specs=placed,
        out_specs=(
            P("dp", None),
            P("dp", None),
            P(),
            P(),
            P(None, "dp", "tensor"),
            P(None, "tensor"),
            P("tensor", "dp"),
            P(),
            P(),
            P(),
            P(),
            P("dp", "tensor"),
            P("tensor"),
            P("tensor", "dp"),
            P(),
            P(),
        ),
        check_vma=False,
    )
```

```python
import functools
import math

import jax
import jax.numpy as jnp
from jax import lax
from jax.experimental import pallas as pl
from jax.experimental.pallas import tpu as pltpu
from jax.sharding import PartitionSpec as P

HD = 64
ROWS = 640
HALF = 320
EXTRA = 5
EPS = 1e-06
MASKED = -1e30
F32 = jnp.float32
BF16 = jnp.bfloat16
MIB = 1024 * 1024
VM = pltpu.VMEM


def nn(a, b):
    return lax.dot_general(a, b, (((1,), (0,)), ((), ())), preferred_element_type=F32)


def nt(a, b):
    return lax.dot_general(a, b, (((1,), (1,)), ((), ())), preferred_element_type=F32)


def tn(a, b):
    return lax.dot_general(a, b, (((0,), (0,)), ((), ())), preferred_element_type=F32)


def row(ref):
    return ref[...].reshape(1, ref.shape[-1])


def stats(v):
    mean = jnp.mean(v, axis=-1, keepdims=True)
    centred = v - mean
    spread = jnp.mean(centred * centred, axis=-1, keepdims=True)
    rstd = lax.rsqrt(spread + EPS)
    return centred * rstd, rstd


def ends_of(grid_ref, pack):
    ends = []
    total = jnp.int32(0)
    for image in range(4):
        total = total + grid_ref[pack, image, 0] * grid_ref[pack, image, 1] + EXTRA
        ends.append(total)
    return ends


def segment_at(position, ends):
    found = jnp.zeros(position.shape, jnp.int32)
    for end in ends:
        found = found + jnp.where(position >= end, 1, 0)
    return found


def key_extras(ends, base):
    shape = (ROWS, 128)
    seg = segment_at(lax.broadcasted_iota(jnp.int32, shape, 0), ends)
    lane = lax.broadcasted_iota(jnp.int32, shape, 1) - base
    mask = jnp.where(lane == seg, 0.0, MASKED)
    inside = (lane >= 0) & (lane < 5)
    ones = (lane >= 5) & (lane < 8)
    return jnp.where(inside, mask, jnp.where(ones, 1.0, 0.0)).astype(BF16)


def query_extras(ends, shift):
    shape = (16, ROWS)
    part = lax.broadcasted_iota(jnp.int32, shape, 0)
    if ends is None:
        extra = jnp.zeros(shape, F32)
    else:
        seg = segment_at(lax.broadcasted_iota(jnp.int32, shape, 1), ends)
        extra = jnp.where(part == seg, 1.0, 0.0)
    if shift is not None:
        high = shift.astype(BF16).astype(F32)
        rest = shift - high
        middle = rest.astype(BF16).astype(F32)
        low = rest - middle
        extra = jnp.where(part == 5, high, extra)
        extra = jnp.where(part == 6, middle, extra)
        extra = jnp.where(part == 7, low, extra)
    return jnp.concatenate([extra.astype(BF16), jnp.zeros((48, ROWS), BF16)], axis=0)


def keys_of(head, tiles_ref, start, low_extra, high_extra):
    lane = lax.broadcasted_iota(jnp.int32, (ROWS, 128), 1)
    at = start + 128 * (head // 2)
    tile = tiles_ref[:, at : at + 128]
    if head % 2 == 0:
        return jnp.where(lane < 64, tile, high_extra)
    return jnp.where(lane < 64, low_extra, tile)


def queries_of(head, rows_ref, extra):
    own = rows_ref[64 * head : 64 * head + 64, :]
    return jnp.concatenate([own, extra] if head % 2 == 0 else [extra, own], axis=0)


def attention_forward(
    pack,
    place_ref,
    grid_ref,
    x_ref,
    gain_ref,
    bias_ref,
    w_ref,
    bqv_ref,
    saved_ref,
    keep_ref,
    send_ref,
    lse_ref,
    qt_ref,
    vt_ref,
    ot_ref,
    o_ref,
):
    gain, bias = row(gain_ref), row(bias_ref)
    width = x_ref.shape[1]
    for r in range(0, ROWS, 160):
        normed, _ = stats(x_ref[r : r + 160, :].astype(F32))
        saved_ref[r : r + 160, :width] = (normed * gain + bias).astype(BF16)
    n1 = saved_ref[:, :width]
    cols = 3 * HD
    q = (nt(n1, w_ref[0]) + bqv_ref[0:1, :]) * (1.0 / math.sqrt(HD))
    saved_ref[:, width : width + cols] = q.astype(BF16)
    qt_ref[...] = q.T.astype(BF16)
    saved_ref[:, width + 256 : width + 256 + cols] = nt(n1, w_ref[1]).astype(BF16)
    v = nt(n1, w_ref[2]) + bqv_ref[1:2, :]
    saved_ref[:, width + 512 : width + 512 + cols] = v.astype(BF16)
    vt_ref[...] = v.T.astype(BF16)
    ends = ends_of(grid_ref, pack)
    low_extra, high_extra = key_extras(ends, 0), key_extras(ends, 64)
    extra = query_extras(ends, None)
    for head in range(3):
        s = nn(keys_of(head, saved_ref, width + 256, low_extra, high_extra), queries_of(head, qt_ref, extra))
        top = jnp.max(s, axis=0, keepdims=True)
        e = jnp.exp(s - top)
        total = jnp.sum(e, axis=0, keepdims=True)
        o = nn(vt_ref[64 * head : 64 * head + 64, :], e.astype(BF16)) / total
        ot_ref[64 * head : 64 * head + 64, :] = o
        lse_ref[head : head + 1, :] = top + jnp.log(total)
    o_ref[...] = ot_ref[...].T
    half = place_ref[0]
    saved_ref[:, width + 768 : width + 768 + cols] = o_ref[...].astype(BF16)
    keep_ref[...] = o_ref[pl.ds(pl.multiple_of(half * HALF, HALF), HALF), :].astype(BF16)
    send_ref[...] = o_ref[pl.ds(pl.multiple_of((1 - half) * HALF, HALF), HALF), :].astype(BF16)


def attention_backward(
    pack,
    has_sum,
    last,
    place_ref,
    grid_ref,
    mine_ref,
    other_ref,
    wp_ref,
    w_ref,
    saved_ref,
    lse_ref,
    *rest,
):
    if has_sum:
        g_in_ref, b_in_ref, *rest = rest
    if last:
        gain_ref, bias_ref, keep_ref, send_ref, l_ref, *rest = rest
    else:
        keep_ref, send_ref, *rest = rest
    g_ref, b_ref, dy_ref, do_ref, dot_ref, dqt_ref, dqkv_ref, dn_ref, qt_ref, kt_ref = rest
    half = place_ref[0]
    dy_ref[pl.ds(pl.multiple_of(half * HALF, HALF), HALF), :] = mine_ref[...]
    dy_ref[pl.ds(pl.multiple_of((1 - half) * HALF, HALF), HALF), :] = other_ref[...]
    dy = dy_ref[...]
    do_ref[...] = nt(dy, wp_ref[...]).astype(BF16)
    dot_ref[...] = nt(wp_ref[...], dy).astype(BF16)
    ends = ends_of(grid_ref, pack)
    low_extra, high_extra = key_extras(ends, 0), key_extras(ends, 64)
    cols = 3 * HD
    width = dy.shape[1]
    q_at, k_at, v_at = width, width + 256, width + 512
    qt_ref[...] = saved_ref[:, q_at : q_at + cols].T
    kt_ref[...] = saved_ref[:, k_at : k_at + cols].T
    o = saved_ref[:, width + 768 : width + 768 + cols]
    weighted = o.astype(F32) * do_ref[...].astype(F32)
    dqt_ref[...] = weighted.T
    inners = [jnp.sum(dqt_ref[64 * h : 64 * h + 64, :], axis=0, keepdims=True) for h in range(3)]
    for head in range(3):
        a, b = 64 * head, 64 * head + 64
        inner = inners[head]
        shifted = query_extras(ends, -lse_ref[head : head + 1, :])
        p = jnp.exp(
            nn(keys_of(head, saved_ref, k_at, low_extra, high_extra), queries_of(head, qt_ref, shifted))
        )
        dp = nn(
            keys_of(head, saved_ref, v_at, low_extra, high_extra),
            queries_of(head, dot_ref, query_extras(None, -inner)),
        )
        ds = (p * dp).astype(BF16)
        dqkv_ref[:, 2 * cols + a : 2 * cols + b] = nn(p.astype(BF16), do_ref[:, a:b]).astype(BF16)
        dqkv_ref[:, cols + a : cols + b] = nn(ds, saved_ref[:, q_at + a : q_at + b]).astype(BF16)
        dqt_ref[a:b, :] = nn(kt_ref[a:b, :], ds)
    dqkv_ref[:, :cols] = (dqt_ref[...].T * (1.0 / math.sqrt(HD))).astype(BF16)
    dn = nn(dqkv_ref[:, :cols], w_ref[0])
    dn = dn + nn(dqkv_ref[:, cols : 2 * cols], w_ref[1])
    dn = dn + nn(dqkv_ref[:, 2 * cols : 3 * cols], w_ref[2])
    dn_ref[...] = dn
    keep_ref[...] = dn_ref[pl.ds(pl.multiple_of(half * HALF, HALF), HALF), :].astype(BF16)
    send_ref[...] = dn_ref[pl.ds(pl.multiple_of((1 - half) * HALF, HALF), HALF), :].astype(BF16)
    g_qkv = tn(saved_ref[:, :width], dqkv_ref[...])
    g_proj = tn(dy, o)
    if has_sum:
        g_qkv = g_qkv + g_in_ref[:, : 3 * cols].astype(F32)
        g_proj = g_proj + g_in_ref[:, 3 * cols :].astype(F32)
    g_ref[:, : 3 * cols] = g_qkv.astype(g_ref.dtype)
    g_ref[:, 3 * cols :] = g_proj.astype(g_ref.dtype)
    sums = jnp.sum(dqkv_ref[...].astype(F32), axis=0, keepdims=True)
    sums = sums + b_in_ref[...] if has_sum else sums
    b_ref[...] = sums
    if last:
        plain = jnp.zeros((width, 1), F32)
        mixed = jnp.zeros((width, 1), F32)
        for c in range(3):
            at = slice(c * cols, (c + 1) * cols)
            w = w_ref[c].astype(F32).T
            plain = plain + jnp.sum(w * sums[:, at], axis=1, keepdims=True)
            mixed = mixed + jnp.sum(w * g_qkv[:, at], axis=1, keepdims=True)
        wide = jnp.concatenate([mixed, plain, jnp.zeros((width, 126), F32)], axis=1).T
        l_ref[0:1, :] = (wide[0:1, :] - row(bias_ref) * wide[1:2, :]) / row(gain_ref)
        l_ref[1:2, :] = wide[1:2, :]


def hidden_part(n2, dz, w1_ref, b1, w2_ref):
    u = nn(n2, w1_ref[...]) + b1
    cdf = 0.5 * (1.0 + lax.erf(u * (1.0 / math.sqrt(2.0))))
    density = jnp.exp(-0.5 * (u * u)) * (1.0 / math.sqrt(2.0 * math.pi))
    g = (u * cdf).astype(BF16)
    du = (nt(dz, w2_ref[...]) * (cdf + u * density)).astype(BF16)
    return g, du, nt(du, w1_ref[...])


def project_mlp(
    pack,
    place_ref,
    grid_ref,
    x_ref,
    o0,
    o1,
    o2,
    o3,
    p0,
    p1,
    p2,
    p3,
    bp_ref,
    s1_ref,
    gain_ref,
    bias_ref,
    cot_ref,
    s2_ref,
    w1_ref,
    b1_ref,
    w2_ref,
    v1_ref,
    c1_ref,
    v2_ref,
    yb_ref,
    n2_ref,
    dn_ref,
    g_ref,
    du_ref,
    dz_ref,
    sum_ref,
):
    y0, y1, y2, y3 = (nn(o[...], p[...]).astype(BF16).astype(F32) for o, p in ((o0, p0), (o1, p1), (o2, p2), (o3, p3)))
    yb = (y0 + y1) + (y2 + y3) + row(bp_ref)
    yb_ref[...] = yb.astype(BF16)
    normed, _ = stats(x_ref[...].astype(F32) + row(s1_ref) * yb)
    n2 = (normed * row(gain_ref) + row(bias_ref)).astype(BF16)
    n2_ref[...] = n2
    dd = cot_ref[...].astype(F32) * live_half(grid_ref, pack, place_ref[0])
    dz = (row(s2_ref) * dd).astype(BF16)
    dz_ref[...] = dz
    hidden = w1_ref.shape[1]
    g, du, dn = hidden_part(n2, dz, w1_ref, row(b1_ref), w2_ref)
    g_ref[:, :hidden] = g
    du_ref[:, :hidden] = du
    sum_ref[0:1, :] = colsum(du.astype(F32))
    g, du, dn_other = hidden_part(n2, dz, v1_ref, row(c1_ref), v2_ref)
    g_ref[:, hidden:] = g
    du_ref[:, hidden:] = du
    sum_ref[1:2, :] = colsum(du.astype(F32))
    dn_ref[...] = (dn + dn_other).astype(BF16)


def mlp_output(pack, place_ref, grid_ref, g_ref, w2_ref, v2_ref, cot_ref, z_ref, sum_ref):
    hidden = w2_ref.shape[0]
    z = nn(g_ref[:, :hidden], w2_ref[...]) + nn(g_ref[:, hidden:], v2_ref[...])
    z_ref[...] = z.astype(BF16)
    dd = cot_ref[...].astype(F32) * live_half(grid_ref, pack, place_ref[0])
    sum_ref[0:1, :] = colsum(dd * z)
    sum_ref[1:2, :] = colsum(dd)


def add_rows(a_ref, b_ref, out_ref):
    out_ref[...] = (a_ref[...].astype(F32) + b_ref[...].astype(F32)).astype(BF16)


def mlp_weights(n0, n1, n2, z0, z1, z2, u0, u1, u2, g0, g1, g2, *rest):
    *added, out_ref = rest
    mid = u0.shape[1]
    first = tn(n0[...], u0[...]) + tn(n1[...], u1[...]) + tn(n2[...], u2[...])
    second = tn(z0[...], g0[...]) + tn(z1[...], g1[...]) + tn(z2[...], g2[...])
    if added:
        first = first + added[0][:, :mid].astype(F32)
        second = second + added[0][:, mid:].astype(F32)
    out_ref[:, :mid] = first.astype(BF16)
    out_ref[:, mid:] = second.astype(BF16)


def live_half(grid_ref, pack, half):
    position = lax.broadcasted_iota(jnp.int32, (HALF, 1), 0) + half * HALF
    return jnp.where(position < ends_of(grid_ref, pack)[3], 1.0, 0.0)


def colsum(v):
    return jnp.sum(v, axis=0, keepdims=True)


def norm2_backward(
    pack, place_ref, grid_ref, a_ref, b_ref, x_ref, cot_ref, yb_ref, s1_ref, gain_ref, dh_ref, dy_ref, sum_ref
):
    half = place_ref[0]
    live = live_half(grid_ref, pack, half)
    scale = row(s1_ref)
    yb = yb_ref[...].astype(F32)
    h1 = x_ref[...].astype(F32) + scale * yb
    nh, rstd = stats(h1)
    dn2 = a_ref[...].astype(F32) + b_ref[...].astype(F32)
    e = dn2 * row(gain_ref)
    inner = e - jnp.mean(e, axis=-1, keepdims=True) - nh * jnp.mean(e * nh, axis=-1, keepdims=True)
    dh1 = cot_ref[...].astype(F32) * live + inner * rstd
    dh_ref[...] = dh1.astype(BF16)
    dy_ref[...] = (scale * dh1).astype(BF16)
    sum_ref[0:1, :] = colsum(dn2 * nh)
    sum_ref[1:2, :] = colsum(dn2)
    sum_ref[2:3, :] = colsum(dh1 * yb)
    sum_ref[3:4, :] = colsum(dh1)


def last_rows(
    pack,
    has_rows,
    place_ref,
    grid_ref,
    a1_ref,
    b1_ref,
    a3_ref,
    b3_ref,
    x_ref,
    dh_ref,
    yb_ref,
    gain_ref,
    s1_ref,
    s2_ref,
    bf_ref,
    *rest,
):
    gt_ref, out_ref, send_ref = rest[2:] if has_rows else rest
    live = live_half(grid_ref, pack, place_ref[0])
    x = x_ref[...].astype(F32)
    zb = a3_ref[...].astype(F32) + b3_ref[...].astype(F32) + row(bf_ref)
    out = (live * (x + row(s1_ref) * yb_ref[...].astype(F32) + row(s2_ref) * zb)).astype(BF16)
    out_ref[...] = out
    send_ref[HALF:, :] = out
    nx, rstd = stats(x)
    e = (a1_ref[...].astype(F32) + b1_ref[...].astype(F32)) * row(gain_ref)
    inner = e - jnp.mean(e, axis=-1, keepdims=True) - nx * jnp.mean(e * nx, axis=-1, keepdims=True)
    gt = (dh_ref[...].astype(F32) + inner * rstd).astype(BF16)
    gt_ref[...] = gt
    send_ref[:HALF, :] = gt


def place_rows(place_ref, *refs):
    got, (gt_ref, out_ref, sems) = refs[: len(refs) - 5], refs[len(refs) - 3 :]
    copies = []
    for p, ref in enumerate(got):
        at = pl.ds(pl.multiple_of((2 * p + 1 - place_ref[0]) * HALF, HALF), HALF)
        copies.append(pltpu.make_async_copy(ref.at[pl.ds(0, HALF), :], gt_ref.at[at, :], sems.at[2 * p]))
        copies.append(pltpu.make_async_copy(ref.at[pl.ds(HALF, HALF), :], out_ref.at[at, :], sems.at[2 * p + 1]))
    for copy in copies:
        copy.start()
    for copy in copies:
        copy.wait()


def full():
    return pl.BlockSpec(memory_space=VM)


def smem():
    return pl.BlockSpec(memory_space=pltpu.SMEM)


def shaped(*shape, dtype=BF16):
    return jax.ShapeDtypeStruct(shape, dtype)


def kernel_call(pinned, body, operands, in_specs, out_shape, flops, place=None, out_specs=None, scratch=(), steps=1, limit=16, name=None, after=(), aliases=None):
    prefetch = 0 if place is None else 1
    operands = [pltpu.with_memory_space_constraint(o, pltpu.HBM) if id(o) in pinned else o for o in operands]
    count = len(out_shape)
    moved = sum(math.prod(s.shape) * s.dtype.itemsize for s in out_shape)
    moved += sum(o.size * o.dtype.itemsize for o in operands)
    if after:
        skip = prefetch + len(operands)
        inner = body

        def body(*refs):
            inner(*refs[:skip], *refs[skip + len(after) :])

        operands = (*operands, *after)
        in_specs = (*in_specs, *(pl.BlockSpec(memory_space=pl.ANY) for _ in after))
    fixed = []
    for spec, operand in zip(in_specs, operands):
        if spec is None:
            rank = operand.ndim
            spec = pl.BlockSpec(operand.shape, lambda *_, rank=rank: (0,) * rank)
        fixed.append(spec)
    outs = []
    for index, shape in enumerate(out_shape):
        spec = out_specs[index] if out_specs else None
        if spec is None:
            rank = len(shape.shape)
            spec = pl.BlockSpec(shape.shape, lambda *_, rank=rank: (0,) * rank)
        outs.append(spec)
    grid_spec = pltpu.PrefetchScalarGridSpec(
        num_scalar_prefetch=prefetch,
        grid=(steps,),
        in_specs=fixed,
        out_specs=outs,
        scratch_shapes=list(scratch),
    )
    made = pl.pallas_call(
        body,
        out_shape=list(out_shape),
        grid_spec=grid_spec,
        input_output_aliases={prefetch + k: v for k, v in (aliases or {}).items()},
        compiler_params=pltpu.CompilerParams(vmem_limit_bytes=limit * MIB),
        cost_estimate=pl.CostEstimate(flops=3 * 10**10, bytes_accessed=int(moved), transcendentals=0),
        name=name,
    )
    del count
    return made(*(() if place is None else (place,)), *operands)


CORE = [(0, 1), (1, 0), (2, 3), (3, 2)]
OVER_Y = [(0, 2), (2, 0), (1, 3), (3, 1)]


def to_core(v):
    return lax.ppermute(v, "tensor", CORE)


def to_far(v):
    return lax.ppermute(v, "tensor", [(0, 3), (3, 0), (1, 2), (2, 1)])


def to_y(v):
    return lax.ppermute(v, "tensor", OVER_Y)


def to_dp(v, flip, count):
    return lax.ppermute(v, "dp", [(i, i ^ flip) for i in range(count)])


def swapped(grads, count):
    rows, columns = grads.shape
    return lax.all_to_all(grads.reshape(count, rows // count, columns), "dp", 0, 0)


def summed_share(grads, count):
    rows, columns = grads.shape
    low, high = lax.axis_index("dp") % 2, lax.axis_index("dp") // 2
    blocks = grads.reshape(count // 2, 2, rows // count, columns)
    mine = lax.dynamic_index_in_dim(blocks, low, 1, keepdims=False)
    theirs = lax.dynamic_index_in_dim(blocks, 1 - low, 1, keepdims=False)
    blocks = (mine.astype(F32) + to_dp(theirs, 1, count).astype(F32)).astype(BF16)
    parts = [lax.dynamic_index_in_dim(blocks, high, 0)]
    for flip in range(1, count // 2):
        parts.append(to_dp(lax.dynamic_index_in_dim(blocks, high ^ flip, 0), 2 * flip, count))
    return parts


def on_device(
    count,
    tokens,
    patch_grids,
    ln1_gain,
    ln1_bias,
    w_qkv,
    b_qv,
    w_proj,
    b_proj,
    scale1,
    ln2_gain,
    ln2_bias,
    w_fc1,
    b_fc1,
    w_fc2,
    b_fc2,
    scale2,
    cotangent,
):
    packs = patch_grids.shape[0]
    w_qkv = w_qkv.transpose(0, 2, 1)
    width = tokens.shape[1]
    cols = w_qkv.shape[1]
    hidden = w_fc1.shape[1]
    half = lax.axis_index("tensor") % 2
    place = jnp.full((1,), half, jnp.int32)

    fixed = (tokens, cotangent, ln1_gain, ln1_bias, b_qv, b_proj, scale1, ln2_gain, ln2_bias, b_fc1, b_fc2, scale2, w_qkv)
    call = functools.partial(kernel_call, [id(v) for v in fixed])

    def whole_pack(p):
        return pl.BlockSpec((ROWS, width), lambda *_, p=p: (p, 0))

    def half_pack(p):
        return pl.BlockSpec((HALF, width), lambda i, at, p=p: (2 * p + at[0], 0))

    wp1 = to_core(w_proj)
    wp2 = to_y(w_proj)
    wp3 = to_far(w_proj)
    near_w1, near_w2, near_b1 = to_core(w_fc1), to_core(w_fc2), to_core(b_fc1)

    previous = []

    def run(*args, after=(), **settings):
        made = call(*args, after=(*previous, *after), **settings)
        previous[:] = [made[-1]]
        return made

    def near_sum(keep, send, name):
        (total,) = run(add_rows, (keep, send), (None, None), (shaped(HALF, width),), HALF * width, name=name)
        return total

    kept = []
    heads = []
    for p in range(packs):
        saved, keep, send, lse = run(
            functools.partial(attention_forward, p),
            (patch_grids, tokens, ln1_gain, ln1_bias, w_qkv, b_qv),
            (smem(), whole_pack(p), None, None, None, None),
            (pltpu.HBM((ROWS, width + 1024), BF16), shaped(HALF, cols), shaped(HALF, cols), shaped(8, ROWS, dtype=F32)),
            2 * ROWS * width * 3 * cols + 4 * 3 * ROWS * ROWS * 256,
            place=place,
            scratch=(
                pltpu.VMEM((cols, ROWS), BF16),
                pltpu.VMEM((cols, ROWS), BF16),
                pltpu.VMEM((cols, ROWS), F32),
                pltpu.VMEM((ROWS, cols), F32),
            ),
            name=f"attention_forward_{p}",
            after=((), (near_w1, near_w2, near_b1, wp1), (heads[0][1], wp2, wp3) if heads else ())[p] if p < 3 else (),
        )
        kept.append((saved, lse))
        heads.append((keep, to_core(send), to_y(keep), to_far(send)))

    parts = []

    def hidden_pack(p):
        parts.append(
            run(
                functools.partial(project_mlp, p),
                (
                    patch_grids,
                    tokens,
                    *heads[p],
                    w_proj,
                    wp1,
                    wp2,
                    wp3,
                    b_proj,
                    scale1,
                    ln2_gain,
                    ln2_bias,
                    cotangent,
                    scale2,
                    w_fc1,
                    b_fc1,
                    w_fc2,
                    near_w1,
                    near_b1,
                    near_w2,
                ),
                (smem(), half_pack(p)) + (None,) * 12 + (half_pack(p),) + (None,) * 7,
                (
                    shaped(HALF, width),
                    shaped(HALF, width),
                    shaped(HALF, width),
                    shaped(HALF, 2 * hidden),
                    shaped(HALF, 2 * hidden),
                    shaped(HALF, width),
                    shaped(2, hidden, dtype=F32),
                ),
                8 * ROWS * width * hidden,
                place=place,
                limit=28,
                name=f"project_mlp_{p}",
            )
        )

    def weights(part, added, name):
        lanes = [pl.BlockSpec((HALF, 256), lambda i: (0, i)) for _ in range(2 * packs)]
        units = [pl.BlockSpec((HALF, hidden), lambda i: (0, part)) for _ in range(2 * packs)]
        (g_fc,) = run(
            mlp_weights,
            [v[i] for i in (1, 5, 4, 3) for v in parts] + added,
            lanes + units + [pl.BlockSpec((256, 2 * hidden), lambda i: (i, 0)) for _ in added],
            (shaped(width, 2 * hidden),),
            4 * packs * ROWS * width * hidden,
            out_specs=[pl.BlockSpec((256, 2 * hidden), lambda i: (i, 0))],
            steps=width // 256,
            name=name,
        )
        return g_fc

    def norm2_pack(p, near, far):
        dh1, dy, part = run(
            functools.partial(norm2_backward, p),
            (patch_grids, near, far, tokens, cotangent, parts[p][0], scale1, ln2_gain),
            (smem(), None, None, half_pack(p), half_pack(p), None, None, None),
            (shaped(HALF, width), shaped(HALF, width), shaped(4, width, dtype=F32)),
            30 * HALF * width,
            place=place,
            name=f"norm2_backward_{p}",
        )
        return dh1, dy, to_core(dy), part

    def attention_pack(p, dy, dy_other, before):
        saved, lse = kept[p]
        last = p == packs - 1
        operands = [patch_grids, dy, dy_other, w_proj, w_qkv, saved, lse, *before]
        if last:
            operands += [ln1_gain, ln1_bias]
        keep, send, *norm_sums, g_attn, bias_sums = run(
            functools.partial(attention_backward, p, bool(before), last),
            operands,
            [smem()] + [None] * (len(operands) - 1),
            (
                shaped(HALF, width),
                shaped(HALF, width),
                *([shaped(2, width, dtype=F32)] if last else []),
                shaped(width, 4 * cols),
                shaped(1, 3 * cols, dtype=F32),
            ),
            12 * ROWS * width * cols + 10 * 3 * ROWS * ROWS * 256,
            place=place,
            scratch=(
                pltpu.VMEM((ROWS, width), BF16),
                pltpu.VMEM((ROWS, cols), BF16),
                pltpu.VMEM((cols, ROWS), BF16),
                pltpu.VMEM((cols, ROWS), F32),
                pltpu.VMEM((ROWS, 3 * cols), BF16),
                pltpu.VMEM((ROWS, width), F32),
                pltpu.VMEM((cols, ROWS), BF16),
                pltpu.VMEM((cols, ROWS), BF16),
            ),
            name=f"attention_backward_{p}",
        )
        return keep, to_core(send), (g_attn, bias_sums), norm_sums

    anywhere = pl.BlockSpec(memory_space=pl.ANY)
    whole_rows = pltpu.HBM((packs * ROWS, width), BF16)
    rows = []
    sent = []

    def last_pack(p, far1, far3):
        operands = [patch_grids, near1[p], far1, near3[p][0], far3, tokens, back2[p][0], parts[p][0], ln1_gain, scale1, scale2, b_fc2]
        specs = [smem(), None, None, None, None, half_pack(p)] + [None] * 6
        made = run(
            functools.partial(last_rows, p, bool(rows)),
            operands + rows,
            specs + [anywhere] * len(rows),
            (whole_rows, whole_rows, shaped(2 * HALF, width)),
            30 * HALF * width,
            place=place,
            out_specs=[half_pack(p), half_pack(p), None],
            name=f"last_rows_{p}",
            aliases={len(operands) + i: i for i in range(len(rows))},
        )
        rows[:] = made[:2]
        sent.append(to_core(made[2]))

    for p in range(packs):
        hidden_pack(p)
    far2 = [to_y(v[2]) for v in parts]
    near3 = []

    def output_part(p):
        near3.append(
            run(
                functools.partial(mlp_output, p),
                (patch_grids, parts[p][3], w_fc2, near_w2, cotangent),
                (smem(), None, None, None, half_pack(p)),
                (shaped(HALF, width), shaped(2, width, dtype=F32)),
                4 * HALF * width * hidden,
                place=place,
                name=f"mlp_output_{p}",
            )
        )

    output_part(0)
    back2 = [norm2_pack(0, parts[0][2], far2[0])]
    g_near = to_core(weights(1, [], "mlp_weights_near"))
    back2.append(norm2_pack(1, parts[1][2], far2[1]))
    near1 = []
    carried = ()
    for p in range(packs):
        keep, other, carried, norm_sums = attention_pack(p, back2[p][1], back2[p][2], carried)
        if p == 0:
            fc_parts = swapped(weights(0, [g_near], "mlp_weights_own"), count)
        else:
            output_part(p)
        near1.append(near_sum(keep, other, f"near1_{p}"))
        if p + 2 < packs:
            back2.append(norm2_pack(p + 2, parts[p + 2][2], far2[p + 2]))
    far1 = [to_y(v) for v in near1]
    far3 = [to_y(v[0]) for v in near3]
    attn_parts = summed_share(carried[0], count)
    (small,) = run(
        gather_small,
        (norm_sums[0], *[b[3] for b in back2], *[v[6] for v in parts], *[v[1] for v in near3], carried[1]),
        (None,) * (2 + 3 * packs),
        (shaped(16, max(width, hidden), dtype=F32),),
        width,
        name="gather_small",
    )

    for p in range(packs - 1):
        last_pack(p, far1[p], far3[p])
        if p == 0:
            (small,) = run(
                small_core, (small, to_core(small)), (None, None), (shaped(*small.shape, dtype=F32),), width, name="small_core"
            )
            flip = 1
            while flip < count:
                small = small + to_dp(small, flip, count)
                flip *= 2
    grad_w_fc1, grad_w_fc2 = run(
        finish_mlp,
        (fc_parts,),
        (None,),
        (shaped(width // count, hidden, dtype=F32), shaped(width // count, hidden, dtype=F32)),
        width * hidden,
        name="finish_mlp",
    )
    last_pack(packs - 1, far1[-1], far3[-1])
    vector = shaped(width, dtype=F32)
    grad_w_qkv, grad_w_proj = run(
        finish_attention,
        attn_parts,
        (None,) * len(attn_parts),
        (shaped(3, width // count, cols, dtype=F32), shaped(width // count, cols, dtype=F32)),
        width * cols,
        name="finish_attention",
    )
    vectors = run(
        finish_small,
        (small, to_y(small), scale1, scale2, b_fc2),
        (None,) * 5,
        (vector, vector, shaped(2, cols, dtype=F32), vector, vector, vector, vector, shaped(hidden, dtype=F32), vector, vector),
        width,
        name="finish_small",
    )
    gain1, bias1, bqv, bp, sc1, gain2, bias2, b1, b2, sc2 = vectors
    grad_tokens, out = call(
        place_rows,
        [*sent, *rows],
        [None] * packs + [anywhere] * 2,
        (whole_rows, whole_rows),
        packs * ROWS * width,
        place=place,
        out_specs=[anywhere, anywhere],
        scratch=(pltpu.SemaphoreType.DMA((2 * packs,)),),
        name="place_rows",
        aliases={packs: 0, packs + 1: 1},
    )
    return (
        out,
        grad_tokens,
        gain1,
        bias1,
        grad_w_qkv,
        bqv,
        grad_w_proj.T,
        bp,
        sc1,
        gain2,
        bias2,
        grad_w_fc1,
        b1,
        grad_w_fc2.T,
        b2,
        sc2,
    )


def total_of(*parts_refs):
    total = 0.0
    for ref in parts_refs:
        for i in range(ref.shape[0]):
            total = total + ref[i].astype(F32)
    return total


def finish_mlp(parts_ref, w1_ref, w2_ref):
    total = total_of(parts_ref)
    hidden = w1_ref.shape[1]
    w1_ref[...] = total[:, :hidden]
    w2_ref[...] = total[:, hidden:]


def finish_attention(*refs):
    *parts, qkv_ref, proj_ref = refs
    total = total_of(*parts)
    cols = qkv_ref.shape[2]
    for i in range(3):
        qkv_ref[i] = total[:, i * cols : (i + 1) * cols]
    proj_ref[...] = total[:, 3 * cols :]


def gather_small(ln_ref, n0, n1, n2, h0, h1, h2, z0, z1, z2, bias_ref, out_ref):
    width, hidden, cols = ln_ref.shape[1], h0.shape[1], bias_ref.shape[1] // 3
    out_ref[...] = jnp.zeros(out_ref.shape, F32)
    out_ref[0:2, :width] = ln_ref[...]
    out_ref[2:6, :width] = n0[...] + n1[...] + n2[...]
    mlp_sums = h0[...] + h1[...] + h2[...]
    out_ref[6:8, :width] = z0[...] + z1[...] + z2[...]
    out_ref[8:9, :hidden] = mlp_sums[0:1, :hidden]
    out_ref[11:12, :hidden] = mlp_sums[1:2, :hidden]
    out_ref[9:10, :cols] = bias_ref[:, :cols]
    out_ref[10:11, :cols] = bias_ref[:, 2 * cols :]


def small_core(own_ref, other_ref, out_ref):
    out_ref[...] = own_ref[...]
    out_ref[0:8, :] = own_ref[0:8, :] + other_ref[0:8, :]
    out_ref[8:9, :] = own_ref[8:9, :] + other_ref[11:12, :]


def finish_small(own_ref, other_ref, s1_ref, s2_ref, b2_ref, *outs):
    total, both = own_ref[...], own_ref[...] + other_ref[...]
    gain1, bias1, bqv, bp, scale1, gain2, bias2, b1, b2, scale2 = outs
    width, hidden, cols = gain1.shape[0], b1.shape[0], bqv.shape[1]
    gain1[...] = both[0, :width]
    bias1[...] = both[1, :width]
    gain2[...] = total[2, :width]
    bias2[...] = total[3, :width]
    scale1[...] = total[4, :width]
    bp[...] = total[5, :width] * s1_ref[...]
    scale2[...] = both[6, :width] + total[7, :width] * b2_ref[...]
    b2[...] = total[7, :width] * s2_ref[...]
    b1[...] = total[8, :hidden]
    bqv[0:1, :] = total[9:10, :cols]
    bqv[1:2, :] = total[10:11, :cols]


def solution(mesh):
    placed = (
        P("dp", None),
        P("dp", None, None),
        P(),
        P(),
        P(None, None, "tensor"),
        P(None, "tensor"),
        P("tensor", None),
        P(),
        P(),
        P(),
        P(),
        P(None, "tensor"),
        P("tensor"),
        P("tensor", None),
        P(),
        P(),
        P("dp", None),
    )
    return jax.shard_map(
        functools.partial(on_device, mesh.shape["dp"]),
        mesh=mesh,
        in_specs=placed,
        out_specs=(
            P("dp", None),
            P("dp", None),
            P(),
            P(),
            P(None, "dp", "tensor"),
            P(None, "tensor"),
            P("tensor", "dp"),
            P(),
            P(),
            P(),
            P(),
            P("dp", "tensor"),
            P("tensor"),
            P("tensor", "dp"),
            P(),
            P(),
        ),
        check_vma=False,
    )
```

```python
import functools
import math

import jax
import jax.numpy as jnp
from jax import lax
from jax.experimental import pallas as pl
from jax.experimental.pallas import tpu as pltpu
from jax.sharding import PartitionSpec as P

HD = 64
ROWS = 640
HALF = 320
EXTRA = 5
EPS = 1e-06
MASKED = -1e30
F32 = jnp.float32
BF16 = jnp.bfloat16
MIB = 1024 * 1024
VM = pltpu.VMEM


def nn(a, b):
    return lax.dot_general(a, b, (((1,), (0,)), ((), ())), preferred_element_type=F32)


def nt(a, b):
    return lax.dot_general(a, b, (((1,), (1,)), ((), ())), preferred_element_type=F32)


def tn(a, b):
    return lax.dot_general(a, b, (((0,), (0,)), ((), ())), preferred_element_type=F32)


def row(ref):
    return ref[...].reshape(1, ref.shape[-1])


def stats(v):
    mean = jnp.mean(v, axis=-1, keepdims=True)
    centred = v - mean
    spread = jnp.mean(centred * centred, axis=-1, keepdims=True)
    rstd = lax.rsqrt(spread + EPS)
    return centred * rstd, rstd


def ends_of(grid_ref, pack):
    ends = []
    total = jnp.int32(0)
    for image in range(4):
        total = total + grid_ref[pack, image, 0] * grid_ref[pack, image, 1] + EXTRA
        ends.append(total)
    return ends


def segment_at(position, ends):
    found = jnp.zeros(position.shape, jnp.int32)
    for end in ends:
        found = found + jnp.where(position >= end, 1, 0)
    return found


def key_extras(ends, base):
    shape = (ROWS, 128)
    seg = segment_at(lax.broadcasted_iota(jnp.int32, shape, 0), ends)
    lane = lax.broadcasted_iota(jnp.int32, shape, 1) - base
    mask = jnp.where(lane == seg, 0.0, MASKED)
    inside = (lane >= 0) & (lane < 5)
    ones = (lane >= 5) & (lane < 8)
    return jnp.where(inside, mask, jnp.where(ones, 1.0, 0.0)).astype(BF16)


def query_extras(ends, shift):
    shape = (16, ROWS)
    part = lax.broadcasted_iota(jnp.int32, shape, 0)
    if ends is None:
        extra = jnp.zeros(shape, F32)
    else:
        seg = segment_at(lax.broadcasted_iota(jnp.int32, shape, 1), ends)
        extra = jnp.where(part == seg, 1.0, 0.0)
    if shift is not None:
        high = shift.astype(BF16).astype(F32)
        rest = shift - high
        middle = rest.astype(BF16).astype(F32)
        low = rest - middle
        extra = jnp.where(part == 5, high, extra)
        extra = jnp.where(part == 6, middle, extra)
        extra = jnp.where(part == 7, low, extra)
    return jnp.concatenate([extra.astype(BF16), jnp.zeros((48, ROWS), BF16)], axis=0)


def keys_of(head, tiles_ref, start, low_extra, high_extra):
    lane = lax.broadcasted_iota(jnp.int32, (ROWS, 128), 1)
    at = start + 128 * (head // 2)
    tile = tiles_ref[:, at : at + 128]
    if head % 2 == 0:
        return jnp.where(lane < 64, tile, high_extra)
    return jnp.where(lane < 64, low_extra, tile)


def queries_of(head, rows_ref, extra):
    own = rows_ref[64 * head : 64 * head + 64, :]
    return jnp.concatenate([own, extra] if head % 2 == 0 else [extra, own], axis=0)


def attention_forward(
    pack,
    place_ref,
    grid_ref,
    x_ref,
    gain_ref,
    bias_ref,
    w_ref,
    bqv_ref,
    saved_ref,
    keep_ref,
    send_ref,
    lse_ref,
    qt_ref,
    vt_ref,
    ot_ref,
    o_ref,
):
    gain, bias = row(gain_ref), row(bias_ref)
    width = x_ref.shape[1]
    for r in range(0, ROWS, 160):
        normed, _ = stats(x_ref[r : r + 160, :].astype(F32))
        saved_ref[r : r + 160, :width] = (normed * gain + bias).astype(BF16)
    n1 = saved_ref[:, :width]
    cols = 3 * HD
    q = (nt(n1, w_ref[0]) + bqv_ref[0:1, :]) * (1.0 / math.sqrt(HD))
    saved_ref[:, width : width + cols] = q.astype(BF16)
    qt_ref[...] = q.T.astype(BF16)
    saved_ref[:, width + 256 : width + 256 + cols] = nt(n1, w_ref[1]).astype(BF16)
    v = nt(n1, w_ref[2]) + bqv_ref[1:2, :]
    saved_ref[:, width + 512 : width + 512 + cols] = v.astype(BF16)
    vt_ref[...] = v.T.astype(BF16)
    ends = ends_of(grid_ref, pack)
    low_extra, high_extra = key_extras(ends, 0), key_extras(ends, 64)
    extra = query_extras(ends, None)
    for head in range(3):
        s = nn(keys_of(head, saved_ref, width + 256, low_extra, high_extra), queries_of(head, qt_ref, extra))
        top = jnp.max(s, axis=0, keepdims=True)
        e = jnp.exp(s - top)
        total = jnp.sum(e, axis=0, keepdims=True)
        o = nn(vt_ref[64 * head : 64 * head + 64, :], e.astype(BF16)) / total
        ot_ref[64 * head : 64 * head + 64, :] = o
        lse_ref[head : head + 1, :] = top + jnp.log(total)
    o_ref[...] = ot_ref[...].T
    half = place_ref[0]
    saved_ref[:, width + 768 : width + 768 + cols] = o_ref[...].astype(BF16)
    keep_ref[...] = o_ref[pl.ds(pl.multiple_of(half * HALF, HALF), HALF), :].astype(BF16)
    send_ref[...] = o_ref[pl.ds(pl.multiple_of((1 - half) * HALF, HALF), HALF), :].astype(BF16)


def attention_backward(
    pack,
    has_sum,
    last,
    place_ref,
    grid_ref,
    mine_ref,
    other_ref,
    wp_ref,
    w_ref,
    saved_ref,
    lse_ref,
    *rest,
):
    if has_sum:
        g_in_ref, b_in_ref, *rest = rest
    if last:
        gain_ref, bias_ref, keep_ref, send_ref, l_ref, *rest = rest
    else:
        keep_ref, send_ref, *rest = rest
    g_ref, b_ref, dy_ref, do_ref, dot_ref, dqt_ref, dqkv_ref, dn_ref, qt_ref, kt_ref = rest
    half = place_ref[0]
    dy_ref[pl.ds(pl.multiple_of(half * HALF, HALF), HALF), :] = mine_ref[...]
    dy_ref[pl.ds(pl.multiple_of((1 - half) * HALF, HALF), HALF), :] = other_ref[...]
    dy = dy_ref[...]
    do_ref[...] = nt(dy, wp_ref[...]).astype(BF16)
    dot_ref[...] = nt(wp_ref[...], dy).astype(BF16)
    ends = ends_of(grid_ref, pack)
    low_extra, high_extra = key_extras(ends, 0), key_extras(ends, 64)
    cols = 3 * HD
    width = dy.shape[1]
    q_at, k_at, v_at = width, width + 256, width + 512
    qt_ref[...] = saved_ref[:, q_at : q_at + cols].T
    kt_ref[...] = saved_ref[:, k_at : k_at + cols].T
    o = saved_ref[:, width + 768 : width + 768 + cols]
    weighted = o.astype(F32) * do_ref[...].astype(F32)
    dqt_ref[...] = weighted.T
    inners = [jnp.sum(dqt_ref[64 * h : 64 * h + 64, :], axis=0, keepdims=True) for h in range(3)]
    for head in range(3):
        a, b = 64 * head, 64 * head + 64
        inner = inners[head]
        shifted = query_extras(ends, -lse_ref[head : head + 1, :])
        p = jnp.exp(
            nn(keys_of(head, saved_ref, k_at, low_extra, high_extra), queries_of(head, qt_ref, shifted))
        )
        dp = nn(
            keys_of(head, saved_ref, v_at, low_extra, high_extra),
            queries_of(head, dot_ref, query_extras(None, -inner)),
        )
        ds = (p * dp).astype(BF16)
        dqkv_ref[:, 2 * cols + a : 2 * cols + b] = nn(p.astype(BF16), do_ref[:, a:b]).astype(BF16)
        dqkv_ref[:, cols + a : cols + b] = nn(ds, saved_ref[:, q_at + a : q_at + b]).astype(BF16)
        dqt_ref[a:b, :] = nn(kt_ref[a:b, :], ds)
    dqkv_ref[:, :cols] = (dqt_ref[...].T * (1.0 / math.sqrt(HD))).astype(BF16)
    dn = nn(dqkv_ref[:, :cols], w_ref[0])
    dn = dn + nn(dqkv_ref[:, cols : 2 * cols], w_ref[1])
    dn = dn + nn(dqkv_ref[:, 2 * cols : 3 * cols], w_ref[2])
    dn_ref[...] = dn
    keep_ref[...] = dn_ref[pl.ds(pl.multiple_of(half * HALF, HALF), HALF), :].astype(BF16)
    send_ref[...] = dn_ref[pl.ds(pl.multiple_of((1 - half) * HALF, HALF), HALF), :].astype(BF16)
    g_qkv = tn(saved_ref[:, :width], dqkv_ref[...])
    g_proj = tn(dy, o)
    if has_sum:
        g_qkv = g_qkv + g_in_ref[:, : 3 * cols].astype(F32)
        g_proj = g_proj + g_in_ref[:, 3 * cols :].astype(F32)
    g_ref[:, : 3 * cols] = g_qkv.astype(g_ref.dtype)
    g_ref[:, 3 * cols :] = g_proj.astype(g_ref.dtype)
    sums = jnp.sum(dqkv_ref[...].astype(F32), axis=0, keepdims=True)
    sums = sums + b_in_ref[...] if has_sum else sums
    b_ref[...] = sums
    if last:
        plain = jnp.zeros((width, 1), F32)
        mixed = jnp.zeros((width, 1), F32)
        for c in range(3):
            at = slice(c * cols, (c + 1) * cols)
            w = w_ref[c].astype(F32).T
            plain = plain + jnp.sum(w * sums[:, at], axis=1, keepdims=True)
            mixed = mixed + jnp.sum(w * g_qkv[:, at], axis=1, keepdims=True)
        wide = jnp.concatenate([mixed, plain, jnp.zeros((width, 126), F32)], axis=1).T
        l_ref[0:1, :] = (wide[0:1, :] - row(bias_ref) * wide[1:2, :]) / row(gain_ref)
        l_ref[1:2, :] = wide[1:2, :]


def hidden_part(n2, dz, w1_ref, b1, w2_ref):
    u = nn(n2, w1_ref[...]) + b1
    cdf = 0.5 * (1.0 + lax.erf(u * (1.0 / math.sqrt(2.0))))
    density = jnp.exp(-0.5 * (u * u)) * (1.0 / math.sqrt(2.0 * math.pi))
    g = (u * cdf).astype(BF16)
    du = (nt(dz, w2_ref[...]) * (cdf + u * density)).astype(BF16)
    return g, du, nt(du, w1_ref[...])


def project_mlp(
    pack,
    place_ref,
    grid_ref,
    x_ref,
    o0,
    o1,
    o2,
    o3,
    p0,
    p1,
    p2,
    p3,
    bp_ref,
    s1_ref,
    gain_ref,
    bias_ref,
    cot_ref,
    s2_ref,
    w1_ref,
    b1_ref,
    w2_ref,
    v1_ref,
    c1_ref,
    v2_ref,
    yb_ref,
    n2_ref,
    dn_ref,
    g_ref,
    du_ref,
    dz_ref,
    sum_ref,
):
    y0, y1, y2, y3 = (nn(o[...], p[...]).astype(BF16).astype(F32) for o, p in ((o0, p0), (o1, p1), (o2, p2), (o3, p3)))
    yb = (y0 + y1) + (y2 + y3) + row(bp_ref)
    yb_ref[...] = yb.astype(BF16)
    normed, _ = stats(x_ref[...].astype(F32) + row(s1_ref) * yb)
    n2 = (normed * row(gain_ref) + row(bias_ref)).astype(BF16)
    n2_ref[...] = n2
    dd = cot_ref[...].astype(F32) * live_half(grid_ref, pack, place_ref[0])
    dz = (row(s2_ref) * dd).astype(BF16)
    dz_ref[...] = dz
    hidden = w1_ref.shape[1]
    g, du, dn = hidden_part(n2, dz, w1_ref, row(b1_ref), w2_ref)
    g_ref[:, :hidden] = g
    du_ref[:, :hidden] = du
    sum_ref[0:1, :] = colsum(du.astype(F32))
    g, du, dn_other = hidden_part(n2, dz, v1_ref, row(c1_ref), v2_ref)
    g_ref[:, hidden:] = g
    du_ref[:, hidden:] = du
    sum_ref[1:2, :] = colsum(du.astype(F32))
    dn_ref[...] = (dn + dn_other).astype(BF16)


def mlp_output(pack, place_ref, grid_ref, g_ref, w2_ref, v2_ref, cot_ref, z_ref, sum_ref):
    hidden = w2_ref.shape[0]
    z = nn(g_ref[:, :hidden], w2_ref[...]) + nn(g_ref[:, hidden:], v2_ref[...])
    z_ref[...] = z.astype(BF16)
    dd = cot_ref[...].astype(F32) * live_half(grid_ref, pack, place_ref[0])
    sum_ref[0:1, :] = colsum(dd * z)
    sum_ref[1:2, :] = colsum(dd)


def add_rows(a_ref, b_ref, out_ref):
    out_ref[...] = (a_ref[...].astype(F32) + b_ref[...].astype(F32)).astype(BF16)


def mlp_weights(n0, n1, n2, z0, z1, z2, u0, u1, u2, g0, g1, g2, *rest):
    *added, out_ref = rest
    mid = u0.shape[1]
    first = tn(n0[...], u0[...]) + tn(n1[...], u1[...]) + tn(n2[...], u2[...])
    second = tn(z0[...], g0[...]) + tn(z1[...], g1[...]) + tn(z2[...], g2[...])
    if added:
        first = first + added[0][:, :mid].astype(F32)
        second = second + added[0][:, mid:].astype(F32)
    out_ref[:, :mid] = first.astype(BF16)
    out_ref[:, mid:] = second.astype(BF16)


def live_half(grid_ref, pack, half):
    position = lax.broadcasted_iota(jnp.int32, (HALF, 1), 0) + half * HALF
    return jnp.where(position < ends_of(grid_ref, pack)[3], 1.0, 0.0)


def colsum(v):
    return jnp.sum(v, axis=0, keepdims=True)


def norm2_backward(
    pack, place_ref, grid_ref, a_ref, b_ref, x_ref, cot_ref, yb_ref, s1_ref, gain_ref, dh_ref, dy_ref, sum_ref
):
    half = place_ref[0]
    live = live_half(grid_ref, pack, half)
    scale = row(s1_ref)
    yb = yb_ref[...].astype(F32)
    h1 = x_ref[...].astype(F32) + scale * yb
    nh, rstd = stats(h1)
    dn2 = a_ref[...].astype(F32) + b_ref[...].astype(F32)
    e = dn2 * row(gain_ref)
    inner = e - jnp.mean(e, axis=-1, keepdims=True) - nh * jnp.mean(e * nh, axis=-1, keepdims=True)
    dh1 = cot_ref[...].astype(F32) * live + inner * rstd
    dh_ref[...] = dh1.astype(BF16)
    dy_ref[...] = (scale * dh1).astype(BF16)
    sum_ref[0:1, :] = colsum(dn2 * nh)
    sum_ref[1:2, :] = colsum(dn2)
    sum_ref[2:3, :] = colsum(dh1 * yb)
    sum_ref[3:4, :] = colsum(dh1)


def last_rows(
    pack,
    has_rows,
    place_ref,
    grid_ref,
    a1_ref,
    b1_ref,
    a3_ref,
    b3_ref,
    x_ref,
    dh_ref,
    yb_ref,
    gain_ref,
    s1_ref,
    s2_ref,
    bf_ref,
    *rest,
):
    gt_ref, out_ref, send_ref = rest[2:] if has_rows else rest
    live = live_half(grid_ref, pack, place_ref[0])
    x = x_ref[...].astype(F32)
    zb = a3_ref[...].astype(F32) + b3_ref[...].astype(F32) + row(bf_ref)
    out = (live * (x + row(s1_ref) * yb_ref[...].astype(F32) + row(s2_ref) * zb)).astype(BF16)
    out_ref[...] = out
    send_ref[HALF:, :] = out
    nx, rstd = stats(x)
    e = (a1_ref[...].astype(F32) + b1_ref[...].astype(F32)) * row(gain_ref)
    inner = e - jnp.mean(e, axis=-1, keepdims=True) - nx * jnp.mean(e * nx, axis=-1, keepdims=True)
    gt = (dh_ref[...].astype(F32) + inner * rstd).astype(BF16)
    gt_ref[...] = gt
    send_ref[:HALF, :] = gt


def place_rows(place_ref, *refs):
    got, (gt_ref, out_ref, sems) = refs[: len(refs) - 5], refs[len(refs) - 3 :]
    copies = []
    for p, ref in enumerate(got):
        at = pl.ds(pl.multiple_of((2 * p + 1 - place_ref[0]) * HALF, HALF), HALF)
        copies.append(pltpu.make_async_copy(ref.at[pl.ds(0, HALF), :], gt_ref.at[at, :], sems.at[2 * p]))
        copies.append(pltpu.make_async_copy(ref.at[pl.ds(HALF, HALF), :], out_ref.at[at, :], sems.at[2 * p + 1]))
    for copy in copies:
        copy.start()
    for copy in copies:
        copy.wait()


def full():
    return pl.BlockSpec(memory_space=VM)


def smem():
    return pl.BlockSpec(memory_space=pltpu.SMEM)


def shaped(*shape, dtype=BF16):
    return jax.ShapeDtypeStruct(shape, dtype)


def kernel_call(pinned, body, operands, in_specs, out_shape, flops, place=None, out_specs=None, scratch=(), steps=1, limit=16, name=None, after=(), aliases=None):
    prefetch = 0 if place is None else 1
    operands = [pltpu.with_memory_space_constraint(o, pltpu.HBM) if id(o) in pinned else o for o in operands]
    count = len(out_shape)
    moved = sum(math.prod(s.shape) * s.dtype.itemsize for s in out_shape)
    moved += sum(o.size * o.dtype.itemsize for o in operands)
    if after:
        skip = prefetch + len(operands)
        inner = body

        def body(*refs):
            inner(*refs[:skip], *refs[skip + len(after) :])

        operands = (*operands, *after)
        in_specs = (*in_specs, *(pl.BlockSpec(memory_space=pl.ANY) for _ in after))
    fixed = []
    for spec, operand in zip(in_specs, operands):
        if spec is None:
            rank = operand.ndim
            spec = pl.BlockSpec(operand.shape, lambda *_, rank=rank: (0,) * rank)
        fixed.append(spec)
    outs = []
    for index, shape in enumerate(out_shape):
        spec = out_specs[index] if out_specs else None
        if spec is None:
            rank = len(shape.shape)
            spec = pl.BlockSpec(shape.shape, lambda *_, rank=rank: (0,) * rank)
        outs.append(spec)
    grid_spec = pltpu.PrefetchScalarGridSpec(
        num_scalar_prefetch=prefetch,
        grid=(steps,),
        in_specs=fixed,
        out_specs=outs,
        scratch_shapes=list(scratch),
    )
    made = pl.pallas_call(
        body,
        out_shape=list(out_shape),
        grid_spec=grid_spec,
        input_output_aliases={prefetch + k: v for k, v in (aliases or {}).items()},
        compiler_params=pltpu.CompilerParams(vmem_limit_bytes=limit * MIB),
        cost_estimate=pl.CostEstimate(flops=3 * 10**10, bytes_accessed=int(moved), transcendentals=0),
        name=name,
    )
    del count
    return made(*(() if place is None else (place,)), *operands)


CORE = [(0, 1), (1, 0), (2, 3), (3, 2)]
OVER_Y = [(0, 2), (2, 0), (1, 3), (3, 1)]


def to_core(v):
    return lax.ppermute(v, "tensor", CORE)


def to_far(v):
    return lax.ppermute(v, "tensor", [(0, 3), (3, 0), (1, 2), (2, 1)])


def to_y(v):
    return lax.ppermute(v, "tensor", OVER_Y)


def to_dp(v, flip, count):
    return lax.ppermute(v, "dp", [(i, i ^ flip) for i in range(count)])


def swapped(grads, count):
    rows, columns = grads.shape
    return lax.all_to_all(grads.reshape(count, rows // count, columns), "dp", 0, 0)


def summed_share(grads, extra, count):
    rows, columns = grads.shape
    low, high = lax.axis_index("dp") % 2, lax.axis_index("dp") // 2
    blocks = grads.reshape(count, rows // count, columns)
    blocks = jnp.concatenate([jnp.broadcast_to(extra, (count, *extra.shape)), blocks], axis=1)
    blocks = blocks.reshape(count // 2, 2, -1, columns)
    mine = lax.dynamic_index_in_dim(blocks, low, 1, keepdims=False)
    theirs = lax.dynamic_index_in_dim(blocks, 1 - low, 1, keepdims=False)
    blocks = (mine.astype(F32) + to_dp(theirs, 1, count).astype(F32)).astype(BF16)
    parts = [lax.dynamic_index_in_dim(blocks, high, 0)]
    for flip in range(1, count // 2):
        parts.append(to_dp(lax.dynamic_index_in_dim(blocks, high ^ flip, 0), 2 * flip, count))
    return parts


def on_device(
    count,
    tokens,
    patch_grids,
    ln1_gain,
    ln1_bias,
    w_qkv,
    b_qv,
    w_proj,
    b_proj,
    scale1,
    ln2_gain,
    ln2_bias,
    w_fc1,
    b_fc1,
    w_fc2,
    b_fc2,
    scale2,
    cotangent,
):
    packs = patch_grids.shape[0]
    w_qkv = w_qkv.transpose(0, 2, 1)
    width = tokens.shape[1]
    cols = w_qkv.shape[1]
    hidden = w_fc1.shape[1]
    half = lax.axis_index("tensor") % 2
    place = jnp.full((1,), half, jnp.int32)

    fixed = (tokens, cotangent, ln1_gain, ln1_bias, b_qv, b_proj, scale1, ln2_gain, ln2_bias, b_fc1, b_fc2, scale2, w_qkv)
    call = functools.partial(kernel_call, [id(v) for v in fixed])

    def whole_pack(p):
        return pl.BlockSpec((ROWS, width), lambda *_, p=p: (p, 0))

    def half_pack(p):
        return pl.BlockSpec((HALF, width), lambda i, at, p=p: (2 * p + at[0], 0))

    wp1 = to_core(w_proj)
    wp2 = to_y(w_proj)
    wp3 = to_far(w_proj)
    near_w1, near_w2, near_b1 = to_core(w_fc1), to_core(w_fc2), to_core(b_fc1)

    previous = []

    def run(*args, after=(), **settings):
        made = call(*args, after=(*previous, *after), **settings)
        previous[:] = [made[-1]]
        return made

    def near_sum(keep, send, name):
        (total,) = run(add_rows, (keep, send), (None, None), (shaped(HALF, width),), HALF * width, name=name)
        return total

    kept = []
    heads = []
    for p in range(packs):
        saved, keep, send, lse = run(
            functools.partial(attention_forward, p),
            (patch_grids, tokens, ln1_gain, ln1_bias, w_qkv, b_qv),
            (smem(), whole_pack(p), None, None, None, None),
            (pltpu.HBM((ROWS, width + 1024), BF16), shaped(HALF, cols), shaped(HALF, cols), shaped(8, ROWS, dtype=F32)),
            2 * ROWS * width * 3 * cols + 4 * 3 * ROWS * ROWS * 256,
            place=place,
            scratch=(
                pltpu.VMEM((cols, ROWS), BF16),
                pltpu.VMEM((cols, ROWS), BF16),
                pltpu.VMEM((cols, ROWS), F32),
                pltpu.VMEM((ROWS, cols), F32),
            ),
            name=f"attention_forward_{p}",
            after=((), (near_w1, near_w2, near_b1, wp1), (heads[0][1], wp2, wp3) if heads else ())[p] if p < 3 else (),
        )
        kept.append((saved, lse))
        heads.append((keep, to_core(send), to_y(keep), to_far(send)))

    parts = []

    def hidden_pack(p):
        parts.append(
            run(
                functools.partial(project_mlp, p),
                (
                    patch_grids,
                    tokens,
                    *heads[p],
                    w_proj,
                    wp1,
                    wp2,
                    wp3,
                    b_proj,
                    scale1,
                    ln2_gain,
                    ln2_bias,
                    cotangent,
                    scale2,
                    w_fc1,
                    b_fc1,
                    w_fc2,
                    near_w1,
                    near_b1,
                    near_w2,
                ),
                (smem(), half_pack(p)) + (None,) * 12 + (half_pack(p),) + (None,) * 7,
                (
                    shaped(HALF, width),
                    shaped(HALF, width),
                    shaped(HALF, width),
                    shaped(HALF, 2 * hidden),
                    shaped(HALF, 2 * hidden),
                    shaped(HALF, width),
                    shaped(2, hidden, dtype=F32),
                ),
                8 * ROWS * width * hidden,
                place=place,
                limit=28,
                name=f"project_mlp_{p}",
            )
        )

    def weights(part, added, name):
        lanes = [pl.BlockSpec((HALF, 256), lambda i: (0, i)) for _ in range(2 * packs)]
        units = [pl.BlockSpec((HALF, hidden), lambda i: (0, part)) for _ in range(2 * packs)]
        (g_fc,) = run(
            mlp_weights,
            [v[i] for i in (1, 5, 4, 3) for v in parts] + added,
            lanes + units + [pl.BlockSpec((256, 2 * hidden), lambda i: (i, 0)) for _ in added],
            (shaped(width, 2 * hidden),),
            4 * packs * ROWS * width * hidden,
            out_specs=[pl.BlockSpec((256, 2 * hidden), lambda i: (i, 0))],
            steps=width // 256,
            name=name,
        )
        return g_fc

    def norm2_pack(p, near, far):
        dh1, dy, part = run(
            functools.partial(norm2_backward, p),
            (patch_grids, near, far, tokens, cotangent, parts[p][0], scale1, ln2_gain),
            (smem(), None, None, half_pack(p), half_pack(p), None, None, None),
            (shaped(HALF, width), shaped(HALF, width), shaped(4, width, dtype=F32)),
            30 * HALF * width,
            place=place,
            name=f"norm2_backward_{p}",
        )
        return dh1, dy, to_core(dy), part

    def attention_pack(p, dy, dy_other, before):
        saved, lse = kept[p]
        last = p == packs - 1
        operands = [patch_grids, dy, dy_other, w_proj, w_qkv, saved, lse, *before]
        if last:
            operands += [ln1_gain, ln1_bias]
        keep, send, *norm_sums, g_attn, bias_sums = run(
            functools.partial(attention_backward, p, bool(before), last),
            operands,
            [smem()] + [None] * (len(operands) - 1),
            (
                shaped(HALF, width),
                shaped(HALF, width),
                *([shaped(2, width, dtype=F32)] if last else []),
                shaped(width, 4 * cols),
                shaped(1, 3 * cols, dtype=F32),
            ),
            12 * ROWS * width * cols + 10 * 3 * ROWS * ROWS * 256,
            place=place,
            scratch=(
                pltpu.VMEM((ROWS, width), BF16),
                pltpu.VMEM((ROWS, cols), BF16),
                pltpu.VMEM((cols, ROWS), BF16),
                pltpu.VMEM((cols, ROWS), F32),
                pltpu.VMEM((ROWS, 3 * cols), BF16),
                pltpu.VMEM((ROWS, width), F32),
                pltpu.VMEM((cols, ROWS), BF16),
                pltpu.VMEM((cols, ROWS), BF16),
            ),
            name=f"attention_backward_{p}",
        )
        return keep, to_core(send), (g_attn, bias_sums), norm_sums

    anywhere = pl.BlockSpec(memory_space=pl.ANY)
    whole_rows = pltpu.HBM((packs * ROWS, width), BF16)
    rows = []
    sent = []

    def last_pack(p, far1, far3):
        operands = [patch_grids, near1[p], far1, near3[p][0], far3, tokens, back2[p][0], parts[p][0], ln1_gain, scale1, scale2, b_fc2]
        specs = [smem(), None, None, None, None, half_pack(p)] + [None] * 6
        made = run(
            functools.partial(last_rows, p, bool(rows)),
            operands + rows,
            specs + [anywhere] * len(rows),
            (whole_rows, whole_rows, shaped(2 * HALF, width)),
            30 * HALF * width,
            place=place,
            out_specs=[half_pack(p), half_pack(p), None],
            name=f"last_rows_{p}",
            aliases={len(operands) + i: i for i in range(len(rows))},
        )
        rows[:] = made[:2]
        sent.append(to_core(made[2]))

    for p in range(packs):
        hidden_pack(p)
    far2 = [to_y(v[2]) for v in parts]
    near3 = []

    def output_part(p):
        near3.append(
            run(
                functools.partial(mlp_output, p),
                (patch_grids, parts[p][3], w_fc2, near_w2, cotangent),
                (smem(), None, None, None, half_pack(p)),
                (shaped(HALF, width), shaped(2, width, dtype=F32)),
                4 * HALF * width * hidden,
                place=place,
                name=f"mlp_output_{p}",
            )
        )

    output_part(0)
    back2 = [norm2_pack(0, parts[0][2], far2[0])]
    g_near = to_core(weights(1, [], "mlp_weights_near"))
    back2.append(norm2_pack(1, parts[1][2], far2[1]))
    near1 = []
    carried = ()
    for p in range(packs):
        keep, other, carried, norm_sums = attention_pack(p, back2[p][1], back2[p][2], carried)
        if p == 0:
            fc_parts = swapped(weights(0, [g_near], "mlp_weights_own"), count)
        else:
            output_part(p)
        if p == packs - 1:
            (small,) = run(
                gather_small,
                (norm_sums[0], *[b[3] for b in back2], *[v[6] for v in parts], *[v[1] for v in near3], carried[1]),
                (None,) * (2 + 3 * packs),
                (shaped(16, max(width, hidden), dtype=F32),),
                width,
                name="gather_small",
            )
        near1.append(near_sum(keep, other, f"near1_{p}"))
        if p + 2 < packs:
            back2.append(norm2_pack(p + 2, parts[p + 2][2], far2[p + 2]))
    far1 = [to_y(v) for v in near1]
    far3 = [to_y(v[0]) for v in near3]
    (small,) = run(
        small_core, (small, to_core(small)), (None, None), (shaped(*small.shape),), width, name="small_core"
    )
    attn_parts = summed_share(carried[0], small, count)

    for p in range(packs - 1):
        last_pack(p, far1[p], far3[p])
    grad_w_fc1, grad_w_fc2 = run(
        finish_mlp,
        (fc_parts,),
        (None,),
        (shaped(width // count, hidden, dtype=F32), shaped(width // count, hidden, dtype=F32)),
        width * hidden,
        name="finish_mlp",
    )
    last_pack(packs - 1, far1[-1], far3[-1])
    vector = shaped(width, dtype=F32)
    grad_w_qkv, grad_w_proj, small = run(
        finish_attention,
        attn_parts,
        (None,) * len(attn_parts),
        (shaped(3, width // count, cols, dtype=F32), shaped(width // count, cols, dtype=F32), shaped(*small.shape, dtype=F32)),
        width * cols,
        name="finish_attention",
    )
    vectors = run(
        finish_small,
        (small, to_y(small), scale1, scale2, b_fc2),
        (None,) * 5,
        (vector, vector, shaped(2, cols, dtype=F32), vector, vector, vector, vector, shaped(hidden, dtype=F32), vector, vector),
        width,
        name="finish_small",
    )
    gain1, bias1, bqv, bp, sc1, gain2, bias2, b1, b2, sc2 = vectors
    grad_tokens, out = call(
        place_rows,
        [*sent, *rows],
        [None] * packs + [anywhere] * 2,
        (whole_rows, whole_rows),
        packs * ROWS * width,
        place=place,
        out_specs=[anywhere, anywhere],
        scratch=(pltpu.SemaphoreType.DMA((2 * packs,)),),
        name="place_rows",
        aliases={packs: 0, packs + 1: 1},
    )
    return (
        out,
        grad_tokens,
        gain1,
        bias1,
        grad_w_qkv,
        bqv,
        grad_w_proj.T,
        bp,
        sc1,
        gain2,
        bias2,
        grad_w_fc1,
        b1,
        grad_w_fc2.T,
        b2,
        sc2,
    )


def total_of(*parts_refs):
    parts = [ref[i].astype(F32) for ref in parts_refs for i in range(ref.shape[0])]
    while len(parts) > 1:
        parts = [a + b for a, b in zip(parts[::2], parts[1::2])]
    return parts[0]


def finish_mlp(parts_ref, w1_ref, w2_ref):
    total = total_of(parts_ref)
    hidden = w1_ref.shape[1]
    w1_ref[...] = total[:, :hidden]
    w2_ref[...] = total[:, hidden:]


def finish_attention(*refs):
    *parts, qkv_ref, proj_ref, small_ref = refs
    total = total_of(*parts)
    small = small_ref.shape[0]
    share, cols = proj_ref.shape
    for i in range(3):
        qkv_ref[i] = total[small : small + share, i * cols : (i + 1) * cols]
    proj_ref[...] = total[small : small + share, 3 * cols :]
    small_ref[...] = total[:small, :]


def gather_small(ln_ref, n0, n1, n2, h0, h1, h2, z0, z1, z2, bias_ref, out_ref):
    width, hidden, cols = ln_ref.shape[1], h0.shape[1], bias_ref.shape[1] // 3
    out_ref[...] = jnp.zeros(out_ref.shape, F32)
    out_ref[0:2, :width] = ln_ref[...]
    out_ref[2:6, :width] = n0[...] + n1[...] + n2[...]
    mlp_sums = h0[...] + h1[...] + h2[...]
    out_ref[6:8, :width] = z0[...] + z1[...] + z2[...]
    out_ref[8:9, :hidden] = mlp_sums[0:1, :hidden]
    out_ref[11:12, :hidden] = mlp_sums[1:2, :hidden]
    out_ref[9:10, :cols] = bias_ref[:, :cols]
    out_ref[10:11, :cols] = bias_ref[:, 2 * cols :]


def small_core(own_ref, other_ref, out_ref):
    both = own_ref[...] + other_ref[...]
    out_ref[...] = own_ref[...].astype(BF16)
    out_ref[0:8, :] = both[0:8, :].astype(BF16)
    out_ref[8:9, :] = (own_ref[8:9, :] + other_ref[11:12, :]).astype(BF16)


def finish_small(own_ref, other_ref, s1_ref, s2_ref, b2_ref, *outs):
    total, both = own_ref[...], own_ref[...] + other_ref[...]
    gain1, bias1, bqv, bp, scale1, gain2, bias2, b1, b2, scale2 = outs
    width, hidden, cols = gain1.shape[0], b1.shape[0], bqv.shape[1]
    gain1[...] = both[0, :width]
    bias1[...] = both[1, :width]
    gain2[...] = total[2, :width]
    bias2[...] = total[3, :width]
    scale1[...] = total[4, :width]
    bp[...] = total[5, :width] * s1_ref[...]
    scale2[...] = both[6, :width] + total[7, :width] * b2_ref[...]
    b2[...] = total[7, :width] * s2_ref[...]
    b1[...] = total[8, :hidden]
    bqv[0:1, :] = total[9:10, :cols]
    bqv[1:2, :] = total[10:11, :cols]


def solution(mesh):
    placed = (
        P("dp", None),
        P("dp", None, None),
        P(),
        P(),
        P(None, None, "tensor"),
        P(None, "tensor"),
        P("tensor", None),
        P(),
        P(),
        P(),
        P(),
        P(None, "tensor"),
        P("tensor"),
        P("tensor", None),
        P(),
        P(),
        P("dp", None),
    )
    return jax.shard_map(
        functools.partial(on_device, mesh.shape["dp"]),
        mesh=mesh,
        in_specs=placed,
        out_specs=(
            P("dp", None),
            P("dp", None),
            P(),
            P(),
            P(None, "dp", "tensor"),
            P(None, "tensor"),
            P("tensor", "dp"),
            P(),
            P(),
            P(),
            P(),
            P("dp", "tensor"),
            P("tensor"),
            P("tensor", "dp"),
            P(),
            P(),
        ),
        check_vma=False,
    )
```

```python
import functools
import math

import jax
import jax.numpy as jnp
from jax import lax
from jax.experimental import pallas as pl
from jax.experimental.pallas import tpu as pltpu
from jax.sharding import PartitionSpec as P

HD = 64
ROWS = 640
HALF = 320
EXTRA = 5
EPS = 1e-06
MASKED = -1e30
F32 = jnp.float32
BF16 = jnp.bfloat16
MIB = 1024 * 1024
VM = pltpu.VMEM


def nn(a, b):
    return lax.dot_general(a, b, (((1,), (0,)), ((), ())), preferred_element_type=F32)


def nt(a, b):
    return lax.dot_general(a, b, (((1,), (1,)), ((), ())), preferred_element_type=F32)


def tn(a, b):
    return lax.dot_general(a, b, (((0,), (0,)), ((), ())), preferred_element_type=F32)


def row(ref):
    return ref[...].reshape(1, ref.shape[-1])


def stats(v):
    mean = jnp.mean(v, axis=-1, keepdims=True)
    centred = v - mean
    spread = jnp.mean(centred * centred, axis=-1, keepdims=True)
    rstd = lax.rsqrt(spread + EPS)
    return centred * rstd, rstd


def ends_of(grid_ref, pack):
    ends = []
    total = jnp.int32(0)
    for image in range(4):
        total = total + grid_ref[pack, image, 0] * grid_ref[pack, image, 1] + EXTRA
        ends.append(total)
    return ends


def segment_at(position, ends):
    found = jnp.zeros(position.shape, jnp.int32)
    for end in ends:
        found = found + jnp.where(position >= end, 1, 0)
    return found


def key_extras(ends, base):
    shape = (ROWS, 128)
    seg = segment_at(lax.broadcasted_iota(jnp.int32, shape, 0), ends)
    lane = lax.broadcasted_iota(jnp.int32, shape, 1) - base
    mask = jnp.where(lane == seg, 0.0, MASKED)
    inside = (lane >= 0) & (lane < 5)
    ones = (lane >= 5) & (lane < 8)
    return jnp.where(inside, mask, jnp.where(ones, 1.0, 0.0)).astype(BF16)


def query_extras(ends, shift):
    shape = (16, ROWS)
    part = lax.broadcasted_iota(jnp.int32, shape, 0)
    if ends is None:
        extra = jnp.zeros(shape, F32)
    else:
        seg = segment_at(lax.broadcasted_iota(jnp.int32, shape, 1), ends)
        extra = jnp.where(part == seg, 1.0, 0.0)
    if shift is not None:
        high = shift.astype(BF16).astype(F32)
        rest = shift - high
        middle = rest.astype(BF16).astype(F32)
        low = rest - middle
        extra = jnp.where(part == 5, high, extra)
        extra = jnp.where(part == 6, middle, extra)
        extra = jnp.where(part == 7, low, extra)
    return jnp.concatenate([extra.astype(BF16), jnp.zeros((48, ROWS), BF16)], axis=0)


def keys_of(head, tiles_ref, start, low_extra, high_extra):
    lane = lax.broadcasted_iota(jnp.int32, (ROWS, 128), 1)
    at = start + 128 * (head // 2)
    tile = tiles_ref[:, at : at + 128]
    if head % 2 == 0:
        return jnp.where(lane < 64, tile, high_extra)
    return jnp.where(lane < 64, low_extra, tile)


def queries_of(head, rows_ref, extra):
    own = rows_ref[64 * head : 64 * head + 64, :]
    return jnp.concatenate([own, extra] if head % 2 == 0 else [extra, own], axis=0)


def attention_forward(
    pack,
    place_ref,
    grid_ref,
    x_ref,
    gain_ref,
    bias_ref,
    w_ref,
    bqv_ref,
    saved_ref,
    keep_ref,
    send_ref,
    lse_ref,
    qt_ref,
    vt_ref,
    ot_ref,
    o_ref,
):
    gain, bias = row(gain_ref), row(bias_ref)
    width = x_ref.shape[1]
    for r in range(0, ROWS, 160):
        normed, _ = stats(x_ref[r : r + 160, :].astype(F32))
        saved_ref[r : r + 160, :width] = (normed * gain + bias).astype(BF16)
    n1 = saved_ref[:, :width]
    cols = 3 * HD
    q = (nt(n1, w_ref[0]) + bqv_ref[0:1, :]) * (1.0 / math.sqrt(HD))
    saved_ref[:, width : width + cols] = q.astype(BF16)
    qt_ref[...] = q.T.astype(BF16)
    saved_ref[:, width + 256 : width + 256 + cols] = nt(n1, w_ref[1]).astype(BF16)
    v = nt(n1, w_ref[2]) + bqv_ref[1:2, :]
    saved_ref[:, width + 512 : width + 512 + cols] = v.astype(BF16)
    vt_ref[...] = v.T.astype(BF16)
    ends = ends_of(grid_ref, pack)
    low_extra, high_extra = key_extras(ends, 0), key_extras(ends, 64)
    extra = query_extras(ends, None)
    for head in range(3):
        s = nn(keys_of(head, saved_ref, width + 256, low_extra, high_extra), queries_of(head, qt_ref, extra))
        top = jnp.max(s, axis=0, keepdims=True)
        e = jnp.exp(s - top)
        total = jnp.sum(e, axis=0, keepdims=True)
        o = nn(vt_ref[64 * head : 64 * head + 64, :], e.astype(BF16)) / total
        ot_ref[64 * head : 64 * head + 64, :] = o
        lse_ref[head : head + 1, :] = top + jnp.log(total)
    o_ref[...] = ot_ref[...].T
    half = place_ref[0]
    saved_ref[:, width + 768 : width + 768 + cols] = o_ref[...].astype(BF16)
    keep_ref[...] = o_ref[pl.ds(pl.multiple_of(half * HALF, HALF), HALF), :].astype(BF16)
    send_ref[...] = o_ref[pl.ds(pl.multiple_of((1 - half) * HALF, HALF), HALF), :].astype(BF16)


def attention_backward(
    pack,
    has_sum,
    last,
    place_ref,
    grid_ref,
    mine_ref,
    other_ref,
    wp_ref,
    w_ref,
    saved_ref,
    lse_ref,
    *rest,
):
    if has_sum:
        g_in_ref, b_in_ref, *rest = rest
    if last:
        gain_ref, bias_ref, keep_ref, send_ref, l_ref, *rest = rest
    else:
        keep_ref, send_ref, *rest = rest
    g_ref, b_ref, dy_ref, do_ref, dot_ref, dqt_ref, dqkv_ref, dn_ref, qt_ref, kt_ref = rest
    half = place_ref[0]
    dy_ref[pl.ds(pl.multiple_of(half * HALF, HALF), HALF), :] = mine_ref[...]
    dy_ref[pl.ds(pl.multiple_of((1 - half) * HALF, HALF), HALF), :] = other_ref[...]
    dy = dy_ref[...]
    do_ref[...] = nt(dy, wp_ref[...]).astype(BF16)
    dot_ref[...] = nt(wp_ref[...], dy).astype(BF16)
    ends = ends_of(grid_ref, pack)
    low_extra, high_extra = key_extras(ends, 0), key_extras(ends, 64)
    cols = 3 * HD
    width = dy.shape[1]
    q_at, k_at, v_at = width, width + 256, width + 512
    qt_ref[...] = saved_ref[:, q_at : q_at + cols].T
    kt_ref[...] = saved_ref[:, k_at : k_at + cols].T
    o = saved_ref[:, width + 768 : width + 768 + cols]
    weighted = o.astype(F32) * do_ref[...].astype(F32)
    dqt_ref[...] = weighted.T
    inners = [jnp.sum(dqt_ref[64 * h : 64 * h + 64, :], axis=0, keepdims=True) for h in range(3)]
    for head in range(3):
        a, b = 64 * head, 64 * head + 64
        inner = inners[head]
        shifted = query_extras(ends, -lse_ref[head : head + 1, :])
        p = jnp.exp(
            nn(keys_of(head, saved_ref, k_at, low_extra, high_extra), queries_of(head, qt_ref, shifted))
        )
        dp = nn(
            keys_of(head, saved_ref, v_at, low_extra, high_extra),
            queries_of(head, dot_ref, query_extras(None, -inner)),
        )
        ds = (p * dp).astype(BF16)
        dqkv_ref[:, 2 * cols + a : 2 * cols + b] = nn(p.astype(BF16), do_ref[:, a:b]).astype(BF16)
        dqkv_ref[:, cols + a : cols + b] = nn(ds, saved_ref[:, q_at + a : q_at + b]).astype(BF16)
        dqt_ref[a:b, :] = nn(kt_ref[a:b, :], ds)
    dqkv_ref[:, :cols] = (dqt_ref[...].T * (1.0 / math.sqrt(HD))).astype(BF16)
    dn = nn(dqkv_ref[:, :cols], w_ref[0])
    dn = dn + nn(dqkv_ref[:, cols : 2 * cols], w_ref[1])
    dn = dn + nn(dqkv_ref[:, 2 * cols : 3 * cols], w_ref[2])
    dn_ref[...] = dn
    keep_ref[...] = dn_ref[pl.ds(pl.multiple_of(half * HALF, HALF), HALF), :].astype(BF16)
    send_ref[...] = dn_ref[pl.ds(pl.multiple_of((1 - half) * HALF, HALF), HALF), :].astype(BF16)
    g_qkv = tn(saved_ref[:, :width], dqkv_ref[...])
    g_proj = tn(dy, o)
    if has_sum:
        g_qkv = g_qkv + g_in_ref[:, : 3 * cols].astype(F32)
        g_proj = g_proj + g_in_ref[:, 3 * cols :].astype(F32)
    g_ref[:, : 3 * cols] = g_qkv.astype(g_ref.dtype)
    g_ref[:, 3 * cols :] = g_proj.astype(g_ref.dtype)
    sums = jnp.sum(dqkv_ref[...].astype(F32), axis=0, keepdims=True)
    sums = sums + b_in_ref[...] if has_sum else sums
    b_ref[...] = sums
    if last:
        plain = jnp.zeros((width, 1), F32)
        mixed = jnp.zeros((width, 1), F32)
        for c in range(3):
            at = slice(c * cols, (c + 1) * cols)
            w = w_ref[c].astype(F32).T
            plain = plain + jnp.sum(w * sums[:, at], axis=1, keepdims=True)
            mixed = mixed + jnp.sum(w * g_qkv[:, at], axis=1, keepdims=True)
        wide = jnp.concatenate([mixed, plain, jnp.zeros((width, 126), F32)], axis=1).T
        l_ref[0:1, :] = (wide[0:1, :] - row(bias_ref) * wide[1:2, :]) / row(gain_ref)
        l_ref[1:2, :] = wide[1:2, :]


def hidden_part(n2, dz, w1_ref, b1, w2_ref):
    u = nn(n2, w1_ref[...]) + b1
    cdf = 0.5 * (1.0 + lax.erf(u * (1.0 / math.sqrt(2.0))))
    density = jnp.exp(-0.5 * (u * u)) * (1.0 / math.sqrt(2.0 * math.pi))
    g = (u * cdf).astype(BF16)
    du = (nt(dz, w2_ref[...]) * (cdf + u * density)).astype(BF16)
    return g, du, nt(du, w1_ref[...])


def project_mlp(
    pack,
    place_ref,
    grid_ref,
    x_ref,
    o0,
    o1,
    o2,
    o3,
    p0,
    p1,
    p2,
    p3,
    bp_ref,
    s1_ref,
    gain_ref,
    bias_ref,
    cot_ref,
    s2_ref,
    w1_ref,
    b1_ref,
    w2_ref,
    v1_ref,
    c1_ref,
    v2_ref,
    yb_ref,
    n2_ref,
    dn_ref,
    g_ref,
    du_ref,
    dz_ref,
    sum_ref,
):
    y0, y1, y2, y3 = (nn(o[...], p[...]).astype(BF16).astype(F32) for o, p in ((o0, p0), (o1, p1), (o2, p2), (o3, p3)))
    yb = (y0 + y1) + (y2 + y3) + row(bp_ref)
    yb_ref[...] = yb.astype(BF16)
    normed, _ = stats(x_ref[...].astype(F32) + row(s1_ref) * yb)
    n2 = (normed * row(gain_ref) + row(bias_ref)).astype(BF16)
    n2_ref[...] = n2
    dd = cot_ref[...].astype(F32) * live_half(grid_ref, pack, place_ref[0])
    dz = (row(s2_ref) * dd).astype(BF16)
    dz_ref[...] = dz
    hidden = w1_ref.shape[1]
    g, du, dn = hidden_part(n2, dz, w1_ref, row(b1_ref), w2_ref)
    g_ref[:, :hidden] = g
    du_ref[:, :hidden] = du
    sum_ref[0:1, :] = colsum(du.astype(F32))
    g, du, dn_other = hidden_part(n2, dz, v1_ref, row(c1_ref), v2_ref)
    g_ref[:, hidden:] = g
    du_ref[:, hidden:] = du
    sum_ref[1:2, :] = colsum(du.astype(F32))
    dn_ref[...] = (dn + dn_other).astype(BF16)


def mlp_output(pack, place_ref, grid_ref, g_ref, w2_ref, v2_ref, cot_ref, z_ref, sum_ref):
    hidden = w2_ref.shape[0]
    z = nn(g_ref[:, :hidden], w2_ref[...]) + nn(g_ref[:, hidden:], v2_ref[...])
    z_ref[...] = z.astype(BF16)
    dd = cot_ref[...].astype(F32) * live_half(grid_ref, pack, place_ref[0])
    sum_ref[0:1, :] = colsum(dd * z)
    sum_ref[1:2, :] = colsum(dd)


def add_rows(a_ref, b_ref, out_ref):
    out_ref[...] = (a_ref[...].astype(F32) + b_ref[...].astype(F32)).astype(BF16)


def mlp_weights(n0, n1, n2, z0, z1, z2, u0, u1, u2, g0, g1, g2, *rest):
    *added, out_ref = rest
    mid = u0.shape[1]
    first = tn(n0[...], u0[...]) + tn(n1[...], u1[...]) + tn(n2[...], u2[...])
    second = tn(z0[...], g0[...]) + tn(z1[...], g1[...]) + tn(z2[...], g2[...])
    if added:
        first = first + added[0][:, :mid].astype(F32)
        second = second + added[0][:, mid:].astype(F32)
    out_ref[:, :mid] = first.astype(BF16)
    out_ref[:, mid:] = second.astype(BF16)


def live_half(grid_ref, pack, half):
    position = lax.broadcasted_iota(jnp.int32, (HALF, 1), 0) + half * HALF
    return jnp.where(position < ends_of(grid_ref, pack)[3], 1.0, 0.0)


def colsum(v):
    return jnp.sum(v, axis=0, keepdims=True)


def norm2_backward(
    pack, place_ref, grid_ref, a_ref, b_ref, x_ref, cot_ref, yb_ref, s1_ref, gain_ref, dh_ref, dy_ref, sum_ref
):
    half = place_ref[0]
    live = live_half(grid_ref, pack, half)
    scale = row(s1_ref)
    yb = yb_ref[...].astype(F32)
    h1 = x_ref[...].astype(F32) + scale * yb
    nh, rstd = stats(h1)
    dn2 = a_ref[...].astype(F32) + b_ref[...].astype(F32)
    e = dn2 * row(gain_ref)
    inner = e - jnp.mean(e, axis=-1, keepdims=True) - nh * jnp.mean(e * nh, axis=-1, keepdims=True)
    dh1 = cot_ref[...].astype(F32) * live + inner * rstd
    dh_ref[...] = dh1.astype(BF16)
    dy_ref[...] = (scale * dh1).astype(BF16)
    sum_ref[0:1, :] = colsum(dn2 * nh)
    sum_ref[1:2, :] = colsum(dn2)
    sum_ref[2:3, :] = colsum(dh1 * yb)
    sum_ref[3:4, :] = colsum(dh1)


def last_rows(
    pack,
    has_rows,
    place_ref,
    grid_ref,
    a1_ref,
    b1_ref,
    a3_ref,
    b3_ref,
    x_ref,
    dh_ref,
    yb_ref,
    gain_ref,
    s1_ref,
    s2_ref,
    bf_ref,
    *rest,
):
    gt_ref, out_ref, send_ref = rest[2:] if has_rows else rest
    live = live_half(grid_ref, pack, place_ref[0])
    x = x_ref[...].astype(F32)
    zb = a3_ref[...].astype(F32) + b3_ref[...].astype(F32) + row(bf_ref)
    out = (live * (x + row(s1_ref) * yb_ref[...].astype(F32) + row(s2_ref) * zb)).astype(BF16)
    out_ref[...] = out
    send_ref[HALF:, :] = out
    nx, rstd = stats(x)
    e = (a1_ref[...].astype(F32) + b1_ref[...].astype(F32)) * row(gain_ref)
    inner = e - jnp.mean(e, axis=-1, keepdims=True) - nx * jnp.mean(e * nx, axis=-1, keepdims=True)
    gt = (dh_ref[...].astype(F32) + inner * rstd).astype(BF16)
    gt_ref[...] = gt
    send_ref[:HALF, :] = gt


def place_rows(place_ref, *refs):
    got, (gt_ref, out_ref, sems) = refs[: len(refs) - 5], refs[len(refs) - 3 :]
    copies = []
    for p, ref in enumerate(got):
        at = pl.ds(pl.multiple_of((2 * p + 1 - place_ref[0]) * HALF, HALF), HALF)
        copies.append(pltpu.make_async_copy(ref.at[pl.ds(0, HALF), :], gt_ref.at[at, :], sems.at[2 * p]))
        copies.append(pltpu.make_async_copy(ref.at[pl.ds(HALF, HALF), :], out_ref.at[at, :], sems.at[2 * p + 1]))
    for copy in copies:
        copy.start()
    for copy in copies:
        copy.wait()


def full():
    return pl.BlockSpec(memory_space=VM)


def smem():
    return pl.BlockSpec(memory_space=pltpu.SMEM)


def shaped(*shape, dtype=BF16):
    return jax.ShapeDtypeStruct(shape, dtype)


def kernel_call(pinned, body, operands, in_specs, out_shape, flops, place=None, out_specs=None, scratch=(), steps=1, limit=16, name=None, after=(), aliases=None):
    prefetch = 0 if place is None else 1
    operands = [pltpu.with_memory_space_constraint(o, pltpu.HBM) if id(o) in pinned else o for o in operands]
    count = len(out_shape)
    moved = sum(math.prod(s.shape) * s.dtype.itemsize for s in out_shape)
    moved += sum(o.size * o.dtype.itemsize for o in operands)
    if after:
        skip = prefetch + len(operands)
        inner = body

        def body(*refs):
            inner(*refs[:skip], *refs[skip + len(after) :])

        operands = (*operands, *after)
        in_specs = (*in_specs, *(pl.BlockSpec(memory_space=pl.ANY) for _ in after))
    fixed = []
    for spec, operand in zip(in_specs, operands):
        if spec is None:
            rank = operand.ndim
            spec = pl.BlockSpec(operand.shape, lambda *_, rank=rank: (0,) * rank)
        fixed.append(spec)
    outs = []
    for index, shape in enumerate(out_shape):
        spec = out_specs[index] if out_specs else None
        if spec is None:
            rank = len(shape.shape)
            spec = pl.BlockSpec(shape.shape, lambda *_, rank=rank: (0,) * rank)
        outs.append(spec)
    grid_spec = pltpu.PrefetchScalarGridSpec(
        num_scalar_prefetch=prefetch,
        grid=(steps,),
        in_specs=fixed,
        out_specs=outs,
        scratch_shapes=list(scratch),
    )
    made = pl.pallas_call(
        body,
        out_shape=list(out_shape),
        grid_spec=grid_spec,
        input_output_aliases={prefetch + k: v for k, v in (aliases or {}).items()},
        compiler_params=pltpu.CompilerParams(vmem_limit_bytes=limit * MIB),
        cost_estimate=pl.CostEstimate(flops=3 * 10**10, bytes_accessed=int(moved), transcendentals=0),
        name=name,
    )
    del count
    return made(*(() if place is None else (place,)), *operands)


CORE = [(0, 1), (1, 0), (2, 3), (3, 2)]
OVER_Y = [(0, 2), (2, 0), (1, 3), (3, 1)]


def to_core(v):
    return lax.ppermute(v, "tensor", CORE)


def to_far(v):
    return lax.ppermute(v, "tensor", [(0, 3), (3, 0), (1, 2), (2, 1)])


def to_y(v):
    return lax.ppermute(v, "tensor", OVER_Y)


def to_dp(v, flip, count):
    return lax.ppermute(v, "dp", [(i, i ^ flip) for i in range(count)])


def swapped(grads, count):
    rows, columns = grads.shape
    return lax.all_to_all(grads.reshape(count, rows // count, columns), "dp", 0, 0)


def summed_share(grads, extra, count):
    rows, columns = grads.shape
    low, high = lax.axis_index("dp") % 2, lax.axis_index("dp") // 2
    blocks = grads.reshape(count, rows // count, columns)
    blocks = jnp.concatenate([jnp.broadcast_to(extra, (count, *extra.shape)), blocks], axis=1)
    blocks = blocks.reshape(count // 2, 2, -1, columns)
    mine = lax.dynamic_index_in_dim(blocks, low, 1, keepdims=False)
    theirs = lax.dynamic_index_in_dim(blocks, 1 - low, 1, keepdims=False)
    blocks = (mine.astype(F32) + to_dp(theirs, 1, count).astype(F32)).astype(BF16)
    parts = [lax.dynamic_index_in_dim(blocks, high, 0)]
    for flip in range(1, count // 2):
        parts.append(to_dp(lax.dynamic_index_in_dim(blocks, high ^ flip, 0), 2 * flip, count))
    return parts


def on_device(
    count,
    tokens,
    patch_grids,
    ln1_gain,
    ln1_bias,
    w_qkv,
    b_qv,
    w_proj,
    b_proj,
    scale1,
    ln2_gain,
    ln2_bias,
    w_fc1,
    b_fc1,
    w_fc2,
    b_fc2,
    scale2,
    cotangent,
):
    packs = patch_grids.shape[0]
    w_qkv = w_qkv.transpose(0, 2, 1)
    width = tokens.shape[1]
    cols = w_qkv.shape[1]
    hidden = w_fc1.shape[1]
    half = lax.axis_index("tensor") % 2
    place = jnp.full((1,), half, jnp.int32)

    fixed = (tokens, cotangent, ln1_gain, ln1_bias, b_qv, b_proj, scale1, ln2_gain, ln2_bias, b_fc1, b_fc2, scale2, w_qkv)
    call = functools.partial(kernel_call, [id(v) for v in fixed])

    def whole_pack(p):
        return pl.BlockSpec((ROWS, width), lambda *_, p=p: (p, 0))

    def half_pack(p):
        return pl.BlockSpec((HALF, width), lambda i, at, p=p: (2 * p + at[0], 0))

    wp1 = to_core(w_proj)
    wp2 = to_y(w_proj)
    wp3 = to_far(w_proj)
    near_w1, near_w2, near_b1 = to_core(w_fc1), to_core(w_fc2), to_core(b_fc1)

    previous = []

    def run(*args, after=(), **settings):
        made = call(*args, after=(*previous, *after), **settings)
        previous[:] = [made[-1]]
        return made

    def near_sum(keep, send, name):
        (total,) = run(add_rows, (keep, send), (None, None), (shaped(HALF, width),), HALF * width, name=name)
        return total

    kept = []
    heads = []
    for p in range(packs):
        saved, keep, send, lse = run(
            functools.partial(attention_forward, p),
            (patch_grids, tokens, ln1_gain, ln1_bias, w_qkv, b_qv),
            (smem(), whole_pack(p), None, None, None, None),
            (pltpu.HBM((ROWS, width + 1024), BF16), shaped(HALF, cols), shaped(HALF, cols), shaped(8, ROWS, dtype=F32)),
            2 * ROWS * width * 3 * cols + 4 * 3 * ROWS * ROWS * 256,
            place=place,
            scratch=(
                pltpu.VMEM((cols, ROWS), BF16),
                pltpu.VMEM((cols, ROWS), BF16),
                pltpu.VMEM((cols, ROWS), F32),
                pltpu.VMEM((ROWS, cols), F32),
            ),
            name=f"attention_forward_{p}",
            after=((), (near_w1, near_w2, near_b1, wp1), (heads[0][1], wp2, wp3) if heads else ())[p] if p < 3 else (),
        )
        kept.append((saved, lse))
        heads.append((keep, to_core(send), to_y(keep), to_far(send)))

    parts = []

    def hidden_pack(p):
        parts.append(
            run(
                functools.partial(project_mlp, p),
                (
                    patch_grids,
                    tokens,
                    *heads[p],
                    w_proj,
                    wp1,
                    wp2,
                    wp3,
                    b_proj,
                    scale1,
                    ln2_gain,
                    ln2_bias,
                    cotangent,
                    scale2,
                    w_fc1,
                    b_fc1,
                    w_fc2,
                    near_w1,
                    near_b1,
                    near_w2,
                ),
                (smem(), half_pack(p)) + (None,) * 12 + (half_pack(p),) + (None,) * 7,
                (
                    shaped(HALF, width),
                    shaped(HALF, width),
                    shaped(HALF, width),
                    shaped(HALF, 2 * hidden),
                    shaped(HALF, 2 * hidden),
                    shaped(HALF, width),
                    shaped(2, hidden, dtype=F32),
                ),
                8 * ROWS * width * hidden,
                place=place,
                limit=28,
                name=f"project_mlp_{p}",
            )
        )

    def weights(part, added, name):
        lanes = [pl.BlockSpec((HALF, 256), lambda i: (0, i)) for _ in range(2 * packs)]
        units = [pl.BlockSpec((HALF, hidden), lambda i: (0, part)) for _ in range(2 * packs)]
        (g_fc,) = run(
            mlp_weights,
            [v[i] for i in (1, 5, 4, 3) for v in parts] + added,
            lanes + units + [pl.BlockSpec((256, 2 * hidden), lambda i: (i, 0)) for _ in added],
            (shaped(width, 2 * hidden),),
            4 * packs * ROWS * width * hidden,
            out_specs=[pl.BlockSpec((256, 2 * hidden), lambda i: (i, 0))],
            steps=width // 256,
            name=name,
        )
        return g_fc

    def norm2_pack(p, near, far):
        dh1, dy, part = run(
            functools.partial(norm2_backward, p),
            (patch_grids, near, far, tokens, cotangent, parts[p][0], scale1, ln2_gain),
            (smem(), None, None, half_pack(p), half_pack(p), None, None, None),
            (shaped(HALF, width), shaped(HALF, width), shaped(4, width, dtype=F32)),
            30 * HALF * width,
            place=place,
            name=f"norm2_backward_{p}",
        )
        return dh1, dy, to_core(dy), part

    def attention_pack(p, dy, dy_other, before):
        saved, lse = kept[p]
        last = p == packs - 1
        operands = [patch_grids, dy, dy_other, w_proj, w_qkv, saved, lse, *before]
        if last:
            operands += [ln1_gain, ln1_bias]
        keep, send, *norm_sums, g_attn, bias_sums = run(
            functools.partial(attention_backward, p, bool(before), last),
            operands,
            [smem()] + [None] * (len(operands) - 1),
            (
                shaped(HALF, width),
                shaped(HALF, width),
                *([shaped(2, width, dtype=F32)] if last else []),
                shaped(width, 4 * cols),
                shaped(1, 3 * cols, dtype=F32),
            ),
            12 * ROWS * width * cols + 10 * 3 * ROWS * ROWS * 256,
            place=place,
            scratch=(
                pltpu.VMEM((ROWS, width), BF16),
                pltpu.VMEM((ROWS, cols), BF16),
                pltpu.VMEM((cols, ROWS), BF16),
                pltpu.VMEM((cols, ROWS), F32),
                pltpu.VMEM((ROWS, 3 * cols), BF16),
                pltpu.VMEM((ROWS, width), F32),
                pltpu.VMEM((cols, ROWS), BF16),
                pltpu.VMEM((cols, ROWS), BF16),
            ),
            name=f"attention_backward_{p}",
        )
        return keep, to_core(send), (g_attn, bias_sums), norm_sums

    anywhere = pl.BlockSpec(memory_space=pl.ANY)
    whole_rows = pltpu.HBM((packs * ROWS, width), BF16)
    rows = []
    sent = []

    def last_pack(p, far1, far3):
        operands = [patch_grids, near1[p], far1, near3[p][0], far3, tokens, back2[p][0], parts[p][0], ln1_gain, scale1, scale2, b_fc2]
        specs = [smem(), None, None, None, None, half_pack(p)] + [None] * 6
        made = run(
            functools.partial(last_rows, p, bool(rows)),
            operands + rows,
            specs + [anywhere] * len(rows),
            (whole_rows, whole_rows, shaped(2 * HALF, width)),
            30 * HALF * width,
            place=place,
            out_specs=[half_pack(p), half_pack(p), None],
            name=f"last_rows_{p}",
            aliases={len(operands) + i: i for i in range(len(rows))},
        )
        rows[:] = made[:2]
        sent.append(to_core(made[2]))

    for p in range(packs):
        hidden_pack(p)
    far2 = [to_y(v[2]) for v in parts]
    near3 = []

    def output_part(p):
        near3.append(
            run(
                functools.partial(mlp_output, p),
                (patch_grids, parts[p][3], w_fc2, near_w2, cotangent),
                (smem(), None, None, None, half_pack(p)),
                (shaped(HALF, width), shaped(2, width, dtype=F32)),
                4 * HALF * width * hidden,
                place=place,
                name=f"mlp_output_{p}",
            )
        )

    output_part(0)
    back2 = [norm2_pack(0, parts[0][2], far2[0])]
    g_near = to_core(weights(1, [], "mlp_weights_near"))
    back2.append(norm2_pack(1, parts[1][2], far2[1]))
    near1 = []
    carried = ()
    for p in range(packs):
        keep, other, carried, norm_sums = attention_pack(p, back2[p][1], back2[p][2], carried)
        if p == 0:
            fc_parts = swapped(weights(0, [g_near], "mlp_weights_own"), count)
        elif p + 1 < packs:
            back2.append(norm2_pack(p + 1, parts[p + 1][2], far2[p + 1]))
        else:
            for later in range(1, packs):
                output_part(later)
        if p == packs - 1:
            (small,) = run(
                gather_small,
                (norm_sums[0], *[b[3] for b in back2], *[v[6] for v in parts], *[v[1] for v in near3], carried[1]),
                (None,) * (2 + 3 * packs),
                (shaped(16, max(width, hidden), dtype=F32),),
                width,
                name="gather_small",
            )
        near1.append(near_sum(keep, other, f"near1_{p}"))
    far1 = [to_y(v) for v in near1]
    far3 = [to_y(v[0]) for v in near3]
    (small,) = run(
        small_core, (small, to_core(small)), (None, None), (shaped(*small.shape),), width, name="small_core"
    )
    attn_parts = summed_share(carried[0], small, count)

    for p in range(packs - 1):
        last_pack(p, far1[p], far3[p])
    grad_w_fc1, grad_w_fc2 = run(
        finish_mlp,
        (fc_parts,),
        (None,),
        (shaped(width // count, hidden, dtype=F32), shaped(width // count, hidden, dtype=F32)),
        width * hidden,
        name="finish_mlp",
    )
    last_pack(packs - 1, far1[-1], far3[-1])
    vector = shaped(width, dtype=F32)
    grad_w_qkv, grad_w_proj, small = run(
        finish_attention,
        attn_parts,
        (None,) * len(attn_parts),
        (shaped(3, width // count, cols, dtype=F32), shaped(width // count, cols, dtype=F32), shaped(*small.shape, dtype=F32)),
        width * cols,
        name="finish_attention",
    )
    vectors = run(
        finish_small,
        (small, to_y(small), scale1, scale2, b_fc2),
        (None,) * 5,
        (vector, vector, shaped(2, cols, dtype=F32), vector, vector, vector, vector, shaped(hidden, dtype=F32), vector, vector),
        width,
        name="finish_small",
    )
    gain1, bias1, bqv, bp, sc1, gain2, bias2, b1, b2, sc2 = vectors
    grad_tokens, out = call(
        place_rows,
        [*sent, *rows],
        [None] * packs + [anywhere] * 2,
        (whole_rows, whole_rows),
        packs * ROWS * width,
        place=place,
        out_specs=[anywhere, anywhere],
        scratch=(pltpu.SemaphoreType.DMA((2 * packs,)),),
        name="place_rows",
        aliases={packs: 0, packs + 1: 1},
    )
    return (
        out,
        grad_tokens,
        gain1,
        bias1,
        grad_w_qkv,
        bqv,
        grad_w_proj.T,
        bp,
        sc1,
        gain2,
        bias2,
        grad_w_fc1,
        b1,
        grad_w_fc2.T,
        b2,
        sc2,
    )


def total_of(*parts_refs):
    parts = [ref[i].astype(F32) for ref in parts_refs for i in range(ref.shape[0])]
    while len(parts) > 1:
        parts = [a + b for a, b in zip(parts[::2], parts[1::2])]
    return parts[0]


def finish_mlp(parts_ref, w1_ref, w2_ref):
    total = total_of(parts_ref)
    hidden = w1_ref.shape[1]
    w1_ref[...] = total[:, :hidden]
    w2_ref[...] = total[:, hidden:]


def finish_attention(*refs):
    *parts, qkv_ref, proj_ref, small_ref = refs
    total = total_of(*parts)
    small = small_ref.shape[0]
    share, cols = proj_ref.shape
    for i in range(3):
        qkv_ref[i] = total[small : small + share, i * cols : (i + 1) * cols]
    proj_ref[...] = total[small : small + share, 3 * cols :]
    small_ref[...] = total[:small, :]


def gather_small(ln_ref, n0, n1, n2, h0, h1, h2, z0, z1, z2, bias_ref, out_ref):
    width, hidden, cols = ln_ref.shape[1], h0.shape[1], bias_ref.shape[1] // 3
    out_ref[...] = jnp.zeros(out_ref.shape, F32)
    out_ref[0:2, :width] = ln_ref[...]
    out_ref[2:6, :width] = n0[...] + n1[...] + n2[...]
    mlp_sums = h0[...] + h1[...] + h2[...]
    out_ref[6:8, :width] = z0[...] + z1[...] + z2[...]
    out_ref[8:9, :hidden] = mlp_sums[0:1, :hidden]
    out_ref[11:12, :hidden] = mlp_sums[1:2, :hidden]
    out_ref[9:10, :cols] = bias_ref[:, :cols]
    out_ref[10:11, :cols] = bias_ref[:, 2 * cols :]


def small_core(own_ref, other_ref, out_ref):
    both = own_ref[...] + other_ref[...]
    out_ref[...] = own_ref[...].astype(BF16)
    out_ref[0:8, :] = both[0:8, :].astype(BF16)
    out_ref[8:9, :] = (own_ref[8:9, :] + other_ref[11:12, :]).astype(BF16)


def finish_small(own_ref, other_ref, s1_ref, s2_ref, b2_ref, *outs):
    total, both = own_ref[...], own_ref[...] + other_ref[...]
    gain1, bias1, bqv, bp, scale1, gain2, bias2, b1, b2, scale2 = outs
    width, hidden, cols = gain1.shape[0], b1.shape[0], bqv.shape[1]
    gain1[...] = both[0, :width]
    bias1[...] = both[1, :width]
    gain2[...] = total[2, :width]
    bias2[...] = total[3, :width]
    scale1[...] = total[4, :width]
    bp[...] = total[5, :width] * s1_ref[...]
    scale2[...] = both[6, :width] + total[7, :width] * b2_ref[...]
    b2[...] = total[7, :width] * s2_ref[...]
    b1[...] = total[8, :hidden]
    bqv[0:1, :] = total[9:10, :cols]
    bqv[1:2, :] = total[10:11, :cols]


def solution(mesh):
    placed = (
        P("dp", None),
        P("dp", None, None),
        P(),
        P(),
        P(None, None, "tensor"),
        P(None, "tensor"),
        P("tensor", None),
        P(),
        P(),
        P(),
        P(),
        P(None, "tensor"),
        P("tensor"),
        P("tensor", None),
        P(),
        P(),
        P("dp", None),
    )
    return jax.shard_map(
        functools.partial(on_device, mesh.shape["dp"]),
        mesh=mesh,
        in_specs=placed,
        out_specs=(
            P("dp", None),
            P("dp", None),
            P(),
            P(),
            P(None, "dp", "tensor"),
            P(None, "tensor"),
            P("tensor", "dp"),
            P(),
            P(),
            P(),
            P(),
            P("dp", "tensor"),
            P("tensor"),
            P("tensor", "dp"),
            P(),
            P(),
        ),
        check_vma=False,
    )
```

```python
import functools
import math

import jax
import jax.numpy as jnp
from jax import lax
from jax.experimental import pallas as pl
from jax.experimental.pallas import tpu as pltpu
from jax.sharding import PartitionSpec as P

HD = 64
ROWS = 640
HALF = 320
EXTRA = 5
EPS = 1e-06
MASKED = -1e30
F32 = jnp.float32
BF16 = jnp.bfloat16
MIB = 1024 * 1024
VM = pltpu.VMEM


def nn(a, b):
    return lax.dot_general(a, b, (((1,), (0,)), ((), ())), preferred_element_type=F32)


def nt(a, b):
    return lax.dot_general(a, b, (((1,), (1,)), ((), ())), preferred_element_type=F32)


def tn(a, b):
    return lax.dot_general(a, b, (((0,), (0,)), ((), ())), preferred_element_type=F32)


def row(ref):
    return ref[...].reshape(1, ref.shape[-1])


def stats(v):
    mean = jnp.mean(v, axis=-1, keepdims=True)
    centred = v - mean
    spread = jnp.mean(centred * centred, axis=-1, keepdims=True)
    rstd = lax.rsqrt(spread + EPS)
    return centred * rstd, rstd


def ends_of(grid_ref, pack):
    ends = []
    total = jnp.int32(0)
    for image in range(4):
        total = total + grid_ref[pack, image, 0] * grid_ref[pack, image, 1] + EXTRA
        ends.append(total)
    return ends


def segment_at(position, ends):
    found = jnp.zeros(position.shape, jnp.int32)
    for end in ends:
        found = found + jnp.where(position >= end, 1, 0)
    return found


def key_extras(ends, base):
    shape = (ROWS, 128)
    seg = segment_at(lax.broadcasted_iota(jnp.int32, shape, 0), ends)
    lane = lax.broadcasted_iota(jnp.int32, shape, 1) - base
    mask = jnp.where(lane == seg, 0.0, MASKED)
    inside = (lane >= 0) & (lane < 5)
    ones = (lane >= 5) & (lane < 8)
    return jnp.where(inside, mask, jnp.where(ones, 1.0, 0.0)).astype(BF16)


def query_extras(ends, shift):
    shape = (16, ROWS)
    part = lax.broadcasted_iota(jnp.int32, shape, 0)
    if ends is None:
        extra = jnp.zeros(shape, F32)
    else:
        seg = segment_at(lax.broadcasted_iota(jnp.int32, shape, 1), ends)
        extra = jnp.where(part == seg, 1.0, 0.0)
    if shift is not None:
        high = shift.astype(BF16).astype(F32)
        rest = shift - high
        middle = rest.astype(BF16).astype(F32)
        low = rest - middle
        extra = jnp.where(part == 5, high, extra)
        extra = jnp.where(part == 6, middle, extra)
        extra = jnp.where(part == 7, low, extra)
    return jnp.concatenate([extra.astype(BF16), jnp.zeros((48, ROWS), BF16)], axis=0)


def keys_of(head, tiles_ref, start, low_extra, high_extra):
    lane = lax.broadcasted_iota(jnp.int32, (ROWS, 128), 1)
    at = start + 128 * (head // 2)
    tile = tiles_ref[:, at : at + 128]
    if head % 2 == 0:
        return jnp.where(lane < 64, tile, high_extra)
    return jnp.where(lane < 64, low_extra, tile)


def queries_of(head, rows_ref, extra):
    own = rows_ref[64 * head : 64 * head + 64, :]
    return jnp.concatenate([own, extra] if head % 2 == 0 else [extra, own], axis=0)


def attention_forward(
    pack,
    place_ref,
    grid_ref,
    x_ref,
    gain_ref,
    bias_ref,
    w_ref,
    bqv_ref,
    saved_ref,
    keep_ref,
    send_ref,
    lse_ref,
    qt_ref,
    vt_ref,
    ot_ref,
    o_ref,
):
    gain, bias = row(gain_ref), row(bias_ref)
    width = x_ref.shape[1]
    for r in range(0, ROWS, 160):
        normed, _ = stats(x_ref[r : r + 160, :].astype(F32))
        saved_ref[r : r + 160, :width] = (normed * gain + bias).astype(BF16)
    n1 = saved_ref[:, :width]
    cols = 3 * HD
    q = (nt(n1, w_ref[0]) + bqv_ref[0:1, :]) * (1.0 / math.sqrt(HD))
    saved_ref[:, width : width + cols] = q.astype(BF16)
    qt_ref[...] = q.T.astype(BF16)
    saved_ref[:, width + 256 : width + 256 + cols] = nt(n1, w_ref[1]).astype(BF16)
    v = nt(n1, w_ref[2]) + bqv_ref[1:2, :]
    saved_ref[:, width + 512 : width + 512 + cols] = v.astype(BF16)
    vt_ref[...] = v.T.astype(BF16)
    ends = ends_of(grid_ref, pack)
    low_extra, high_extra = key_extras(ends, 0), key_extras(ends, 64)
    extra = query_extras(ends, None)
    for head in range(3):
        s = nn(keys_of(head, saved_ref, width + 256, low_extra, high_extra), queries_of(head, qt_ref, extra))
        top = jnp.max(s, axis=0, keepdims=True)
        e = jnp.exp(s - top)
        total = jnp.sum(e, axis=0, keepdims=True)
        o = nn(vt_ref[64 * head : 64 * head + 64, :], e.astype(BF16)) / total
        ot_ref[64 * head : 64 * head + 64, :] = o
        lse_ref[head : head + 1, :] = top + jnp.log(total)
    o_ref[...] = ot_ref[...].T
    half = place_ref[0]
    saved_ref[:, width + 768 : width + 768 + cols] = o_ref[...].astype(BF16)
    keep_ref[...] = o_ref[pl.ds(pl.multiple_of(half * HALF, HALF), HALF), :].astype(BF16)
    send_ref[...] = o_ref[pl.ds(pl.multiple_of((1 - half) * HALF, HALF), HALF), :].astype(BF16)


def attention_backward(
    pack,
    has_sum,
    last,
    place_ref,
    grid_ref,
    mine_ref,
    other_ref,
    wp_ref,
    w_ref,
    saved_ref,
    lse_ref,
    *rest,
):
    if has_sum:
        g_in_ref, b_in_ref, *rest = rest
    if last:
        gain_ref, bias_ref, keep_ref, send_ref, l_ref, *rest = rest
    else:
        keep_ref, send_ref, *rest = rest
    g_ref, b_ref, dy_ref, do_ref, dot_ref, dqt_ref, dqkv_ref, dn_ref, qt_ref, kt_ref = rest
    half = place_ref[0]
    dy_ref[pl.ds(pl.multiple_of(half * HALF, HALF), HALF), :] = mine_ref[...]
    dy_ref[pl.ds(pl.multiple_of((1 - half) * HALF, HALF), HALF), :] = other_ref[...]
    dy = dy_ref[...]
    do_ref[...] = nt(dy, wp_ref[...]).astype(BF16)
    dot_ref[...] = nt(wp_ref[...], dy).astype(BF16)
    ends = ends_of(grid_ref, pack)
    low_extra, high_extra = key_extras(ends, 0), key_extras(ends, 64)
    cols = 3 * HD
    width = dy.shape[1]
    q_at, k_at, v_at = width, width + 256, width + 512
    qt_ref[...] = saved_ref[:, q_at : q_at + cols].T
    kt_ref[...] = saved_ref[:, k_at : k_at + cols].T
    o = saved_ref[:, width + 768 : width + 768 + cols]
    weighted = o.astype(F32) * do_ref[...].astype(F32)
    dqt_ref[...] = weighted.T
    inners = [jnp.sum(dqt_ref[64 * h : 64 * h + 64, :], axis=0, keepdims=True) for h in range(3)]
    for head in range(3):
        a, b = 64 * head, 64 * head + 64
        inner = inners[head]
        shifted = query_extras(ends, -lse_ref[head : head + 1, :])
        p = jnp.exp(
            nn(keys_of(head, saved_ref, k_at, low_extra, high_extra), queries_of(head, qt_ref, shifted))
        )
        dp = nn(
            keys_of(head, saved_ref, v_at, low_extra, high_extra),
            queries_of(head, dot_ref, query_extras(None, -inner)),
        )
        ds = (p * dp).astype(BF16)
        dqkv_ref[:, 2 * cols + a : 2 * cols + b] = nn(p.astype(BF16), do_ref[:, a:b]).astype(BF16)
        dqkv_ref[:, cols + a : cols + b] = nn(ds, saved_ref[:, q_at + a : q_at + b]).astype(BF16)
        dqt_ref[a:b, :] = nn(kt_ref[a:b, :], ds)
    dqkv_ref[:, :cols] = (dqt_ref[...].T * (1.0 / math.sqrt(HD))).astype(BF16)
    dn = nn(dqkv_ref[:, :cols], w_ref[0])
    dn = dn + nn(dqkv_ref[:, cols : 2 * cols], w_ref[1])
    dn = dn + nn(dqkv_ref[:, 2 * cols : 3 * cols], w_ref[2])
    dn_ref[...] = dn
    keep_ref[...] = dn_ref[pl.ds(pl.multiple_of(half * HALF, HALF), HALF), :].astype(BF16)
    send_ref[...] = dn_ref[pl.ds(pl.multiple_of((1 - half) * HALF, HALF), HALF), :].astype(BF16)
    g_qkv = tn(saved_ref[:, :width], dqkv_ref[...])
    g_proj = tn(dy, o)
    if has_sum:
        g_qkv = g_qkv + g_in_ref[:, : 3 * cols].astype(F32)
        g_proj = g_proj + g_in_ref[:, 3 * cols :].astype(F32)
    g_ref[:, : 3 * cols] = g_qkv.astype(g_ref.dtype)
    g_ref[:, 3 * cols :] = g_proj.astype(g_ref.dtype)
    sums = jnp.sum(dqkv_ref[...].astype(F32), axis=0, keepdims=True)
    sums = sums + b_in_ref[...] if has_sum else sums
    b_ref[...] = sums
    if last:
        plain = jnp.zeros((width, 1), F32)
        mixed = jnp.zeros((width, 1), F32)
        for c in range(3):
            at = slice(c * cols, (c + 1) * cols)
            w = w_ref[c].astype(F32).T
            plain = plain + jnp.sum(w * sums[:, at], axis=1, keepdims=True)
            mixed = mixed + jnp.sum(w * g_qkv[:, at], axis=1, keepdims=True)
        wide = jnp.concatenate([mixed, plain, jnp.zeros((width, 126), F32)], axis=1).T
        l_ref[0:1, :] = (wide[0:1, :] - row(bias_ref) * wide[1:2, :]) / row(gain_ref)
        l_ref[1:2, :] = wide[1:2, :]


def hidden_part(n2, dz, w1_ref, b1, w2_ref):
    u = nn(n2, w1_ref[...]) + b1
    cdf = 0.5 * (1.0 + lax.erf(u * (1.0 / math.sqrt(2.0))))
    density = jnp.exp(-0.5 * (u * u)) * (1.0 / math.sqrt(2.0 * math.pi))
    g = (u * cdf).astype(BF16)
    du = (nt(dz, w2_ref[...]) * (cdf + u * density)).astype(BF16)
    return g, du, nt(du, w1_ref[...])


def project_mlp(
    pack,
    place_ref,
    grid_ref,
    x_ref,
    o0,
    o1,
    o2,
    o3,
    p0,
    p1,
    p2,
    p3,
    bp_ref,
    s1_ref,
    gain_ref,
    bias_ref,
    cot_ref,
    s2_ref,
    w1_ref,
    b1_ref,
    w2_ref,
    v1_ref,
    c1_ref,
    v2_ref,
    yb_ref,
    n2_ref,
    dn_ref,
    g_ref,
    du_ref,
    dz_ref,
    sum_ref,
):
    y0, y1, y2, y3 = (nn(o[...], p[...]).astype(BF16).astype(F32) for o, p in ((o0, p0), (o1, p1), (o2, p2), (o3, p3)))
    yb = (y0 + y1) + (y2 + y3) + row(bp_ref)
    yb_ref[...] = yb.astype(BF16)
    normed, _ = stats(x_ref[...].astype(F32) + row(s1_ref) * yb)
    n2 = (normed * row(gain_ref) + row(bias_ref)).astype(BF16)
    n2_ref[...] = n2
    dd = cot_ref[...].astype(F32) * live_half(grid_ref, pack, place_ref[0])
    dz = (row(s2_ref) * dd).astype(BF16)
    dz_ref[...] = dz
    hidden = w1_ref.shape[1]
    g, du, dn = hidden_part(n2, dz, w1_ref, row(b1_ref), w2_ref)
    g_ref[:, :hidden] = g
    du_ref[:, :hidden] = du
    sum_ref[0:1, :] = colsum(du.astype(F32))
    g, du, dn_other = hidden_part(n2, dz, v1_ref, row(c1_ref), v2_ref)
    g_ref[:, hidden:] = g
    du_ref[:, hidden:] = du
    sum_ref[1:2, :] = colsum(du.astype(F32))
    dn_ref[...] = (dn + dn_other).astype(BF16)


def mlp_output(pack, place_ref, grid_ref, g_ref, w2_ref, v2_ref, cot_ref, z_ref, sum_ref):
    hidden = w2_ref.shape[0]
    z = nn(g_ref[:, :hidden], w2_ref[...]) + nn(g_ref[:, hidden:], v2_ref[...])
    z_ref[...] = z.astype(BF16)
    dd = cot_ref[...].astype(F32) * live_half(grid_ref, pack, place_ref[0])
    sum_ref[0:1, :] = colsum(dd * z)
    sum_ref[1:2, :] = colsum(dd)


def add_rows(a_ref, b_ref, out_ref):
    out_ref[...] = (a_ref[...].astype(F32) + b_ref[...].astype(F32)).astype(BF16)


def mlp_weights(n0, n1, n2, z0, z1, z2, u0, u1, u2, g0, g1, g2, *rest):
    *added, out_ref = rest
    mid = u0.shape[1]
    first = tn(n0[...], u0[...]) + tn(n1[...], u1[...]) + tn(n2[...], u2[...])
    second = tn(z0[...], g0[...]) + tn(z1[...], g1[...]) + tn(z2[...], g2[...])
    if added:
        first = first + added[0][:, :mid].astype(F32)
        second = second + added[0][:, mid:].astype(F32)
    out_ref[:, :mid] = first.astype(BF16)
    out_ref[:, mid:] = second.astype(BF16)


def live_half(grid_ref, pack, half):
    position = lax.broadcasted_iota(jnp.int32, (HALF, 1), 0) + half * HALF
    return jnp.where(position < ends_of(grid_ref, pack)[3], 1.0, 0.0)


def colsum(v):
    return jnp.sum(v, axis=0, keepdims=True)


def norm2_backward(
    pack, place_ref, grid_ref, a_ref, b_ref, x_ref, cot_ref, yb_ref, s1_ref, gain_ref, dh_ref, dy_ref, sum_ref
):
    half = place_ref[0]
    live = live_half(grid_ref, pack, half)
    scale = row(s1_ref)
    yb = yb_ref[...].astype(F32)
    h1 = x_ref[...].astype(F32) + scale * yb
    nh, rstd = stats(h1)
    dn2 = a_ref[...].astype(F32) + b_ref[...].astype(F32)
    e = dn2 * row(gain_ref)
    inner = e - jnp.mean(e, axis=-1, keepdims=True) - nh * jnp.mean(e * nh, axis=-1, keepdims=True)
    dh1 = cot_ref[...].astype(F32) * live + inner * rstd
    dh_ref[...] = dh1.astype(BF16)
    dy_ref[...] = (scale * dh1).astype(BF16)
    sum_ref[0:1, :] = colsum(dn2 * nh)
    sum_ref[1:2, :] = colsum(dn2)
    sum_ref[2:3, :] = colsum(dh1 * yb)
    sum_ref[3:4, :] = colsum(dh1)


def last_rows(
    pack,
    has_rows,
    place_ref,
    grid_ref,
    a1_ref,
    b1_ref,
    a3_ref,
    b3_ref,
    x_ref,
    dh_ref,
    yb_ref,
    gain_ref,
    s1_ref,
    s2_ref,
    bf_ref,
    *rest,
):
    gt_ref, out_ref, send_ref = rest[2:] if has_rows else rest
    live = live_half(grid_ref, pack, place_ref[0])
    x = x_ref[...].astype(F32)
    zb = a3_ref[...].astype(F32) + b3_ref[...].astype(F32) + row(bf_ref)
    out = (live * (x + row(s1_ref) * yb_ref[...].astype(F32) + row(s2_ref) * zb)).astype(BF16)
    out_ref[...] = out
    send_ref[HALF:, :] = out
    nx, rstd = stats(x)
    e = (a1_ref[...].astype(F32) + b1_ref[...].astype(F32)) * row(gain_ref)
    inner = e - jnp.mean(e, axis=-1, keepdims=True) - nx * jnp.mean(e * nx, axis=-1, keepdims=True)
    gt = (dh_ref[...].astype(F32) + inner * rstd).astype(BF16)
    gt_ref[...] = gt
    send_ref[:HALF, :] = gt


def place_rows(place_ref, *refs):
    got, (gt_ref, out_ref, sems) = refs[: len(refs) - 5], refs[len(refs) - 3 :]
    copies = []
    for p, ref in enumerate(got):
        at = pl.ds(pl.multiple_of((2 * p + 1 - place_ref[0]) * HALF, HALF), HALF)
        copies.append(pltpu.make_async_copy(ref.at[pl.ds(0, HALF), :], gt_ref.at[at, :], sems.at[2 * p]))
        copies.append(pltpu.make_async_copy(ref.at[pl.ds(HALF, HALF), :], out_ref.at[at, :], sems.at[2 * p + 1]))
    for copy in copies:
        copy.start()
    for copy in copies:
        copy.wait()


def full():
    return pl.BlockSpec(memory_space=VM)


def smem():
    return pl.BlockSpec(memory_space=pltpu.SMEM)


def shaped(*shape, dtype=BF16):
    return jax.ShapeDtypeStruct(shape, dtype)


def kernel_call(pinned, body, operands, in_specs, out_shape, flops, place=None, out_specs=None, scratch=(), steps=1, limit=16, name=None, after=(), aliases=None):
    prefetch = 0 if place is None else 1
    operands = [pltpu.with_memory_space_constraint(o, pltpu.HBM) if id(o) in pinned else o for o in operands]
    count = len(out_shape)
    moved = sum(math.prod(s.shape) * s.dtype.itemsize for s in out_shape)
    moved += sum(o.size * o.dtype.itemsize for o in operands)
    if after:
        skip = prefetch + len(operands)
        inner = body

        def body(*refs):
            inner(*refs[:skip], *refs[skip + len(after) :])

        operands = (*operands, *after)
        in_specs = (*in_specs, *(pl.BlockSpec(memory_space=pl.ANY) for _ in after))
    fixed = []
    for spec, operand in zip(in_specs, operands):
        if spec is None:
            rank = operand.ndim
            spec = pl.BlockSpec(operand.shape, lambda *_, rank=rank: (0,) * rank)
        fixed.append(spec)
    outs = []
    for index, shape in enumerate(out_shape):
        spec = out_specs[index] if out_specs else None
        if spec is None:
            rank = len(shape.shape)
            spec = pl.BlockSpec(shape.shape, lambda *_, rank=rank: (0,) * rank)
        outs.append(spec)
    grid_spec = pltpu.PrefetchScalarGridSpec(
        num_scalar_prefetch=prefetch,
        grid=(steps,),
        in_specs=fixed,
        out_specs=outs,
        scratch_shapes=list(scratch),
    )
    made = pl.pallas_call(
        body,
        out_shape=list(out_shape),
        grid_spec=grid_spec,
        input_output_aliases={prefetch + k: v for k, v in (aliases or {}).items()},
        compiler_params=pltpu.CompilerParams(vmem_limit_bytes=limit * MIB),
        cost_estimate=pl.CostEstimate(flops=3 * 10**10, bytes_accessed=int(moved), transcendentals=0),
        name=name,
    )
    del count
    return made(*(() if place is None else (place,)), *operands)


CORE = [(0, 1), (1, 0), (2, 3), (3, 2)]
OVER_Y = [(0, 2), (2, 0), (1, 3), (3, 1)]


def to_core(v):
    return lax.ppermute(v, "tensor", CORE)


def to_far(v):
    return lax.ppermute(v, "tensor", [(0, 3), (3, 0), (1, 2), (2, 1)])


def to_y(v):
    return lax.ppermute(v, "tensor", OVER_Y)


def to_dp(v, flip, count):
    return lax.ppermute(v, "dp", [(i, i ^ flip) for i in range(count)])


def swapped(grads, count):
    rows, columns = grads.shape
    return lax.all_to_all(grads.reshape(count, rows // count, columns), "dp", 0, 0)


def summed_share(grads, extra, count):
    rows, columns = grads.shape
    low, high = lax.axis_index("dp") % 2, lax.axis_index("dp") // 2
    blocks = grads.reshape(count, rows // count, columns)
    blocks = jnp.concatenate([jnp.broadcast_to(extra, (count, *extra.shape)), blocks], axis=1)
    blocks = blocks.reshape(count // 2, 2, -1, columns)
    mine = lax.dynamic_index_in_dim(blocks, low, 1, keepdims=False)
    theirs = lax.dynamic_index_in_dim(blocks, 1 - low, 1, keepdims=False)
    blocks = (mine.astype(F32) + to_dp(theirs, 1, count).astype(F32)).astype(BF16)
    parts = [lax.dynamic_index_in_dim(blocks, high, 0)]
    for flip in range(1, count // 2):
        parts.append(to_dp(lax.dynamic_index_in_dim(blocks, high ^ flip, 0), 2 * flip, count))
    return parts


def on_device(
    count,
    tokens,
    patch_grids,
    ln1_gain,
    ln1_bias,
    w_qkv,
    b_qv,
    w_proj,
    b_proj,
    scale1,
    ln2_gain,
    ln2_bias,
    w_fc1,
    b_fc1,
    w_fc2,
    b_fc2,
    scale2,
    cotangent,
):
    packs = patch_grids.shape[0]
    w_qkv = w_qkv.transpose(0, 2, 1)
    width = tokens.shape[1]
    cols = w_qkv.shape[1]
    hidden = w_fc1.shape[1]
    half = lax.axis_index("tensor") % 2
    place = jnp.full((1,), half, jnp.int32)

    fixed = (tokens, cotangent, ln1_gain, ln1_bias, b_qv, b_proj, scale1, ln2_gain, ln2_bias, b_fc1, b_fc2, scale2, w_qkv)
    call = functools.partial(kernel_call, [id(v) for v in fixed])

    def whole_pack(p):
        return pl.BlockSpec((ROWS, width), lambda *_, p=p: (p, 0))

    def half_pack(p):
        return pl.BlockSpec((HALF, width), lambda i, at, p=p: (2 * p + at[0], 0))

    wp1 = to_core(w_proj)
    wp2 = to_y(w_proj)
    wp3 = to_far(w_proj)
    near_w1, near_w2, near_b1 = to_core(w_fc1), to_core(w_fc2), to_core(b_fc1)

    previous = []

    def run(*args, after=(), **settings):
        made = call(*args, after=(*previous, *after), **settings)
        previous[:] = [made[-1]]
        return made

    def near_sum(keep, send, name):
        (total,) = run(add_rows, (keep, send), (None, None), (shaped(HALF, width),), HALF * width, name=name)
        return total

    kept = []
    heads = []
    for p in range(packs):
        saved, keep, send, lse = run(
            functools.partial(attention_forward, p),
            (patch_grids, tokens, ln1_gain, ln1_bias, w_qkv, b_qv),
            (smem(), whole_pack(p), None, None, None, None),
            (pltpu.HBM((ROWS, width + 1024), BF16), shaped(HALF, cols), shaped(HALF, cols), shaped(8, ROWS, dtype=F32)),
            2 * ROWS * width * 3 * cols + 4 * 3 * ROWS * ROWS * 256,
            place=place,
            scratch=(
                pltpu.VMEM((cols, ROWS), BF16),
                pltpu.VMEM((cols, ROWS), BF16),
                pltpu.VMEM((cols, ROWS), F32),
                pltpu.VMEM((ROWS, cols), F32),
            ),
            name=f"attention_forward_{p}",
            after=((), (near_w1, near_w2, near_b1, wp1), (heads[0][1], wp2, wp3) if heads else ())[p] if p < 3 else (),
        )
        kept.append((saved, lse))
        heads.append((keep, to_core(send), to_y(keep), to_far(send)))

    parts = []

    def hidden_pack(p):
        parts.append(
            run(
                functools.partial(project_mlp, p),
                (
                    patch_grids,
                    tokens,
                    *heads[p],
                    w_proj,
                    wp1,
                    wp2,
                    wp3,
                    b_proj,
                    scale1,
                    ln2_gain,
                    ln2_bias,
                    cotangent,
                    scale2,
                    w_fc1,
                    b_fc1,
                    w_fc2,
                    near_w1,
                    near_b1,
                    near_w2,
                ),
                (smem(), half_pack(p)) + (None,) * 12 + (half_pack(p),) + (None,) * 7,
                (
                    shaped(HALF, width),
                    shaped(HALF, width),
                    shaped(HALF, width),
                    shaped(HALF, 2 * hidden),
                    shaped(HALF, 2 * hidden),
                    shaped(HALF, width),
                    shaped(2, hidden, dtype=F32),
                ),
                8 * ROWS * width * hidden,
                place=place,
                limit=28,
                name=f"project_mlp_{p}",
            )
        )

    def weights(part, added, name):
        lanes = [pl.BlockSpec((HALF, 256), lambda i: (0, i)) for _ in range(2 * packs)]
        units = [pl.BlockSpec((HALF, hidden), lambda i: (0, part)) for _ in range(2 * packs)]
        (g_fc,) = run(
            mlp_weights,
            [v[i] for i in (1, 5, 4, 3) for v in parts] + added,
            lanes + units + [pl.BlockSpec((256, 2 * hidden), lambda i: (i, 0)) for _ in added],
            (shaped(width, 2 * hidden),),
            4 * packs * ROWS * width * hidden,
            out_specs=[pl.BlockSpec((256, 2 * hidden), lambda i: (i, 0))],
            steps=width // 256,
            name=name,
        )
        return g_fc

    def norm2_pack(p, near, far):
        dh1, dy, part = run(
            functools.partial(norm2_backward, p),
            (patch_grids, near, far, tokens, cotangent, parts[p][0], scale1, ln2_gain),
            (smem(), None, None, half_pack(p), half_pack(p), None, None, None),
            (shaped(HALF, width), shaped(HALF, width), shaped(4, width, dtype=F32)),
            30 * HALF * width,
            place=place,
            name=f"norm2_backward_{p}",
        )
        return dh1, dy, to_core(dy), part

    def attention_pack(p, dy, dy_other, before):
        saved, lse = kept[p]
        last = p == packs - 1
        operands = [patch_grids, dy, dy_other, w_proj, w_qkv, saved, lse, *before]
        if last:
            operands += [ln1_gain, ln1_bias]
        keep, send, *norm_sums, g_attn, bias_sums = run(
            functools.partial(attention_backward, p, bool(before), last),
            operands,
            [smem()] + [None] * (len(operands) - 1),
            (
                shaped(HALF, width),
                shaped(HALF, width),
                *([shaped(2, width, dtype=F32)] if last else []),
                shaped(width, 4 * cols),
                shaped(1, 3 * cols, dtype=F32),
            ),
            12 * ROWS * width * cols + 10 * 3 * ROWS * ROWS * 256,
            place=place,
            scratch=(
                pltpu.VMEM((ROWS, width), BF16),
                pltpu.VMEM((ROWS, cols), BF16),
                pltpu.VMEM((cols, ROWS), BF16),
                pltpu.VMEM((cols, ROWS), F32),
                pltpu.VMEM((ROWS, 3 * cols), BF16),
                pltpu.VMEM((ROWS, width), F32),
                pltpu.VMEM((cols, ROWS), BF16),
                pltpu.VMEM((cols, ROWS), BF16),
            ),
            name=f"attention_backward_{p}",
        )
        return keep, to_core(send), (g_attn, bias_sums), norm_sums

    anywhere = pl.BlockSpec(memory_space=pl.ANY)
    whole_rows = pltpu.HBM((packs * ROWS, width), BF16)
    rows = []
    sent = []

    def last_pack(p, far1, far3):
        operands = [patch_grids, near1[p], far1, near3[p][0], far3, tokens, back2[p][0], parts[p][0], ln1_gain, scale1, scale2, b_fc2]
        specs = [smem(), None, None, None, None, half_pack(p)] + [None] * 6
        made = run(
            functools.partial(last_rows, p, bool(rows)),
            operands + rows,
            specs + [anywhere] * len(rows),
            (whole_rows, whole_rows, shaped(2 * HALF, width)),
            30 * HALF * width,
            place=place,
            out_specs=[half_pack(p), half_pack(p), None],
            name=f"last_rows_{p}",
            aliases={len(operands) + i: i for i in range(len(rows))},
        )
        rows[:] = made[:2]
        sent.append(to_core(made[2]))

    for p in range(packs):
        hidden_pack(p)
    far2 = [to_y(v[2]) for v in parts]
    near3 = []

    def output_part(p):
        near3.append(
            run(
                functools.partial(mlp_output, p),
                (patch_grids, parts[p][3], w_fc2, near_w2, cotangent),
                (smem(), None, None, None, half_pack(p)),
                (shaped(HALF, width), shaped(2, width, dtype=F32)),
                4 * HALF * width * hidden,
                place=place,
                name=f"mlp_output_{p}",
            )
        )

    output_part(0)
    back2 = [norm2_pack(0, parts[0][2], far2[0])]
    g_near = to_core(weights(1, [], "mlp_weights_near"))
    back2.append(norm2_pack(1, parts[1][2], far2[1]))
    near1 = []
    carried = ()
    for p in range(packs):
        keep, other, carried, norm_sums = attention_pack(p, back2[p][1], back2[p][2], carried)
        if p == 0:
            fc_parts = swapped(weights(0, [g_near], "mlp_weights_own"), count)
        elif p + 1 < packs:
            back2.append(norm2_pack(p + 1, parts[p + 1][2], far2[p + 1]))
        else:
            for later in range(1, packs):
                output_part(later)
        if p == packs - 1:
            (small,) = run(
                gather_small,
                (norm_sums[0], *[b[3] for b in back2], *[v[6] for v in parts], *[v[1] for v in near3], carried[1]),
                (None,) * (2 + 3 * packs),
                (shaped(16, max(width, hidden), dtype=F32),),
                width,
                name="gather_small",
            )
        near1.append(near_sum(keep, other, f"near1_{p}"))
    far1 = [to_y(v) for v in near1]
    far3 = [to_y(v[0]) for v in near3]
    (small,) = run(
        small_core, (small, to_core(small)), (None, None), (shaped(*small.shape),), width, name="small_core"
    )
    attn_parts = summed_share(carried[0], small, count)

    for p in range(packs - 1):
        last_pack(p, far1[p], far3[p])
    last_pack(packs - 1, far1[-1], far3[-1])
    grad_w_fc1, grad_w_fc2 = run(
        finish_mlp,
        (fc_parts,),
        (None,),
        (shaped(width // count, hidden, dtype=F32), shaped(width // count, hidden, dtype=F32)),
        width * hidden,
        name="finish_mlp",
    )
    vector = shaped(width, dtype=F32)
    grad_w_qkv, grad_w_proj, small = run(
        finish_attention,
        attn_parts,
        (None,) * len(attn_parts),
        (shaped(3, width // count, cols, dtype=F32), shaped(width // count, cols, dtype=F32), shaped(*small.shape, dtype=F32)),
        width * cols,
        name="finish_attention",
    )
    vectors = run(
        finish_small,
        (small, to_y(small), scale1, scale2, b_fc2),
        (None,) * 5,
        (vector, vector, shaped(2, cols, dtype=F32), vector, vector, vector, vector, shaped(hidden, dtype=F32), vector, vector),
        width,
        name="finish_small",
    )
    gain1, bias1, bqv, bp, sc1, gain2, bias2, b1, b2, sc2 = vectors
    grad_tokens, out = call(
        place_rows,
        [*sent, *rows],
        [None] * packs + [anywhere] * 2,
        (whole_rows, whole_rows),
        packs * ROWS * width,
        place=place,
        out_specs=[anywhere, anywhere],
        scratch=(pltpu.SemaphoreType.DMA((2 * packs,)),),
        name="place_rows",
        aliases={packs: 0, packs + 1: 1},
    )
    return (
        out,
        grad_tokens,
        gain1,
        bias1,
        grad_w_qkv,
        bqv,
        grad_w_proj.T,
        bp,
        sc1,
        gain2,
        bias2,
        grad_w_fc1,
        b1,
        grad_w_fc2.T,
        b2,
        sc2,
    )


def total_of(*parts_refs):
    parts = [ref[i].astype(F32) for ref in parts_refs for i in range(ref.shape[0])]
    while len(parts) > 1:
        parts = [a + b for a, b in zip(parts[::2], parts[1::2])]
    return parts[0]


def finish_mlp(parts_ref, w1_ref, w2_ref):
    total = total_of(parts_ref)
    hidden = w1_ref.shape[1]
    w1_ref[...] = total[:, :hidden]
    w2_ref[...] = total[:, hidden:]


def finish_attention(*refs):
    *parts, qkv_ref, proj_ref, small_ref = refs
    total = total_of(*parts)
    small = small_ref.shape[0]
    share, cols = proj_ref.shape
    for i in range(3):
        qkv_ref[i] = total[small : small + share, i * cols : (i + 1) * cols]
    proj_ref[...] = total[small : small + share, 3 * cols :]
    small_ref[...] = total[:small, :]


def gather_small(ln_ref, n0, n1, n2, h0, h1, h2, z0, z1, z2, bias_ref, out_ref):
    width, hidden, cols = ln_ref.shape[1], h0.shape[1], bias_ref.shape[1] // 3
    out_ref[...] = jnp.zeros(out_ref.shape, F32)
    out_ref[0:2, :width] = ln_ref[...]
    out_ref[2:6, :width] = n0[...] + n1[...] + n2[...]
    mlp_sums = h0[...] + h1[...] + h2[...]
    out_ref[6:8, :width] = z0[...] + z1[...] + z2[...]
    out_ref[8:9, :hidden] = mlp_sums[0:1, :hidden]
    out_ref[11:12, :hidden] = mlp_sums[1:2, :hidden]
    out_ref[9:10, :cols] = bias_ref[:, :cols]
    out_ref[10:11, :cols] = bias_ref[:, 2 * cols :]


def small_core(own_ref, other_ref, out_ref):
    both = own_ref[...] + other_ref[...]
    out_ref[...] = own_ref[...].astype(BF16)
    out_ref[0:8, :] = both[0:8, :].astype(BF16)
    out_ref[8:9, :] = (own_ref[8:9, :] + other_ref[11:12, :]).astype(BF16)


def finish_small(own_ref, other_ref, s1_ref, s2_ref, b2_ref, *outs):
    total, both = own_ref[...], own_ref[...] + other_ref[...]
    gain1, bias1, bqv, bp, scale1, gain2, bias2, b1, b2, scale2 = outs
    width, hidden, cols = gain1.shape[0], b1.shape[0], bqv.shape[1]
    gain1[...] = both[0, :width]
    bias1[...] = both[1, :width]
    gain2[...] = total[2, :width]
    bias2[...] = total[3, :width]
    scale1[...] = total[4, :width]
    bp[...] = total[5, :width] * s1_ref[...]
    scale2[...] = both[6, :width] + total[7, :width] * b2_ref[...]
    b2[...] = total[7, :width] * s2_ref[...]
    b1[...] = total[8, :hidden]
    bqv[0:1, :] = total[9:10, :cols]
    bqv[1:2, :] = total[10:11, :cols]


def solution(mesh):
    placed = (
        P("dp", None),
        P("dp", None, None),
        P(),
        P(),
        P(None, None, "tensor"),
        P(None, "tensor"),
        P("tensor", None),
        P(),
        P(),
        P(),
        P(),
        P(None, "tensor"),
        P("tensor"),
        P("tensor", None),
        P(),
        P(),
        P("dp", None),
    )
    return jax.shard_map(
        functools.partial(on_device, mesh.shape["dp"]),
        mesh=mesh,
        in_specs=placed,
        out_specs=(
            P("dp", None),
            P("dp", None),
            P(),
            P(),
            P(None, "dp", "tensor"),
            P(None, "tensor"),
            P("tensor", "dp"),
            P(),
            P(),
            P(),
            P(),
            P("dp", "tensor"),
            P("tensor"),
            P("tensor", "dp"),
            P(),
            P(),
        ),
        check_vma=False,
    )
```
